128 devices in a mesh: tile: 32 (over z, y_lo, x), comp: 4 (over y_hi, core).
Axes of the slice: x: 4, y: 4 (y_hi: 2, y_lo: 2; y = y_hi * 2 + y_lo), z: 4, core: 2. Of those that a mesh axis runs over, the one named last changes fastest.
Arguments:
- atm_state: float32 [4, 16, 1024, 512], P(None, None, 'tile', 'comp'), may hold values from -6 to 6
- level_winds: float32 [2, 16], replicated, may hold values from -1 to 1
- physics_flags: int32 [1024, 512], P('tile', 'comp'), may hold values from 0 to 2
- flux_matrix: float32 [12, 4], replicated, may hold values from -3 to 3
- regrid_source: int32 [1024, 8], P(('tile', 'comp')), may hold values from 0 to 4095, as said below
- regrid_weights: bfloat16 [1024, 8, 128, 128], P(('tile', 'comp')), may hold values from -0.1875 to 0.1875
- return_weights: bfloat16 [1024, 8, 128, 128], P(('tile', 'comp')), may hold values from -0.375 to 0.375
- ocean_state: float32 [4, 16, 131072], P(None, None, ('tile', 'comp')), may hold values from -6 to 6
- ocean_neighbors: int32 [6, 131072], P(None, ('tile', 'comp')), may hold values from 0 to 256, as said below
- edge_weights: float32 [6, 131072], P(None, ('tile', 'comp')), may hold values from 0.02 to 0.14
- ocean_coupling: float32 [4, 12], replicated, may hold values from -1.75 to 1.75
Outputs:
- atm_final: float32 [4, 16, 1024, 512], P(None, None, 'tile', 'comp')
- ocean_final: float32 [4, 16, 131072], P(None, None, ('tile', 'comp'))
- ocean_on_atm: float32 [4, 1024, 512], P(None, 'tile', 'comp')
The draws below stay inside these ranges and needn't reach their ends.
Inputs may be any that keep to these rules, and one draw needn't show every extreme that they name: `regrid_source`: every entry of row b names a surface block in the comp column of row b's owner: entry % (devices along comp) equals (b // 8) % (devices along comp). The rows of one ocean device name blocks of any one tile index (x // 32) at most 4 times, exactly 4 times for one of them. Entries may repeat. `ocean_neighbors`: an entry minus 128 is the signed distance of the neighbour from its own cell in the cyclic order of the 131072 cells; distances of exactly 128 and -128 both occur.
All inputs are finite; a program needn't handle non-finite values.
Results may differ from the reference program's by a relative error of at most 0.0039.
Values may be sent and summed in bfloat16 or wider, within the bound.
No kernel may reach another device: no remote copies, remote signals or barrier semaphores. Data moves between devices by JAX's collectives and lax.ppermute only.
A program may use at most 128 MiB of HBM per device.

```python
import math
import jax
import jax.numpy as jnp
import numpy as np
from jax import lax

EX = 8
LEV = 16
FIELDS = 4
NFLUX = 12
ATM_STEPS = 4
OB_DEV = 8
KB = 8
OLEV = 16
OFIELDS = 4
OCEAN_STEPS = 2
HALO = 128
BLK = 128
XN_TOT = 1024
YN_TOT = 512
OBLOCKS = 1024
OCELLS = 131072
CAP = 4
N_TILE = 32
N_COMP = 4


def draw_regrid_source(key, part):
    key = jax.random.fold_in(key, 11)
    device_count = N_TILE * N_COMP
    n_requests = OB_DEV * KB
    slot_count = N_TILE * CAP

    def one_device(device):
        dev_key = jax.random.fold_in(key, device)
        key_first, key_order, key_shuffle, key_rows = jax.random.split(dev_key, 4)
        first_tile = jax.random.randint(key_first, (), 0, N_TILE)
        order = jax.random.permutation(key_order, slot_count)
        slot_tile = jnp.arange(slot_count) // CAP
        score = jnp.where(slot_tile == first_tile, order - slot_count, order)
        chosen = jnp.argsort(score)[:n_requests]
        chosen = chosen[jax.random.permutation(key_shuffle, n_requests)]
        tile_ids = chosen // CAP
        row_ids = jax.random.randint(key_rows, (n_requests,), 0, 4 * EX)
        comp_id = device % N_COMP
        return ((tile_ids * (4 * EX) + row_ids) * N_COMP + comp_id).astype(jnp.int32)
    result = jax.vmap(one_device)(jnp.arange(device_count))
    return result.reshape(device_count * OB_DEV, KB).astype(jnp.int32)


def draw_ocean_neighbors(key, part):
    key = jax.random.fold_in(key, 23)
    cell_total = OB_DEV * BLK * N_TILE * N_COMP
    offsets = jax.random.randint(key, (6, cell_total), 0, 2 * HALO + 1)
    cell_ids = jnp.arange(cell_total)
    offsets = offsets.at[0].set(jnp.where(cell_ids % BLK == 0, 2 * HALO, offsets[0]))
    offsets = offsets.at[1].set(jnp.where(cell_ids % BLK == 1, 0, offsets[1]))
    return offsets.astype(jnp.int32)


def place_ends(values, key, smallest, top_value):
    extent = values.shape
    index_at = [jax.random.randint(jax.random.fold_in(key, axis), (), 0, extent[axis]) for axis in range(len(extent))]
    values = values.at[tuple(index_at)].set(smallest)
    longest = extent.index(max(extent))
    index_at[longest] = (index_at[longest] + 1) % extent[longest]
    return values.at[tuple(index_at)].set(top_value)


def levels(key, extent, cuts, smallest, largest):
    gain, own = 1.0, jax.random.fold_in(key, 6)
    for dim, blocks in cuts:
        steps = jnp.exp(jax.random.uniform(jax.random.fold_in(own, dim), (blocks,), jnp.float32, smallest / len(cuts), largest / len(cuts)))
        gain = gain * jnp.repeat(steps, extent[dim] // blocks).reshape([-1 if axis == dim else 1 for axis in range(len(extent))])
    return gain


def normal_values(key, extent, deviation, bound, pieces=(), held_as=jnp.bfloat16):
    values = jax.random.normal(key, extent, jnp.float32) * deviation
    if len(pieces) > 0:
        values = levels(key, extent, pieces, -0.22, 0.18) * values
    return jnp.clip(values, min=-bound, max=bound).astype(held_as)


def setup_inputs(seed: int = 0) -> dict:
    streams_of = jax.random.split(jax.random.key(seed), 12)
    return {
        "atm_state": normal_values(streams_of[0], (FIELDS, LEV, XN_TOT, YN_TOT), 1.0, 6.0, ((2, 32), (3, 4)), jnp.float32),
        "level_winds": jnp.clip(jax.random.uniform(streams_of[1], (2, LEV), jnp.float32, -1.0, 1.0), -1.0, 1.0),
        "physics_flags": place_ends(jax.random.randint(streams_of[2], (XN_TOT, YN_TOT), 0, 3), jax.random.fold_in(streams_of[2], 1), 0, 2).astype(jnp.int32),
        "flux_matrix": normal_values(streams_of[3], (NFLUX, FIELDS), FIELDS ** -0.5, 3.0, (), jnp.float32),
        "regrid_source": draw_regrid_source(jax.random.fold_in(streams_of[11], 71), 0),
        "regrid_weights": normal_values(streams_of[5], (OBLOCKS, KB, BLK, BLK), (KB * BLK) ** -0.5, 0.1875, ((0, 128),)),
        "return_weights": normal_values(streams_of[6], (OBLOCKS, KB, BLK, BLK), (2 * BLK) ** -0.5, 0.375, ((0, 128),)),
        "ocean_state": normal_values(streams_of[7], (OFIELDS, OLEV, OCELLS), 1.0, 6.0, ((2, 128),), jnp.float32),
        "ocean_neighbors": draw_ocean_neighbors(jax.random.fold_in(streams_of[11], 71), 0),
        "edge_weights": jnp.clip(jnp.exp(math.log(0.14) - 1.9459102 * jax.random.uniform(streams_of[9], (6, OCELLS), jnp.float32) ** levels(streams_of[9], (6, OCELLS), ((1, 128),), -0.2, 0.2)), 0.02, 0.14),
        "ocean_coupling": normal_values(streams_of[10], (OFIELDS, NFLUX), NFLUX ** -0.5, 1.75, (), jnp.float32),
    }


TIME_STEP = 0.02
RELAX_RATE = 5.0
MIXING_RATE = 5.0
OCEAN_MIXING = 0.2
OCEAN_ROTATION = 0.2
FORCING_SCALE = 0.25
SATURATION = 0.5

def gll_derivative():
    points = np.array([-1.0, -1.0 / np.sqrt(5.0), 1.0 / np.sqrt(5.0), 1.0])
    products = np.array([np.prod([points[r] - points[s] for s in range(4) if s != r]) for r in range(4)])
    deriv_table = np.zeros((4, 4))
    for r in range(4):
        for s in range(4):
            if r != s:
                deriv_table[r, s] = products[r] / (products[s] * (points[r] - points[s]))
        deriv_table[r, r] = sum((1.0 / (points[r] - points[s]) for s in range(4) if s != r))
    return 2.0 * deriv_table

def derivative_x(atm_field):
    n_fields, n_levels, x_nodes, y_nodes = atm_field.shape
    shaped = atm_field.reshape(n_fields, n_levels, x_nodes // 4, 4, y_nodes)
    deriv_table = jnp.asarray(gll_derivative(), jnp.float32)
    result = jnp.einsum('ij,flejy->fleiy', deriv_table, shaped, precision=lax.Precision.HIGHEST)
    return result.reshape(atm_field.shape)

def derivative_y(atm_field):
    n_fields, n_levels, x_nodes, y_nodes = atm_field.shape
    shaped = atm_field.reshape(n_fields, n_levels, x_nodes, y_nodes // 4, 4)
    deriv_table = jnp.asarray(gll_derivative(), jnp.float32)
    result = jnp.einsum('ij,flxej->flxei', deriv_table, shaped, precision=lax.Precision.HIGHEST)
    return result.reshape(atm_field.shape)

def vertical_mix(column_field):
    above = jnp.concatenate([column_field[:, 1:], column_field[:, -1:]], axis=1)
    below = jnp.concatenate([column_field[:, :1], column_field[:, :-1]], axis=1)
    return above - 2.0 * column_field + below

def advance(atm_field, level_winds, physics_flags, coriolis):
    slope_x = derivative_x(atm_field)
    slope_y = derivative_y(atm_field)
    wind_x = level_winds[0][None, :, None, None]
    wind_y = level_winds[1][None, :, None, None]
    advection = -(wind_x * slope_x + wind_y * slope_y)
    u_tend = advection[0] - slope_x[3] + coriolis * atm_field[1]
    v_tend = advection[1] - slope_y[3] - coriolis * atm_field[0]
    col_mean = lax.optimization_barrier(jnp.mean(atm_field[2], axis=0, keepdims=True))
    t_tend = advection[2] + jnp.where(physics_flags == 1, RELAX_RATE * (col_mean - atm_field[2]), 0.0)
    h_tend = advection[3] - (slope_x[0] + slope_y[1])
    tendency = jnp.stack([u_tend, v_tend, t_tend, h_tend])
    tendency = tendency + jnp.where(physics_flags == 2, MIXING_RATE * vertical_mix(atm_field), 0.0)
    return atm_field + TIME_STEP * tendency

def average_x(padded):
    inner_count = padded.shape[2] - 2
    middle = padded[:, :, 1:-1]
    left_side = padded[:, :, :-2]
    right_side = padded[:, :, 2:]
    position = (jnp.arange(inner_count) % 4)[:, None]
    return jnp.where(position == 0, 0.5 * (middle + left_side), jnp.where(position == 3, 0.5 * (middle + right_side), middle))

def average_y(padded):
    inner_count = padded.shape[3] - 2
    middle = padded[:, :, :, 1:-1]
    left_side = padded[:, :, :, :-2]
    right_side = padded[:, :, :, 2:]
    position = jnp.arange(inner_count) % 4
    return jnp.where(position == 0, 0.5 * (middle + left_side), jnp.where(position == 3, 0.5 * (middle + right_side), middle))

def surface_flux(atm_field, flux_matrix):
    bottom = atm_field[:, 0]
    wind_speed = jnp.sqrt(bottom[0] * bottom[0] + bottom[1] * bottom[1] + 1.0)
    mixed_flux = jnp.einsum('cf,fxy->xcy', flux_matrix, bottom, precision=lax.Precision.HIGHEST)
    return mixed_flux * wind_speed[:, None, :] / jnp.sqrt(1.0 + SATURATION * mixed_flux * mixed_flux)

def ocean_update(ocean, neighbor_values, edge_weights, forcing, ocean_coupling):
    lateral = lax.optimization_barrier(jnp.sum(edge_weights[None, None] * (neighbor_values - ocean[:, :, None, :]), axis=2))
    zero_part = jnp.zeros_like(ocean[0])
    rotation = jnp.stack([zero_part, zero_part, OCEAN_ROTATION * ocean[3], -OCEAN_ROTATION * ocean[2]])
    top_term = FORCING_SCALE * jnp.einsum('gc,cn->gn', ocean_coupling, forcing, precision=lax.Precision.HIGHEST)
    updated = ocean + lateral + OCEAN_MIXING * vertical_mix(ocean) + rotation
    return updated.at[:, 0].add(top_term)

def regrid_mean(flux_field, regrid_source, regrid_weights):
    blocks = flux_field.reshape(XN_TOT, NFLUX, N_COMP, BLK).transpose(0, 2, 1, 3).reshape(XN_TOT * N_COMP, NFLUX, BLK)
    gathered = blocks[regrid_source]
    device_count = N_TILE * N_COMP

    def one_device(pair):
        flux_part, weight_part = pair
        return jnp.einsum('bkfa,bkac->fbc', flux_part.astype(jnp.float32), weight_part.astype(jnp.float32), precision=lax.Precision.HIGHEST)
    mapped = lax.map(one_device, (gathered.reshape(device_count, OB_DEV, KB, NFLUX, BLK), regrid_weights.reshape(device_count, OB_DEV, KB, BLK, BLK)))
    return mapped.transpose(1, 0, 2, 3).reshape(NFLUX, OCELLS)

def reference(atm_state, level_winds, physics_flags, flux_matrix, regrid_source, regrid_weights, return_weights, ocean_state, ocean_neighbors, edge_weights, ocean_coupling):
    y_global = jnp.arange(YN_TOT).astype(jnp.float32)
    coriolis = 0.5 * jnp.sin(2.0 * jnp.pi * (y_global + 0.5) / YN_TOT)
    atm_field = atm_state
    flux_total = jnp.zeros((XN_TOT, NFLUX, YN_TOT), jnp.float32)
    for step_index in range(ATM_STEPS):
        atm_field = advance(atm_field, level_winds, physics_flags, coriolis)
        padded = jnp.concatenate([atm_field[:, :, -1:], atm_field, atm_field[:, :, :1]], axis=2)
        halfway = average_x(padded)
        padded = jnp.concatenate([halfway[:, :, :, -1:], halfway, halfway[:, :, :, :1]], axis=3)
        atm_field = average_y(padded)
        flux_total = flux_total + surface_flux(atm_field, flux_matrix)
    mean_flux = (flux_total / ATM_STEPS).astype(jnp.bfloat16)
    forcing = regrid_mean(mean_flux, regrid_source, regrid_weights)
    cell_ids = jnp.arange(OCELLS).astype(jnp.int32)
    neighbor_index = ((cell_ids[None, :] + ocean_neighbors.astype(jnp.int32) - HALO) % OCELLS).astype(jnp.int32)
    ocean = ocean_state
    for step_index in range(OCEAN_STEPS):
        neighbor_values = jnp.take(ocean, neighbor_index, axis=2)
        ocean = ocean_update(ocean, neighbor_values, edge_weights, forcing, ocean_coupling)
    surface = ocean[:, 0].astype(jnp.bfloat16)
    device_count = N_TILE * N_COMP

    def one_return(pair):
        surface_part, weight_part = pair
        return jnp.einsum('fbc,bkca->bkfa', surface_part.astype(jnp.float32), weight_part.astype(jnp.float32), precision=lax.Precision.HIGHEST)
    surface_blocks = surface.reshape(OFIELDS, device_count, OB_DEV, BLK).transpose(1, 0, 2, 3)
    parts = lax.map(one_return, (surface_blocks, return_weights.reshape(device_count, OB_DEV, KB, BLK, BLK)))
    parts = parts.reshape(OBLOCKS * KB, OFIELDS, BLK)
    summed = jax.ops.segment_sum(parts, regrid_source.reshape(OBLOCKS * KB), num_segments=XN_TOT * N_COMP)
    ocean_on_atm = summed.reshape(XN_TOT, N_COMP, OFIELDS, BLK).transpose(2, 0, 1, 3).reshape(OFIELDS, XN_TOT, YN_TOT)
    return (atm_field, ocean, ocean_on_atm)
```

```python
import functools

import jax
import jax.numpy as jnp
import ml_dtypes
import numpy as np
from jax import lax
from jax.experimental import pallas as pl
from jax.experimental.pallas import tpu as pltpu
from jax.sharding import PartitionSpec as P

F32 = jnp.float32
BF16 = jnp.bfloat16
I32 = jnp.int32
N_TILE, N_COMP = 32, 4
STEPS = 4
LEVELS = 16
NFLUX = 12
DT = 0.02
VMEM = pl.BlockSpec(memory_space=pltpu.VMEM)
SMEM = pl.BlockSpec(memory_space=pltpu.SMEM)
STATE_PLANES = 64
X_PLANES = 74
Y_PLANES = 12


def gll_derivative():
    points = np.array([-1.0, -1.0 / np.sqrt(5.0), 1.0 / np.sqrt(5.0), 1.0])
    products = np.array(
        [np.prod([points[r] - points[s] for s in range(4) if s != r]) for r in range(4)]
    )
    table = np.zeros((4, 4))
    for r in range(4):
        for s in range(4):
            if r != s:
                table[r, s] = products[r] / (products[s] * (points[r] - points[s]))
    table[0, 0], table[3, 3] = -3.0, 3.0
    return 2.0 * table


DERIV = gll_derivative()
ROW_SCALE = np.array([1.375, 1.125, 1.125, 1.375])


def lane_matrices():
    scaled = (DERIV * ROW_SCALE[:, None]).astype(ml_dtypes.bfloat16).astype(np.float64)
    deriv = np.kron(np.eye(32), scaled)
    average = np.eye(128)
    for e in range(31):
        left, right = 4 * e + 3, 4 * e + 4
        average[left, left] = average[left, right] = 0.5
        average[right, left] = average[right, right] = 0.5
    first = np.concatenate([deriv.T, np.eye(128)], axis=1)
    later = np.concatenate([(deriv @ average).T, average.T], axis=1)
    steps = np.stack([np.concatenate([m, m], axis=0) for m in (first, later)])
    out_a, out_b = np.zeros((128, 128)), np.zeros((128, 128))
    out_a[:, :64] = average.T[:, 16:80]
    out_b[:, 64:] = average.T[:, 48:112]
    final = np.concatenate([out_a, out_a, out_b, out_b], axis=0)
    return steps.astype(ml_dtypes.bfloat16), final.astype(ml_dtypes.bfloat16)


def lane_vectors():
    vec = np.zeros((16, 128), np.float32)
    lane = np.arange(128)
    vec[0] = 1.0 / ROW_SCALE[lane % 4]
    for c in range(N_COMP):
        for h in range(2):
            y = c * 128 + lane + (-16 if h == 0 else 16)
            vec[1 + 2 * c + h] = DT * 0.5 * np.sin(2.0 * np.pi * (y + 0.5) / (128 * N_COMP))
    return vec


def split_bf16(x):
    hi = x.astype(BF16)
    return hi, (x - hi.astype(F32)).astype(BF16)


def iota(shape, dim):
    return lax.broadcasted_iota(I32, shape, dim)


def mm(a, b):
    return jnp.dot(a, b, preferred_element_type=F32)


def mm_t(a, b):
    return lax.dot_general(a, b, (((0,), (0,)), ((), ())), preferred_element_type=F32)


def slots_kernel(src_ref, wanted_ref, tcol_ref):
    s = src_ref[...] >> 2
    tile = (s >> 5).astype(F32)
    row = (s & 31).astype(F32)
    r0, a0 = iota((64, 8), 0), iota((64, 8), 1)
    pick_row = ((r0 >> 3) == a0).astype(F32)
    own = (r0 & 7) == a0
    tile_c = jnp.sum(jnp.where(own, mm(pick_row, tile), 0.0), axis=1, keepdims=True)
    b1, r1 = iota((8, 64), 0), iota((8, 64), 1)
    pick_col = (b1 == (r1 & 7)).astype(F32)
    own_t = b1 == (r1 >> 3)
    tile_r = jnp.sum(jnp.where(own_t, mm(tile, pick_col), 0.0), axis=0, keepdims=True)
    row_r = jnp.sum(jnp.where(own_t, mm(row, pick_col), 0.0), axis=0, keepdims=True)
    same = jnp.where(tile_c == tile_r, 1.0, 0.0)
    sub, lane = iota((64, 64), 0), iota((64, 64), 1)
    rank_c = jnp.sum(jnp.where(lane < sub, same, 0.0), axis=1, keepdims=True)
    rank_r = jnp.sum(jnp.where(sub < lane, same, 0.0), axis=0, keepdims=True)
    slot_c = (tile_c * 4.0 + rank_c).astype(I32)
    slot_r = (tile_r * 4.0 + rank_r).astype(I32)
    slot_wide = jnp.broadcast_to(slot_c, (64, 128))
    field = iota((64, 8, 128), 1)
    tcol = jnp.where(field < 4, slot_wide[:, None, :] * 4 + field, -1)
    tcol_ref[...] = tcol.reshape(512, 128)
    q = iota((512, 64), 0)
    val = jnp.sum(jnp.where((q >> 2) == slot_r, row_r + 1.0, 0.0), axis=1, keepdims=True) - 1.0
    f = (iota((512, 1), 0) & 3).astype(F32)
    target = jnp.where(val >= 0.0, f * 32.0 + val, -1.0)
    wanted_ref[...] = jnp.broadcast_to(target, (512, 128)).astype(BF16)


def x_pack_kernel(par_ref, atm_ref, flags_ref, ocean_ref, off_ref, w_ref, out_ref):
    par = par_ref[0]
    flags = flags_ref[...].astype(F32)
    off = off_ref[...].astype(F32)
    pad = jnp.zeros((2, 128), F32)
    for slot, rows, cells in ((par, 16, 768), (1 - par, 0, 0)):
        out_ref[slot, 0:64] = atm_ref[:, rows : rows + 16, :].astype(BF16)
        out_ref[slot, 64] = flags[rows : rows + 16].astype(BF16)
        for part in range(2):
            lanes = slice(cells + 128 * part, cells + 128 * part + 128)
            values = ocean_ref[:, lanes].reshape(4, 16, 128)
            out_ref[slot, 65 + 4 * part : 69 + 4 * part] = values.astype(BF16)
        last = slice(896, 1024) if cells else slice(0, 128)
        pair = jnp.concatenate([off[:, last], pad, w_ref[:, last], pad], axis=0)
        out_ref[slot, 73] = pair.astype(BF16)


def y_pack_kernel(par_ref, atm_ref, flags_ref, xa_ref, xb_ref, xp_ref, out_ref):
    par_t, par_c = par_ref[0], par_ref[1]
    comp = par_ref[2]
    even = par_t == 0
    lane = iota((64, 128), 1)

    def full_plane(main, p):
        a, b = xa_ref[p].astype(F32), xb_ref[p].astype(F32)
        return jnp.concatenate([main, jnp.where(even, a, b), jnp.where(even, b, a)], axis=0)

    def store(q, planes):
        right = jnp.zeros((64, 128), F32)
        left = jnp.zeros((64, 128), F32)
        for s, plane in enumerate(planes):
            here = (lane >> 4) == s
            right = jnp.where(here, pltpu.roll(plane, (s * 16 + 16) % 128, 1), right)
            left = jnp.where(here, pltpu.roll(plane, s * 16, 1) if s else plane, left)
        out_ref[par_c, q] = right.astype(BF16)
        out_ref[1 - par_c, q] = left.astype(BF16)

    def group(q, _):
        store(q, [full_plane(atm_ref[q * 8 + s], q * 8 + s) for s in range(8)])
        return 0

    lax.fori_loop(0, 8, group, 0)
    store(8, [full_plane(flags_ref[...].astype(F32), 64)])
    for j in range(3):
        for part in range(4):
            p = 65 + 4 * j + part
            rows = slice(16 * part, 16 * part + 16)
            if p >= X_PLANES:
                out_ref[0, 9 + j, rows] = jnp.zeros((16, 128), BF16)
                out_ref[1, 9 + j, rows] = jnp.zeros((16, 128), BF16)
                continue
            a, b = xa_ref[p].astype(F32), xb_ref[p].astype(F32)
            from_left, from_right = jnp.where(even, b, a), jnp.where(even, a, b)
            own_right, own_left = xp_ref[par_t, p].astype(F32), xp_ref[1 - par_t, p].astype(F32)
            right = jnp.where(comp == N_COMP - 1, from_left, own_right)
            left = jnp.where(comp == 0, from_right, own_left)
            out_ref[par_c, 9 + j, rows] = right.astype(BF16)
            out_ref[1 - par_c, 9 + j, rows] = left.astype(BF16)


def atm_kernel(
    par_ref,
    winds_ref,
    fm_ref,
    oc_ref,
    atm_ref,
    flags_ref,
    xa_ref,
    xb_ref,
    ya_ref,
    yb_ref,
    served_ref,
    rhs_ref,
    rout_ref,
    vec_ref,
    out_ref,
    rows_ref,
    cb_ref,
    abuf_ref,
    dbuf_ref,
    cs_ref,
    tm_ref,
    r5_ref,
    m5_ref,
    ts_ref,
    facc_ref,
    gs_ref,
):
    par_t, par_c = par_ref[0], par_ref[1]
    comp = par_ref[2]
    even_t, even_c = par_t == 0, par_c == 0
    lane = iota((64, 128), 1)

    def tiles(main, p, y_right, y_left, slot):
        a, b = xa_ref[p].astype(F32), xb_ref[p].astype(F32)
        full = jnp.concatenate([main, jnp.where(even_t, a, b), jnp.where(even_t, b, a)], axis=0)
        left = pltpu.roll(y_left, (128 - slot * 16) % 128, 1) if slot else y_left
        shift = (112 - slot * 16) % 128
        right = pltpu.roll(y_right, shift, 1) if shift else y_right
        ts_ref[slot, 0] = jnp.where(lane < 16, left, pltpu.roll(full, 16, 1))
        ts_ref[slot, 1] = jnp.where(lane >= 112, right, pltpu.roll(full, 112, 1))

    def y_sides(q):
        a, b = ya_ref[q].astype(F32), yb_ref[q].astype(F32)
        return jnp.where(even_c, a, b), jnp.where(even_c, b, a)

    def put(h, l, k, i, value):
        hi, lo = split_bf16(value)
        cb_ref[h, l, k, i, :, 0:128] = hi
        cb_ref[h, l, k, i, :, 128:256] = lo

    def load_group(q, _):
        y_right, y_left = y_sides(q)
        k, half = q // 2, q % 2
        for s in range(8):
            p = q * 8 + s
            tiles(atm_ref[p], p, y_right, y_left, s)
        for s in range(8):
            for h in range(2):
                for i in range(4):
                    put(h, half * 8 + s, k, i, ts_ref[s, h, pl.ds(i, 16, stride=4), :])
        return 0

    lax.fori_loop(0, 8, load_group, 0)
    y_right, y_left = y_sides(8)
    tiles(flags_ref[...].astype(F32), 64, y_right, y_left, 0)
    for h in range(2):
        for i in range(4):
            flag = ts_ref[0, h, pl.ds(i, 16, stride=4), :]
            r5_ref[h, i] = jnp.where(flag == 1.0, 5.0 * DT, 0.0)
            m5_ref[h, i] = jnp.where(flag == 2.0, 5.0 * DT, 0.0)
            total = jnp.zeros((16, 128), F32)
            for l in range(LEVELS):
                pair = cb_ref[h, l, 2, i].astype(F32)
                total = total + (pair[:, 0:128] + pair[:, 128:256])
            cs_ref[h, i] = total
    facc_ref[...] = jnp.zeros_like(facc_ref)

    def main_view(l):
        left = cb_ref[0, l].reshape(256, 256)
        right = cb_ref[1, l].reshape(256, 256)
        both = jnp.concatenate([left, right], axis=1)
        return mm(both, rout_ref[...]).reshape(4, 4, 16, 128)

    inv = vec_ref[0:1, :]
    dt_y = -DT * inv

    def step(si, _):
        which = jnp.minimum(si, 1)

        def one_tile(h, _):
            ff = vec_ref[pl.ds(1 + 2 * comp + h, 1), :]
            hi, lo = split_bf16(cs_ref[h].reshape(64, 128) * (1.0 / LEVELS))
            tm = mm(jnp.concatenate([hi, lo], axis=1), rhs_ref[which])
            tm_ref[...] = tm[:, 128:256].reshape(4, 16, 128)
            cs_ref[h] = jnp.zeros((4, 16, 128), F32)

            def expand(l):
                both = mm(cb_ref[h, l].reshape(256, 256), rhs_ref[which])
                dbuf_ref[l] = both[:, 0:128].reshape(4, 4, 16, 128)
                abuf_ref[l] = both[:, 128:256].reshape(4, 4, 16, 128)

            expand(0)
            expand(1)

            def level(l, _):
                expand(jnp.minimum(l + 2, LEVELS - 1))
                above, below = jnp.minimum(l + 1, LEVELS - 1), jnp.maximum(l - 1, 0)
                cx = -DT * winds_ref[0, l]
                cy = dt_y * winds_ref[1, l]
                a = [[abuf_ref[l, k, i] for i in range(4)] for k in range(4)]

                def dx(k, i):
                    total = None
                    for j in range(4):
                        if abs(DERIV[i, j]) > 1e-9:
                            term = float(DERIV[i, j]) * a[k][j]
                            total = term if total is None else total + term
                    return total

                new = [[None] * 4 for _ in range(4)]
                for i in range(4):
                    m5 = m5_ref[h, i]
                    d = [dx(k, i) for k in range(4)]
                    dy = [dbuf_ref[l, k, i] for k in range(4)]
                    extra = [
                        ff * a[1][i] - DT * d[3],
                        dt_y * dy[3] - ff * a[0][i],
                        r5_ref[h, i] * (tm_ref[i] - a[2][i]),
                        dt_y * dy[1] - DT * d[0],
                    ]
                    for k in range(4):
                        mix = abuf_ref[above, k, i] + abuf_ref[below, k, i] - 2.0 * a[k][i]
                        new[k][i] = a[k][i] + (
                            (cx * d[k] + cy * dy[k]) + (extra[k] + m5 * mix)
                        )
                for k in range(4):
                    first = 0.5 * (new[k][0] + pltpu.roll(new[k][3], 1, 0))
                    values = [first, new[k][1], new[k][2], pltpu.roll(first, 15, 0)]
                    for i in range(4):
                        put(h, l, k, i, values[i])
                        if k == 2:
                            cs_ref[h, i] += values[i]
                return 0

            lax.fori_loop(0, LEVELS, level, 0)
            return 0

        lax.fori_loop(0, 2, one_tile, 0)
        surface = main_view(0)
        for i in range(4):
            u, v, t, z = [surface[k, i, 0:8] for k in range(4)]
            speed = jnp.sqrt(u * u + v * v + 1.0)
            for c in range(NFLUX):
                m = (fm_ref[c, 0] * u + fm_ref[c, 1] * v) + (fm_ref[c, 2] * t + fm_ref[c, 3] * z)
                facc_ref[c, i] += speed * m * lax.rsqrt(1.0 + 0.5 * (m * m))
        return 0

    lax.fori_loop(0, STEPS, step, 0)

    def finish(l, _):
        value = main_view(l)
        for k in range(4):
            for i in range(4):
                out_ref[k * LEVELS + l, pl.ds(i, 8, stride=4), :] = value[k, i, 0:8]
        return 0

    lax.fori_loop(0, LEVELS, finish, 0)
    for i in range(4):
        mean = [(facc_ref[c, i] * (1.0 / STEPS)).astype(BF16).astype(F32) for c in range(NFLUX)]
        for g in range(4):
            total = oc_ref[g, 0] * mean[0]
            for c in range(1, NFLUX):
                total = total + oc_ref[g, c] * mean[c]
            gs_ref[g, pl.ds(i, 8, stride=4), :] = 0.25 * total
    table = gs_ref[...].reshape(128, 128).astype(BF16)
    pick = served_ref[...].astype(F32) == iota((512, 128), 1).astype(F32)
    rows_ref[...] = mm(jnp.where(pick, 1.0, 0.0).astype(BF16), table).astype(BF16)


def ocean_kernel(par_ref, ocean_ref, off_ref, w_ref, ya_ref, yb_ref, n2_ref, wm_ref, sw_ref, o1_ref):
    even_c = par_ref[1] == 0
    comp = par_ref[2]

    def halo_rows(j, part):
        rows = slice(16 * part, 16 * part + 16)
        a, b = ya_ref[9 + j, rows].astype(F32), yb_ref[9 + j, rows].astype(F32)
        return jnp.where(even_c, b, a), jnp.where(even_c, a, b)

    pieces = [halo_rows(n // 4, n % 4) for n in range(9)]
    left = [jnp.concatenate([p[0] for p in pieces[4 * n : 4 * n + 4]], axis=0) for n in range(2)]
    right = [jnp.concatenate([p[1] for p in pieces[4 * n : 4 * n + 4]], axis=0) for n in range(2)]
    values = {-2: left[0], -1: left[1], 8: right[0], 9: right[1]}
    for b in range(8):
        values[b] = ocean_ref[:, 128 * b : 128 * b + 128]
    offw = {-1: pieces[8][0], 8: pieces[8][1]}
    source = iota((384, 128), 0)
    lane = iota((1, 128), 1)
    level = iota((64, 128), 0) & 15

    def matrix(b):
        if b in offw:
            off, w = offw[b][0:6].astype(I32), offw[b][8:14]
        else:
            cells = slice(128 * b, 128 * b + 128)
            off, w = off_ref[:, cells], w_ref[:, cells].astype(BF16).astype(F32)
        total = jnp.zeros((384, 128), F32)
        for j in range(6):
            total = total + jnp.where(source == lane + off[j : j + 1], w[j : j + 1], 0.0)
        return total.astype(BF16), jnp.sum(w, axis=0, keepdims=True)

    def update(own, window, wm, sw):
        hi, lo = split_bf16(window)
        both = mm(jnp.concatenate([hi, lo], axis=0), wm)
        lateral = both[0:64] + both[64:128] - sw * own
        above = jnp.where(level == 15, own, pltpu.roll(own, 63, 0))
        below = jnp.where(level == 0, own, pltpu.roll(own, 1, 0))
        rot = jnp.concatenate([jnp.zeros((32, 128), F32), 0.2 * own[48:64], -0.2 * own[32:48]], axis=0)
        return own + lateral + 0.2 * (above - 2.0 * own + below) + rot

    for b in range(-1, 9):
        wm, sw = matrix(b)
        if 0 <= b < 8:
            wm_ref[b] = wm
            sw_ref[:, 128 * b : 128 * b + 128] = jnp.broadcast_to(sw, (8, 128))
        window = jnp.concatenate([values[b - 1], values[b], values[b + 1]], axis=1)
        o1_ref[b + 1] = update(values[b], window, wm, sw)
    for b in range(8):
        window = jnp.concatenate([o1_ref[b], o1_ref[b + 1], o1_ref[b + 2]], axis=1)
        cells = slice(128 * b, 128 * b + 128)
        n2_ref[:, cells] = update(o1_ref[b + 1], window, wm_ref[b], sw_ref[0:1, cells])


def request_matrix(tcol_ref):
    parts = []
    for chunk in range(4):
        hit = tcol_ref[...] == iota((512, 128), 1) + 128 * chunk
        parts.append(jnp.where(hit, 1.0, 0.0).astype(BF16))
    return jnp.concatenate(parts, axis=1)


def forcing_kernel(par_ref, rows_ref, tcol_ref, weights_ref, f_ref, edge_ref):
    par_c = par_ref[1]
    gathered = mm(request_matrix(tcol_ref), rows_ref[...])
    for b in range(8):
        lhs = jnp.concatenate(
            [gathered[(b * 8 + k) * 8 : (b * 8 + k) * 8 + 8] for k in range(8)], axis=1
        ).astype(BF16)
        f_ref[:, 128 * b : 128 * b + 128] = mm(lhs, weights_ref[b])
    edge_ref[par_c] = f_ref[:, 896:1024]
    edge_ref[1 - par_c] = f_ref[:, 0:128]


def return_kernel(
    par_ref,
    n2_ref,
    wm_ref,
    sw_ref,
    f_ref,
    ea_ref,
    eb_ref,
    tcol_ref,
    weights_ref,
    ocean_ref,
    sent_ref,
    parts_ref,
):
    even_c = par_ref[1] == 0
    ea, eb = ea_ref[...], eb_ref[...]
    blocks = [jnp.where(even_c, eb, ea)]
    blocks += [f_ref[:, 128 * b : 128 * b + 128] for b in range(8)]
    blocks += [jnp.where(even_c, ea, eb)]
    ocean_ref[...] = n2_ref[...]
    for b in range(8):
        cells = slice(128 * b, 128 * b + 128)
        window = jnp.concatenate(blocks[b : b + 3], axis=1)
        hi, lo = split_bf16(window)
        own = blocks[b + 1]
        both = mm(jnp.concatenate([hi.astype(F32), lo.astype(F32)], axis=0).astype(BF16), wm_ref[b])
        top = both[0:8] + both[8:16] + (1.8 - sw_ref[:, cells]) * own
        surface = []
        for k in range(4):
            value = n2_ref[16 * k : 16 * k + 1, cells] + top[k : k + 1]
            if k == 2:
                value = value + 0.2 * own[3:4]
            if k == 3:
                value = value - 0.2 * own[2:3]
            ocean_ref[16 * k : 16 * k + 1, cells] = value
            below = n2_ref[16 * k + 1 : 16 * k + 2, cells] + 0.2 * own[k : k + 1]
            ocean_ref[16 * k + 1 : 16 * k + 2, cells] = below
            surface.append(value)
        lhs = jnp.concatenate(surface + [jnp.zeros((4, 128), F32)], axis=0).astype(BF16)
        for k in range(8):
            part = mm(lhs, weights_ref[b, k])
            parts_ref[(b * 8 + k) * 8 : (b * 8 + k) * 8 + 8, :] = part
    sent_ref[...] = mm_t(request_matrix(tcol_ref), parts_ref[...].astype(BF16)).astype(BF16)


def collect_kernel(served_ref, incoming_ref, out_ref):
    pick = served_ref[...].astype(F32) == iota((512, 128), 1).astype(F32)
    owner = jnp.where(pick, 1.0, 0.0).astype(BF16)
    out_ref[...] = mm_t(owner, incoming_ref[...]).reshape(4, 32, 128)


def swap_pairs(n):
    near = [(i, i ^ 1) for i in range(n)]
    far = [(i, (i + 1) % n if i % 2 else (i - 1) % n) for i in range(n)]
    return near, far


def exchange(payload, axis, n):
    near, far = swap_pairs(n)
    return lax.ppermute(payload[0], axis, near), lax.ppermute(payload[1], axis, far)


def to_tiles(rows):
    moved = lax.all_to_all(
        rows.reshape(N_TILE, 16, 128), "tile", split_axis=0, concat_axis=0, tiled=True
    )
    return moved.reshape(512, 128)


def call(kernel, out, specs, scratch=(), mib=48, cost=None):
    return pl.pallas_call(
        kernel,
        out_shape=out,
        in_specs=specs,
        out_specs=jax.tree.map(lambda _: VMEM, out),
        scratch_shapes=list(scratch),
        compiler_params=pltpu.CompilerParams(vmem_limit_bytes=mib * 2**20),
        cost_estimate=cost,
    )


def per_device(
    atm_state,
    level_winds,
    physics_flags,
    flux_matrix,
    regrid_source,
    regrid_weights,
    return_weights,
    ocean_state,
    ocean_neighbors,
    edge_weights,
    ocean_coupling,
):
    S = jax.ShapeDtypeStruct
    t, c = lax.axis_index("tile"), lax.axis_index("comp")
    par = jnp.stack([t % 2, c % 2, c, t]).astype(I32)
    atm = atm_state.reshape(64, 32, 128)
    ocean = ocean_state.reshape(64, 1024)
    steps_np, final_np = lane_matrices()
    rhs, rout, vec = jnp.asarray(steps_np), jnp.asarray(final_np), jnp.asarray(lane_vectors())

    wanted, tcol = call(slots_kernel, (S((512, 128), BF16), S((512, 128), I32)), [VMEM])(
        regrid_source
    )
    served = to_tiles(wanted)
    x_payload = call(x_pack_kernel, S((2, X_PLANES, 16, 128), BF16), [SMEM] + [VMEM] * 5)(
        par, atm, physics_flags, ocean, ocean_neighbors, edge_weights
    )
    xa, xb = exchange(x_payload, "tile", N_TILE)
    y_payload = call(y_pack_kernel, S((2, Y_PLANES, 64, 128), BF16), [SMEM] + [VMEM] * 5)(
        par, atm, physics_flags, xa, xb, x_payload
    )
    ya, yb = exchange(y_payload, "comp", N_COMP)
    atm_final, rows = call(
        atm_kernel,
        (S((64, 32, 128), F32), S((512, 128), BF16)),
        [SMEM] * 4 + [VMEM] * 10,
        [
            pltpu.VMEM((2, LEVELS, 4, 4, 16, 256), BF16),
            pltpu.VMEM((LEVELS, 4, 4, 16, 128), F32),
            pltpu.VMEM((LEVELS, 4, 4, 16, 128), F32),
            pltpu.VMEM((2, 4, 16, 128), F32),
            pltpu.VMEM((4, 16, 128), F32),
            pltpu.VMEM((2, 4, 16, 128), F32),
            pltpu.VMEM((2, 4, 16, 128), F32),
            pltpu.VMEM((8, 2, 64, 128), F32),
            pltpu.VMEM((NFLUX, 4, 8, 128), F32),
            pltpu.VMEM((4, 32, 128), F32),
        ],
    )(
        par,
        level_winds,
        flux_matrix,
        ocean_coupling,
        atm,
        physics_flags,
        xa,
        xb,
        ya,
        yb,
        served,
        rhs,
        rout,
        vec,
    )
    mean_rows = to_tiles(rows)
    n2, wm, sw = call(
        ocean_kernel,
        (S((64, 1024), F32), S((8, 384, 128), BF16), S((8, 1024), F32)),
        [SMEM] + [VMEM] * 5,
        [pltpu.VMEM((10, 64, 128), F32)],
        cost=pl.CostEstimate(flops=2**27, bytes_accessed=2**24, transcendentals=0),
    )(par, ocean, ocean_neighbors, edge_weights, ya, yb)
    forcing, edges = call(forcing_kernel, (S((8, 1024), F32), S((2, 8, 128), F32)), [SMEM] + [VMEM] * 3)(
        par, mean_rows, tcol, regrid_weights.reshape(8, 1024, 128)
    )
    ea, eb = exchange(edges, ("tile", "comp"), N_TILE * N_COMP)
    ocean_final, sent = call(
        return_kernel,
        (S((64, 1024), F32), S((512, 128), BF16)),
        [SMEM] + [VMEM] * 8,
        [pltpu.VMEM((512, 128), F32)],
    )(par, n2, wm, sw, forcing, ea, eb, tcol, return_weights)
    incoming = to_tiles(sent)
    ocean_on_atm = call(collect_kernel, S((4, 32, 128), F32), [VMEM] * 2)(served, incoming)
    return (
        atm_final.reshape(atm_state.shape),
        ocean_final.reshape(ocean_state.shape),
        ocean_on_atm,
    )


def solution(mesh):
    return jax.shard_map(
        per_device,
        mesh=mesh,
        in_specs=(
            P(None, None, "tile", "comp"),
            P(),
            P("tile", "comp"),
            P(),
            P(("tile", "comp"), None),
            P(("tile", "comp"), None, None, None),
            P(("tile", "comp"), None, None, None),
            P(None, None, ("tile", "comp")),
            P(None, ("tile", "comp")),
            P(None, ("tile", "comp")),
            P(),
        ),
        out_specs=(
            P(None, None, "tile", "comp"),
            P(None, None, ("tile", "comp")),
            P(None, "tile", "comp"),
        ),
        check_vma=False,
    )
```

```python
import functools

import jax
import jax.numpy as jnp
import ml_dtypes
import numpy as np
from jax import lax
from jax.experimental import pallas as pl
from jax.experimental.pallas import tpu as pltpu
from jax.sharding import PartitionSpec as P

F32 = jnp.float32
BF16 = jnp.bfloat16
I32 = jnp.int32
N_TILE, N_COMP = 32, 4
STEPS = 4
LEVELS = 16
NFLUX = 12
DT = 0.02
VMEM = pl.BlockSpec(memory_space=pltpu.VMEM)
HBM = pl.BlockSpec(memory_space=pltpu.HBM)
SMEM = pl.BlockSpec(memory_space=pltpu.SMEM)
X_PLANES = 74
Y_ROWS = 672


def gll_derivative():
    points = np.array([-1.0, -1.0 / np.sqrt(5.0), 1.0 / np.sqrt(5.0), 1.0])
    products = np.array(
        [np.prod([points[r] - points[s] for s in range(4) if s != r]) for r in range(4)]
    )
    table = np.zeros((4, 4))
    for r in range(4):
        for s in range(4):
            if r != s:
                table[r, s] = products[r] / (products[s] * (points[r] - points[s]))
    table[0, 0], table[3, 3] = -3.0, 3.0
    return 2.0 * table


DERIV = gll_derivative()
ROW_SCALE = np.array([1.375, 1.125, 1.125, 1.375])


SCALED = (DERIV * ROW_SCALE[:, None]).astype(ml_dtypes.bfloat16).astype(np.float64)


def y_nodes():
    lane = np.arange(32)
    return np.where(lane < 16, 143 - lane, 15 - lane)


def lane_operators(nodes):
    count = len(nodes)
    deriv, average = np.zeros((count, count)), np.eye(count)
    where = {int(y): p for p, y in enumerate(nodes)}
    for y, p in where.items():
        for j in range(4):
            deriv[p, where[y - y % 4 + j]] = SCALED[y % 4, j]
        other = y - 1 if y % 4 == 0 else y + 1
        if y % 4 in (0, 3) and other in where:
            average[p, p] = average[p, where[other]] = 0.5
    return deriv, average


def twice(*matrices):
    both = np.concatenate([m.T for m in matrices], axis=1)
    return np.concatenate([both, both], axis=0)


def lane_matrices():
    eye = np.eye(128)
    deriv, average = lane_operators(np.arange(128))
    main = np.stack([twice(deriv, eye), twice(deriv @ average, average)])
    halo_deriv, halo_average = lane_operators(y_nodes())
    dy, av = np.kron(np.eye(4), halo_deriv), np.kron(np.eye(4), halo_average)
    dx = np.kron(SCALED, np.eye(32))
    halo = np.stack([twice(dx, dy, eye), twice(dx @ av, dy @ av, av)])
    return np.concatenate([main, halo], axis=2).astype(ml_dtypes.bfloat16)


def lane_vectors():
    vec = np.zeros((16, 128), np.float32)
    lane = np.arange(128)
    halo = np.tile(y_nodes(), 4)
    vec[0] = 1.0 / ROW_SCALE[lane % 4]
    vec[1] = 1.0 / ROW_SCALE[halo % 4]
    vec[2] = 1.0 / ROW_SCALE[lane // 32]
    for c in range(N_COMP):
        for row, y in ((4 + c, lane), (8 + c, halo)):
            vec[row] = DT * 0.5 * np.sin(2.0 * np.pi * (c * 128 + y + 0.5) / (128 * N_COMP))
    return vec


def split_bf16(x):
    hi = x.astype(BF16)
    return hi, (x - hi.astype(F32)).astype(BF16)


def iota(shape, dim):
    return lax.broadcasted_iota(I32, shape, dim)


def mm(a, b):
    return jnp.dot(a, b, preferred_element_type=F32)


def mm_t(a, b):
    return lax.dot_general(a, b, (((0,), (0,)), ((), ())), preferred_element_type=F32)


def slots_kernel(src_ref, wanted_ref, tcol_ref):
    s = src_ref[...] >> 2
    tile = (s >> 5).astype(F32)
    row = (s & 31).astype(F32)
    r0, a0 = iota((64, 8), 0), iota((64, 8), 1)
    pick_row = ((r0 >> 3) == a0).astype(F32)
    own = (r0 & 7) == a0
    tile_c = jnp.sum(jnp.where(own, mm(pick_row, tile), 0.0), axis=1, keepdims=True)
    b1, r1 = iota((8, 64), 0), iota((8, 64), 1)
    pick_col = (b1 == (r1 & 7)).astype(F32)
    own_t = b1 == (r1 >> 3)
    tile_r = jnp.sum(jnp.where(own_t, mm(tile, pick_col), 0.0), axis=0, keepdims=True)
    row_r = jnp.sum(jnp.where(own_t, mm(row, pick_col), 0.0), axis=0, keepdims=True)
    same = jnp.where(tile_c == tile_r, 1.0, 0.0)
    sub, lane = iota((64, 64), 0), iota((64, 64), 1)
    rank_c = jnp.sum(jnp.where(lane < sub, same, 0.0), axis=1, keepdims=True)
    rank_r = jnp.sum(jnp.where(sub < lane, same, 0.0), axis=0, keepdims=True)
    slot_c = (tile_c * 4.0 + rank_c).astype(I32)
    slot_r = (tile_r * 4.0 + rank_r).astype(I32)
    slot_wide = jnp.broadcast_to(slot_c, (64, 128))
    field = iota((64, 8, 128), 1)
    tcol = jnp.where(field < 4, slot_wide[:, None, :] * 4 + field, -1)
    tcol_ref[...] = tcol.reshape(512, 128)
    q = iota((512, 64), 0)
    val = jnp.sum(jnp.where((q >> 2) == slot_r, row_r + 1.0, 0.0), axis=1, keepdims=True) - 1.0
    f = (iota((512, 1), 0) & 3).astype(F32)
    target = jnp.where(val >= 0.0, f * 32.0 + val, -1.0)
    wanted_ref[...] = jnp.broadcast_to(target, (512, 128)).astype(BF16)


def one_hot(rows, target):
    return jnp.where(iota((rows, 256), 0) == target, 1.0, 0.0).astype(BF16)


def pack_matrix():
    col = iota((1, 256), 1)
    lane = col & 127
    plane = ((lane >> 4) & 1) * 4 + (lane >> 5)
    return one_hot(1024, plane * 128 + (lane & 15) + jnp.where(col < 128, 0, 112))


def unpack_matrix():
    col = iota((1, 256), 1)
    quarter, n = (col & 127) >> 5, col & 31
    base = 32 * quarter + 16 * (col >> 7)
    return one_hot(256, base + jnp.where(n < 16, 15 - n, 159 - n))


def x_pack_kernel(
    par_ref, atm_ref, flags_ref, ocean_ref, off_ref, w_ref, a_ref, b_ref, flags_out_ref
):
    even = par_ref[0] == 0

    def put(index, right, left):
        a_ref[index] = jnp.where(even, right, left).astype(BF16)
        b_ref[index] = jnp.where(even, left, right).astype(BF16)

    put(slice(0, 64), atm_ref[:, 16:32, :], atm_ref[:, 0:16, :])
    flags = flags_ref[...].astype(F32)
    flags_out_ref[...] = flags
    put(64, flags[16:32], flags[0:16])
    for part in range(2):
        right, left = [
            ocean_ref[:, c + 128 * part : c + 128 * part + 128].reshape(4, 16, 128) for c in (768, 0)
        ]
        put(slice(65 + 4 * part, 69 + 4 * part), right, left)
    off = off_ref[...].astype(F32)
    pad = jnp.zeros((2, 128), F32)
    right, left = [
        jnp.concatenate([off[:, c : c + 128], pad, w_ref[:, c : c + 128], pad], axis=0)
        for c in (896, 0)
    ]
    put(73, right, left)


def x_extended(ts_ref, slot, main, xa_ref, xb_ref, p, even):
    a, b = xa_ref[p].astype(F32), xb_ref[p].astype(F32)
    ts_ref[slot, 0:32] = main
    ts_ref[slot, 32:48] = jnp.where(even, a, b)
    ts_ref[slot, 48:64] = jnp.where(even, b, a)
    return [ts_ref[slot, pl.ds(i, 16, stride=4), :] for i in range(4)]


def y_pack_kernel(
    par_ref, atm_ref, flags_ref, xa_ref, xb_ref, pa_ref, pb_ref, a_ref, b_ref, lhs_ref, ts_ref
):
    even_t, even_c = par_ref[0] == 0, par_ref[1] == 0
    comp = par_ref[2]

    def group(q, _):
        for s in range(8):
            p = q * 8 + s
            rows = x_extended(ts_ref, s, atm_ref[p], xa_ref, xb_ref, p, even_t)
            for i in range(4):
                lanes = slice(((s % 2) * 4 + i) * 128, ((s % 2) * 4 + i) * 128 + 128)
                lhs_ref[q * 4 + s // 2, :, lanes] = rows[i].astype(BF16)
        return 0

    lax.fori_loop(0, 8, group, 0)
    rows = x_extended(ts_ref, 0, flags_ref[...], xa_ref, xb_ref, 64, even_t)
    for i in range(4):
        lhs_ref[32, :, 128 * i : 128 * i + 128] = rows[i].astype(BF16)
    lhs_ref[32, :, 512:1024] = jnp.zeros((16, 512), BF16)
    moved = mm(lhs_ref[...].reshape(528, 1024), pack_matrix())
    left, right = moved[:, 0:128], moved[:, 128:256]
    a_ref[0:528] = jnp.where(even_c, right, left).astype(BF16)
    b_ref[0:528] = jnp.where(even_c, left, right).astype(BF16)
    for n in range(9):
        p = 65 + n
        dest = slice(528 + 16 * n, 544 + 16 * n)
        a, b = xa_ref[p].astype(F32), xb_ref[p].astype(F32)
        own_a, own_b = pa_ref[p].astype(F32), pb_ref[p].astype(F32)
        from_left, from_right = jnp.where(even_t, b, a), jnp.where(even_t, a, b)
        own_right, own_left = jnp.where(even_t, own_a, own_b), jnp.where(even_t, own_b, own_a)
        right = jnp.where(comp == N_COMP - 1, from_left, own_right)
        left = jnp.where(comp == 0, from_right, own_left)
        a_ref[dest] = jnp.where(even_c, right, left).astype(BF16)
        b_ref[dest] = jnp.where(even_c, left, right).astype(BF16)


def prepare_kernel(par_ref, atm_ref, flags_ref, xa_ref, xb_ref, cb_ref, flag_ref, ts_ref):
    even_t = par_ref[0] == 0

    def group(q, _):
        for s in range(8):
            p = q * 8 + s
            rows = x_extended(ts_ref, s, atm_ref[p], xa_ref, xb_ref, p, even_t)
            for i in range(4):
                hi, lo = split_bf16(rows[i])
                cb_ref[(q % 2) * 8 + s, q // 2, i, :, 0:128] = hi
                cb_ref[(q % 2) * 8 + s, q // 2, i, :, 128:256] = lo
        return 0

    lax.fori_loop(0, 8, group, 0)
    rows = x_extended(ts_ref, 0, flags_ref[...], xa_ref, xb_ref, 64, even_t)
    for i in range(4):
        flag_ref[i] = rows[i]


def x_slopes(a):
    sums, diffs = (a[0] + a[3], a[1] + a[2]), (a[0] - a[3], a[1] - a[2])
    across = sums[0] - sums[1]
    out = [None] * 4
    for i in range(2):
        d = DERIV[i]
        odd = float((d[0] - d[3]) / 2) * diffs[0] + float((d[1] - d[2]) / 2) * diffs[1]
        even = float((d[0] + d[3]) / 2) * across
        out[i], out[3 - i] = odd + even, odd - even
    return out


def atm_kernel(
    par_ref,
    scal_ref,
    first_ref,
    flag_ref,
    ya_ref,
    yb_ref,
    vec_ref,
    rhs_ref,
    out_ref,
    table_ref,
    cb_ref,
    abuf_ref,
    dbuf_ref,
    hcb_ref,
    hbuf_ref,
    tm_ref,
    mask_ref,
    r5_ref,
    facc_ref,
    gs_ref,
    first_sem,
    copies,
):
    first_copy = pltpu.make_async_copy(first_ref, cb_ref, first_sem)
    first_copy.start()
    even_c = par_ref[1] == 0
    comp = par_ref[2]
    lane = iota((16, 128), 1)
    edge = (lane == 0) | (lane == 127)
    quarter = lane >> 5
    halo_edge = ((lane & 31) == 15) | ((lane & 31) == 16)

    def put(ref, index, value):
        hi, lo = split_bf16(value)
        ref[(*index, slice(None), slice(0, 128))] = hi
        ref[(*index, slice(None), slice(128, 256))] = lo

    ya, yb = ya_ref[0:528].astype(F32), yb_ref[0:528].astype(F32)
    from_right, from_left = jnp.where(even_c, ya, yb), jnp.where(even_c, yb, ya)
    arrived = jnp.concatenate([from_right, from_left], axis=1).astype(BF16)
    halo = mm(arrived, unpack_matrix()).astype(BF16)
    for k in range(4):
        for l in range(LEVELS):
            rows = slice((k * 8 + l // 2) * 16, (k * 8 + l // 2) * 16 + 16)
            lanes = slice((l % 2) * 128, (l % 2) * 128 + 128)
            hcb_ref[l, k, :, 0:128] = halo[rows, lanes]
            hcb_ref[l, k, :, 128:256] = jnp.zeros((16, 128), BF16)
    halo_flag = halo[512:528, 0:128].astype(F32)
    halo_r5 = jnp.where(halo_flag == 1.0, 5.0 * DT, 0.0)
    halo_m5 = jnp.where(halo_flag == 2.0, 5.0 * DT, 0.0)
    halo_keep = 1.0 - 2.0 * halo_m5
    halo_keep_t = halo_keep - halo_r5
    for i in range(4):
        flag = flag_ref[i]
        m5 = jnp.where(flag == 2.0, 5.0 * DT, 0.0)
        r5_ref[i] = jnp.where(flag == 1.0, 5.0 * DT, 0.0)
        mask_ref[0, i] = m5
        mask_ref[1, i] = 1.0 - 2.0 * m5
        mask_ref[2, i] = 1.0 - 2.0 * m5 - r5_ref[i]
    facc_ref[...] = jnp.zeros_like(facc_ref)
    dt_y = -DT * vec_ref[0:1, :]
    halo_dt_y = -DT * vec_ref[1:2, :]
    halo_dt_x = -DT * vec_ref[2:3, :]
    ff = vec_ref[pl.ds(4 + comp, 1), :]
    halo_ff = vec_ref[pl.ds(8 + comp, 1), :]
    for copy in (first_copy, *copies):
        copy.wait()

    def step(si, _):
        which = jnp.minimum(si, 1)
        both = mm(cb_ref[...].reshape(4096, 256), rhs_ref[which, :, 0:256])
        dbuf_ref[...] = both[:, 0:128].reshape(LEVELS, 4, 4, 16, 128)
        abuf_ref[...] = both[:, 128:256].reshape(LEVELS, 4, 4, 16, 128)
        hbuf_ref[...] = mm(hcb_ref[...].reshape(1024, 256), rhs_ref[which, :, 256:640]).reshape(
            LEVELS, 4, 16, 384
        )
        for i in range(4):
            total = abuf_ref[0, 2, i]
            for l in range(1, LEVELS):
                total = total + abuf_ref[l, 2, i]
            mask_ref[3, i] = r5_ref[i] * (total * (1.0 / LEVELS))
        total = hbuf_ref[0, 2, :, 256:384]
        for l in range(1, LEVELS):
            total = total + hbuf_ref[l, 2, :, 256:384]
        tm_ref[...] = halo_r5 * (total * (1.0 / LEVELS))

        def level(l, _):
            above, below = jnp.minimum(l + 1, LEVELS - 1), jnp.maximum(l - 1, 0)
            wind_x, wind_y = scal_ref[l], scal_ref[LEVELS + l]
            cx = -DT * wind_x
            cy = dt_y * wind_y
            a = [[abuf_ref[l, k, i] for i in range(4)] for k in range(4)]

            slopes = [x_slopes(a[k]) for k in range(4)]
            new = [[None] * 4 for _ in range(4)]
            for i in range(4):
                m5, keep, keep_t, relax = [mask_ref[n, i] for n in range(4)]
                d = [slopes[k][i] for k in range(4)]
                dy = [dbuf_ref[l, k, i] for k in range(4)]
                extra = [
                    ff * a[1][i] - DT * d[3],
                    dt_y * dy[3] - ff * a[0][i],
                    relax,
                    dt_y * dy[1] - DT * d[0],
                ]
                for k in range(4):
                    mix = m5 * (abuf_ref[above, k, i] + abuf_ref[below, k, i])
                    own = (keep_t if k == 2 else keep) * a[k][i]
                    new[k][i] = (own + mix) + ((cx * d[k] + cy * dy[k]) + extra[k])

            halo_cx, halo_cy = halo_dt_x * wind_x, halo_dt_y * wind_y
            hx, hy, ha = [
                [hbuf_ref[l, k, :, 128 * n : 128 * n + 128] for k in range(4)] for n in range(3)
            ]
            extra = [
                halo_ff * ha[1] + halo_dt_x * hx[3],
                halo_dt_y * hy[3] - halo_ff * ha[0],
                tm_ref[...],
                halo_dt_y * hy[1] + halo_dt_x * hx[0],
            ]
            for k in range(4):
                first = 0.5 * (new[k][0] + pltpu.roll(new[k][3], 1, 0))
                values = [first, new[k][1], new[k][2], pltpu.roll(first, 15, 0)]
                up, down = hbuf_ref[above, k, :, 256:384], hbuf_ref[below, k, :, 256:384]
                own = (halo_keep_t if k == 2 else halo_keep) * ha[k] + halo_m5 * (up + down)
                own = own + ((halo_cx * hx[k] + halo_cy * hy[k]) + extra[k])
                lower = pltpu.roll(pltpu.roll(own, 32, 1), 1, 0)
                upper = pltpu.roll(pltpu.roll(own, 96, 1), 15, 0)
                partner = jnp.where(quarter == 0, lower, jnp.where(quarter == 3, upper, own))
                own = 0.5 * (own + partner)
                across = None
                for i in range(4):
                    moved = pltpu.roll(values[i], 32 * i + 16, 1)
                    across = moved if i == 0 else jnp.where(quarter == i, moved, across)
                    back = pltpu.roll(own, 112 - 32 * i, 1)
                    put(cb_ref, (l, k, i), jnp.where(edge, 0.5 * (values[i] + back), values[i]))
                put(hcb_ref, (l, k), jnp.where(halo_edge, 0.5 * (own + across), own))
            return 0

        lax.fori_loop(0, LEVELS, level, 0, unroll=2)
        surface = mm(cb_ref[0].reshape(256, 256), rhs_ref[1, :, 128:256]).reshape(4, 4, 16, 128)
        for i in range(4):
            u, v, t, z = [surface[k, i, 0:8] for k in range(4)]
            speed = jnp.sqrt(u * u + v * v + 1.0)
            for c in range(NFLUX):
                m0, m1, m2, m3 = [scal_ref[32 + 4 * c + k] for k in range(4)]
                m = (m0 * u + m1 * v) + (m2 * t + m3 * z)
                facc_ref[c, i] += speed * m * lax.rsqrt(1.0 + 0.5 * (m * m))
        return 0

    lax.fori_loop(0, STEPS, step, 0)
    final = mm(cb_ref[...].reshape(4096, 256), rhs_ref[1, :, 128:256]).reshape(LEVELS, 4, 4, 16, 128)
    for l in range(LEVELS):
        for k in range(4):
            for i in range(4):
                out_ref[k * LEVELS + l, pl.ds(i, 8, stride=4), :] = final[l, k, i, 0:8]
    for i in range(4):
        mean = [(facc_ref[c, i] * (1.0 / STEPS)).astype(BF16).astype(F32) for c in range(NFLUX)]
        for g in range(4):
            total = scal_ref[80 + 12 * g] * mean[0]
            for c in range(1, NFLUX):
                total = total + scal_ref[80 + 12 * g + c] * mean[c]
            gs_ref[g, pl.ds(i, 8, stride=4), :] = 0.25 * total
    table_ref[...] = gs_ref[...].reshape(128, 128).astype(BF16)


def pick_kernel(served_ref, table_ref, rows_ref):
    pick = served_ref[...].astype(F32) == iota((512, 128), 1).astype(F32)
    rows_ref[...] = mm(jnp.where(pick, 1.0, 0.0).astype(BF16), table_ref[...]).astype(BF16)


def ocean_kernel(par_ref, ocean_ref, off_ref, w_ref, ya_ref, yb_ref, n2_ref, wm_ref, sw_ref, o1_ref):
    even_c = par_ref[1] == 0

    def halo_rows(n):
        rows = slice(528 + 16 * n, 544 + 16 * n)
        a, b = ya_ref[rows].astype(F32), yb_ref[rows].astype(F32)
        return jnp.where(even_c, b, a), jnp.where(even_c, a, b)

    pieces = [halo_rows(n) for n in range(9)]
    left = [jnp.concatenate([p[0] for p in pieces[4 * n : 4 * n + 4]], axis=0) for n in range(2)]
    right = [jnp.concatenate([p[1] for p in pieces[4 * n : 4 * n + 4]], axis=0) for n in range(2)]
    values = {-2: left[0], -1: left[1], 8: right[0], 9: right[1]}
    for b in range(8):
        values[b] = ocean_ref[:, 128 * b : 128 * b + 128]
    offw = {-1: pieces[8][0], 8: pieces[8][1]}
    source = iota((384, 128), 0)
    lane = iota((1, 128), 1)
    level = iota((64, 128), 0) & 15

    def matrix(b):
        if b in offw:
            off, w = offw[b][0:6].astype(I32), offw[b][8:14]
        else:
            cells = slice(128 * b, 128 * b + 128)
            off, w = off_ref[:, cells], w_ref[:, cells].astype(BF16).astype(F32)
        total = jnp.zeros((384, 128), F32)
        for j in range(6):
            total = total + jnp.where(source == lane + off[j : j + 1], w[j : j + 1], 0.0)
        return total.astype(BF16), jnp.sum(w, axis=0, keepdims=True)

    def update(own, window, wm, sw):
        hi, lo = split_bf16(window)
        both = mm(jnp.concatenate([hi, lo], axis=0), wm)
        lateral = both[0:64] + both[64:128] - sw * own
        above = jnp.where(level == 15, own, pltpu.roll(own, 63, 0))
        below = jnp.where(level == 0, own, pltpu.roll(own, 1, 0))
        rot = jnp.concatenate([jnp.zeros((32, 128), F32), 0.2 * own[48:64], -0.2 * own[32:48]], axis=0)
        return own + lateral + 0.2 * (above - 2.0 * own + below) + rot

    for b in range(-1, 9):
        wm, sw = matrix(b)
        if 0 <= b < 8:
            wm_ref[b] = wm
            sw_ref[:, 128 * b : 128 * b + 128] = jnp.broadcast_to(sw, (8, 128))
        window = jnp.concatenate([values[b - 1], values[b], values[b + 1]], axis=1)
        o1_ref[b + 1] = update(values[b], window, wm, sw)
    for b in range(8):
        window = jnp.concatenate([o1_ref[b], o1_ref[b + 1], o1_ref[b + 2]], axis=1)
        cells = slice(128 * b, 128 * b + 128)
        n2_ref[:, cells] = update(o1_ref[b + 1], window, wm_ref[b], sw_ref[0:1, cells])


def request_matrix(tcol_ref):
    parts = []
    for chunk in range(4):
        hit = tcol_ref[...] == iota((512, 128), 1) + 128 * chunk
        parts.append(jnp.where(hit, 1.0, 0.0).astype(BF16))
    return jnp.concatenate(parts, axis=1)


def forcing_kernel(par_ref, rows_ref, tcol_ref, weights_ref, f_ref, a_ref, b_ref):
    even_c = par_ref[1] == 0
    gathered = mm(request_matrix(tcol_ref), rows_ref[...])
    for b in range(8):
        lhs = jnp.concatenate(
            [gathered[(b * 8 + k) * 8 : (b * 8 + k) * 8 + 8] for k in range(8)], axis=1
        ).astype(BF16)
        f_ref[:, 128 * b : 128 * b + 128] = mm(lhs, weights_ref[b])
    right, left = f_ref[:, 896:1024], f_ref[:, 0:128]
    a_ref[...] = jnp.where(even_c, right, left)
    b_ref[...] = jnp.where(even_c, left, right)


def return_kernel(
    par_ref,
    n2_ref,
    wm_ref,
    sw_ref,
    f_ref,
    ea_ref,
    eb_ref,
    tcol_ref,
    weights_ref,
    ocean_ref,
    sent_ref,
    parts_ref,
):
    even_c = par_ref[1] == 0
    ea, eb = ea_ref[...], eb_ref[...]
    blocks = [jnp.where(even_c, eb, ea)]
    blocks += [f_ref[:, 128 * b : 128 * b + 128] for b in range(8)]
    blocks += [jnp.where(even_c, ea, eb)]
    ocean_ref[...] = n2_ref[...]
    for b in range(8):
        cells = slice(128 * b, 128 * b + 128)
        window = jnp.concatenate(blocks[b : b + 3], axis=1)
        hi, lo = split_bf16(window)
        own = blocks[b + 1]
        both = mm(jnp.concatenate([hi.astype(F32), lo.astype(F32)], axis=0).astype(BF16), wm_ref[b])
        top = both[0:8] + both[8:16] + (1.8 - sw_ref[:, cells]) * own
        surface = []
        for k in range(4):
            value = n2_ref[16 * k : 16 * k + 1, cells] + top[k : k + 1]
            if k == 2:
                value = value + 0.2 * own[3:4]
            if k == 3:
                value = value - 0.2 * own[2:3]
            ocean_ref[16 * k : 16 * k + 1, cells] = value
            below = n2_ref[16 * k + 1 : 16 * k + 2, cells] + 0.2 * own[k : k + 1]
            ocean_ref[16 * k + 1 : 16 * k + 2, cells] = below
            surface.append(value)
        lhs = jnp.concatenate(surface + [jnp.zeros((4, 128), F32)], axis=0).astype(BF16)
        wide = jnp.concatenate([weights_ref[b, k] for k in range(8)], axis=1)
        parts = mm(lhs, wide)
        for k in range(8):
            rows = slice((b * 8 + k) * 8, (b * 8 + k) * 8 + 8)
            parts_ref[rows, :] = parts[:, 128 * k : 128 * k + 128]
    sent_ref[...] = mm_t(request_matrix(tcol_ref), parts_ref[...].astype(BF16)).astype(BF16)


def collect_kernel(served_ref, incoming_ref, out_ref):
    pick = served_ref[...].astype(F32) == iota((512, 128), 1).astype(F32)
    owner = jnp.where(pick, 1.0, 0.0).astype(BF16)
    out_ref[...] = mm_t(owner, incoming_ref[...]).reshape(4, 32, 128)


def swap_pairs(n):
    near = [(i, i ^ 1) for i in range(n)]
    far = [(i, (i + 1) % n if i % 2 else (i - 1) % n) for i in range(n)]
    return near, far


def exchange(payloads, axis, n):
    near, far = swap_pairs(n)
    return lax.ppermute(payloads[0], axis, near), lax.ppermute(payloads[1], axis, far)


def to_tiles(rows):
    moved = lax.all_to_all(
        rows.reshape(N_TILE, 16, 128), "tile", split_axis=0, concat_axis=0, tiled=True
    )
    return moved.reshape(512, 128)


def call(kernel, out, specs, scratch=(), mib=16, cost=None):
    return pl.pallas_call(
        kernel,
        out_shape=out,
        in_specs=specs,
        out_specs=jax.tree.map(lambda _: VMEM, out),
        scratch_shapes=list(scratch),
        compiler_params=pltpu.CompilerParams(vmem_limit_bytes=mib * 2**20),
        cost_estimate=cost,
    )


def staged(kernel, out, scalars, resident, arrays, scratch=(), late=0, mib=16, cost=None):
    n_lead, n = len(scalars) + len(resident), len(arrays)
    n_out = len(jax.tree.leaves(out))

    def body(*refs):
        lead_refs, hbm_refs = refs[:n_lead], refs[n_lead : n_lead + n]
        out_refs = refs[n_lead + n : n_lead + n + n_out]
        held, (sems, *rest) = refs[-n - 1 - len(scratch) :][:n], refs[-1 - len(scratch) :]
        copies = [pltpu.make_async_copy(hbm_refs[i], held[i], sems.at[i]) for i in range(n)]
        for copy in copies:
            copy.start()
        for copy in copies[: n - late]:
            copy.wait()
        extra = (copies[n - late :],) if late else ()
        kernel(*lead_refs, *held, *out_refs, *rest, *extra)

    buffers = [pltpu.VMEM(a.shape, a.dtype) for a in arrays]
    scratch_shapes = buffers + [pltpu.SemaphoreType.DMA((n,))] + list(scratch)
    specs = [SMEM] * len(scalars) + [VMEM] * len(resident) + [HBM] * n
    return call(body, out, specs, scratch_shapes, mib, cost)(*scalars, *resident, *arrays)


ATM_SCRATCH = (
    pltpu.VMEM((LEVELS, 4, 4, 16, 256), BF16),
    pltpu.VMEM((LEVELS, 4, 4, 16, 128), F32),
    pltpu.VMEM((LEVELS, 4, 4, 16, 128), F32),
    pltpu.VMEM((LEVELS, 4, 16, 256), BF16),
    pltpu.VMEM((LEVELS, 4, 16, 384), F32),
    pltpu.VMEM((16, 128), F32),
    pltpu.VMEM((4, 4, 16, 128), F32),
    pltpu.VMEM((4, 16, 128), F32),
    pltpu.VMEM((NFLUX, 4, 8, 128), F32),
    pltpu.VMEM((4, 32, 128), F32),
    pltpu.SemaphoreType.DMA,
)


def per_device(
    atm_state,
    level_winds,
    physics_flags,
    flux_matrix,
    regrid_source,
    regrid_weights,
    return_weights,
    ocean_state,
    ocean_neighbors,
    edge_weights,
    ocean_coupling,
):
    S = jax.ShapeDtypeStruct
    t, c = lax.axis_index("tile"), lax.axis_index("comp")
    par = jnp.stack([t % 2, c % 2, c, t]).astype(I32)
    atm = atm_state.reshape(64, 32, 128)
    ocean = ocean_state.reshape(64, 1024)
    scal = jnp.concatenate(
        [level_winds.reshape(-1), flux_matrix.reshape(-1), ocean_coupling.reshape(-1)]
    )
    rhs = jnp.asarray(lane_matrices())
    vec = jnp.asarray(lane_vectors())

    xp_a, xp_b, flags = staged(
        x_pack_kernel,
        (S((X_PLANES, 16, 128), BF16),) * 2 + (S((32, 128), F32),),
        (par,),
        (),
        (atm, physics_flags, ocean, ocean_neighbors, edge_weights),
        mib=12,
    )
    xa, xb = exchange((xp_a, xp_b), "tile", N_TILE)
    wanted, tcol = call(slots_kernel, (S((512, 128), BF16), S((512, 128), I32)), [VMEM])(
        regrid_source
    )
    wanted, tcol, xb = lax.optimization_barrier((wanted, tcol, xb))
    served = to_tiles(wanted)
    y_payload = call(
        y_pack_kernel,
        (S((Y_ROWS, 128), BF16),) * 2,
        [SMEM] + [VMEM] * 6,
        [pltpu.VMEM((33, 16, 1024), BF16), pltpu.VMEM((8, 64, 128), F32)],
    )(par, atm, flags, xa, xb, xp_a, xp_b)
    ya, yb = exchange(y_payload, "comp", N_COMP)
    first, flag = call(
        prepare_kernel,
        (S((LEVELS, 4, 4, 16, 256), BF16), S((4, 16, 128), F32)),
        [SMEM] + [VMEM] * 4,
        [pltpu.VMEM((8, 64, 128), F32)],
        cost=pl.CostEstimate(flops=2**23, bytes_accessed=2**23, transcendentals=0),
    )(par, atm, flags, xa, xb)
    atm_final, table = staged(
        atm_kernel,
        (S((64, 32, 128), F32), S((128, 128), BF16)),
        (par, scal),
        (first, flag, ya, yb),
        (vec, rhs),
        ATM_SCRATCH,
        late=1,
        mib=32,
        cost=pl.CostEstimate(flops=2**33, bytes_accessed=2**26, transcendentals=0),
    )
    rows = call(pick_kernel, S((512, 128), BF16), [VMEM] * 2)(served, table)
    mean_rows = to_tiles(rows)
    n2, wm, sw = call(
        ocean_kernel,
        (S((64, 1024), F32), S((8, 384, 128), BF16), S((8, 1024), F32)),
        [SMEM] + [VMEM] * 5,
        [pltpu.VMEM((10, 64, 128), F32)],
        cost=pl.CostEstimate(flops=2**27, bytes_accessed=2**24, transcendentals=0),
    )(par, ocean, ocean_neighbors, edge_weights, ya, yb)
    forcing, *edges = call(
        forcing_kernel,
        (S((8, 1024), F32), S((8, 128), F32), S((8, 128), F32)),
        [SMEM] + [VMEM] * 3,
    )(par, mean_rows, tcol, regrid_weights.reshape(8, 1024, 128))
    ea, eb = exchange(edges, ("tile", "comp"), N_TILE * N_COMP)
    ocean_final, sent = call(
        return_kernel,
        (S((64, 1024), F32), S((512, 128), BF16)),
        [SMEM] + [VMEM] * 8,
        [pltpu.VMEM((512, 128), F32)],
    )(par, n2, wm, sw, forcing, ea, eb, tcol, return_weights)
    incoming = to_tiles(sent)
    ocean_on_atm = call(collect_kernel, S((4, 32, 128), F32), [VMEM] * 2)(served, incoming)
    return (
        atm_final.reshape(atm_state.shape),
        ocean_final.reshape(ocean_state.shape),
        ocean_on_atm,
    )


def solution(mesh):
    return jax.shard_map(
        per_device,
        mesh=mesh,
        in_specs=(
            P(None, None, "tile", "comp"),
            P(),
            P("tile", "comp"),
            P(),
            P(("tile", "comp"), None),
            P(("tile", "comp"), None, None, None),
            P(("tile", "comp"), None, None, None),
            P(None, None, ("tile", "comp")),
            P(None, ("tile", "comp")),
            P(None, ("tile", "comp")),
            P(),
        ),
        out_specs=(
            P(None, None, "tile", "comp"),
            P(None, None, ("tile", "comp")),
            P(None, "tile", "comp"),
        ),
        check_vma=False,
    )
```

```python
import functools

import jax
import jax.numpy as jnp
import ml_dtypes
import numpy as np
from jax import lax
from jax.experimental import pallas as pl
from jax.experimental.pallas import tpu as pltpu
from jax.sharding import PartitionSpec as P

F32 = jnp.float32
BF16 = jnp.bfloat16
I32 = jnp.int32
N_TILE, N_COMP = 32, 4
STEPS = 4
LEVELS = 16
NFLUX = 12
DT = 0.02
VMEM = pl.BlockSpec(memory_space=pltpu.VMEM)
SMEM = pl.BlockSpec(memory_space=pltpu.SMEM)
X_PLANES = 74
Y_ROWS = 672


def gll_derivative():
    points = np.array([-1.0, -1.0 / np.sqrt(5.0), 1.0 / np.sqrt(5.0), 1.0])
    products = np.array(
        [np.prod([points[r] - points[s] for s in range(4) if s != r]) for r in range(4)]
    )
    table = np.zeros((4, 4))
    for r in range(4):
        for s in range(4):
            if r != s:
                table[r, s] = products[r] / (products[s] * (points[r] - points[s]))
    table[0, 0], table[3, 3] = -3.0, 3.0
    return 2.0 * table


DERIV = gll_derivative()
ROW_SCALE = np.array([1.375, 1.125, 1.125, 1.375])


SCALED = (DERIV * ROW_SCALE[:, None]).astype(ml_dtypes.bfloat16).astype(np.float64)


def y_nodes():
    lane = np.arange(32)
    return np.where(lane < 16, 143 - lane, 15 - lane)


def lane_operators(nodes):
    count = len(nodes)
    deriv, average = np.zeros((count, count)), np.eye(count)
    where = {int(y): p for p, y in enumerate(nodes)}
    for y, p in where.items():
        for j in range(4):
            deriv[p, where[y - y % 4 + j]] = SCALED[y % 4, j]
        other = y - 1 if y % 4 == 0 else y + 1
        if y % 4 in (0, 3) and other in where:
            average[p, p] = average[p, where[other]] = 0.5
    return deriv, average


def twice(*matrices):
    both = np.concatenate([m.T for m in matrices], axis=1)
    return np.concatenate([both, both], axis=0)


def lane_matrices():
    eye = np.eye(128)
    deriv, average = lane_operators(np.arange(128))
    main = np.stack([twice(deriv, eye), twice(deriv @ average, average)])
    halo_deriv, halo_average = lane_operators(y_nodes())
    dy, av = np.kron(np.eye(4), halo_deriv), np.kron(np.eye(4), halo_average)
    dx = np.kron(SCALED, np.eye(32))
    halo = np.stack([twice(dx, dy, eye), twice(dx @ av, dy @ av, av)])
    return np.concatenate([main, halo], axis=2).astype(ml_dtypes.bfloat16)


def lane_vectors():
    vec = np.zeros((16, 128), np.float32)
    lane = np.arange(128)
    halo = np.tile(y_nodes(), 4)
    vec[0] = 1.0 / ROW_SCALE[lane % 4]
    vec[1] = 1.0 / ROW_SCALE[halo % 4]
    vec[2] = 1.0 / ROW_SCALE[lane // 32]
    for c in range(N_COMP):
        for row, y in ((4 + c, lane), (8 + c, halo)):
            vec[row] = DT * 0.5 * np.sin(2.0 * np.pi * (c * 128 + y + 0.5) / (128 * N_COMP))
    return vec


def split_bf16(x):
    hi = x.astype(BF16)
    return hi, (x - hi.astype(F32)).astype(BF16)


def iota(shape, dim):
    return lax.broadcasted_iota(I32, shape, dim)


def mm(a, b):
    return jnp.dot(a, b, preferred_element_type=F32)


def mm_t(a, b):
    return lax.dot_general(a, b, (((0,), (0,)), ((), ())), preferred_element_type=F32)


def slots_kernel(src_ref, rhs_ref, vec_ref, wanted_ref, tcol_ref, rhs_out_ref, vec_out_ref):
    rhs_out_ref[...] = rhs_ref[...]
    vec_out_ref[...] = vec_ref[...]
    s = src_ref[...] >> 2
    tile = (s >> 5).astype(F32)
    row = (s & 31).astype(F32)
    r0, a0 = iota((64, 8), 0), iota((64, 8), 1)
    pick_row = ((r0 >> 3) == a0).astype(F32)
    own = (r0 & 7) == a0
    tile_c = jnp.sum(jnp.where(own, mm(pick_row, tile), 0.0), axis=1, keepdims=True)
    b1, r1 = iota((8, 64), 0), iota((8, 64), 1)
    pick_col = (b1 == (r1 & 7)).astype(F32)
    own_t = b1 == (r1 >> 3)
    tile_r = jnp.sum(jnp.where(own_t, mm(tile, pick_col), 0.0), axis=0, keepdims=True)
    row_r = jnp.sum(jnp.where(own_t, mm(row, pick_col), 0.0), axis=0, keepdims=True)
    same = jnp.where(tile_c == tile_r, 1.0, 0.0)
    sub, lane = iota((64, 64), 0), iota((64, 64), 1)
    rank_c = jnp.sum(jnp.where(lane < sub, same, 0.0), axis=1, keepdims=True)
    rank_r = jnp.sum(jnp.where(sub < lane, same, 0.0), axis=0, keepdims=True)
    slot_c = (tile_c * 4.0 + rank_c).astype(I32)
    slot_r = (tile_r * 4.0 + rank_r).astype(I32)
    slot_wide = jnp.broadcast_to(slot_c, (64, 128))
    field = iota((64, 8, 128), 1)
    tcol = jnp.where(field < 4, slot_wide[:, None, :] * 4 + field, -1)
    tcol_ref[...] = tcol.reshape(512, 128)
    q = iota((512, 64), 0)
    val = jnp.sum(jnp.where((q >> 2) == slot_r, row_r + 1.0, 0.0), axis=1, keepdims=True) - 1.0
    f = (iota((512, 1), 0) & 3).astype(F32)
    target = jnp.where(val >= 0.0, f * 32.0 + val, -1.0)
    wanted_ref[...] = jnp.broadcast_to(target, (512, 128)).astype(BF16)


def one_hot(rows, target):
    return jnp.where(iota((rows, 256), 0) == target, 1.0, 0.0).astype(BF16)


def pack_matrix():
    col = iota((1, 256), 1)
    lane = col & 127
    plane = ((lane >> 4) & 1) * 4 + (lane >> 5)
    return one_hot(1024, plane * 128 + (lane & 15) + jnp.where(col < 128, 0, 112))


def unpack_matrix():
    col = iota((1, 256), 1)
    quarter, n = (col & 127) >> 5, col & 31
    base = 32 * quarter + 16 * (col >> 7)
    return one_hot(256, base + jnp.where(n < 16, 15 - n, 159 - n))


def edge_rows(ocean, off, w, flags):
    ends = (0, 128, 768, 896)
    rows = [ocean[:, c : c + 128] for c in ends]
    for array in (off, w):
        rows += [array[:, 0:128].astype(F32), array[:, 896:1024].astype(F32)]
    return jnp.concatenate(rows + [flags.astype(F32)], axis=0)


def x_pack_kernel(par_ref, atm_ref, small_ref, a_ref, b_ref, flags_out_ref):
    even = par_ref[0] == 0

    def put(index, right, left):
        a_ref[index] = jnp.where(even, right, left).astype(BF16)
        b_ref[index] = jnp.where(even, left, right).astype(BF16)

    put(slice(0, 64), atm_ref[:, 16:32, :], atm_ref[:, 0:16, :])
    flags = small_ref[280:312]
    flags_out_ref[...] = flags
    put(64, flags[16:32], flags[0:16])
    for part in range(2):
        left = small_ref[64 * part : 64 * part + 64].reshape(4, 16, 128)
        right = small_ref[128 + 64 * part : 192 + 64 * part].reshape(4, 16, 128)
        put(slice(65 + 4 * part, 69 + 4 * part), right, left)
    pad = jnp.zeros((2, 128), F32)
    left = jnp.concatenate([small_ref[256:262], pad, small_ref[268:274], pad], axis=0)
    right = jnp.concatenate([small_ref[262:268], pad, small_ref[274:280], pad], axis=0)
    put(73, right, left)


def x_extended(ts_ref, slot, main, xa_ref, xb_ref, p, even):
    a, b = xa_ref[p].astype(F32), xb_ref[p].astype(F32)
    ts_ref[slot, 0:32] = main
    ts_ref[slot, 32:48] = jnp.where(even, a, b)
    ts_ref[slot, 48:64] = jnp.where(even, b, a)
    return [ts_ref[slot, pl.ds(i, 16, stride=4), :] for i in range(4)]


def y_pack_kernel(
    par_ref,
    atm_ref,
    flags_ref,
    xa_ref,
    xb_ref,
    pa_ref,
    pb_ref,
    a_ref,
    b_ref,
    cb_ref,
    flag_ref,
    lhs_ref,
    ts_ref,
):
    even_t, even_c = par_ref[0] == 0, par_ref[1] == 0
    comp = par_ref[2]

    def group(q, _):
        for s in range(8):
            p = q * 8 + s
            rows = x_extended(ts_ref, s, atm_ref[p], xa_ref, xb_ref, p, even_t)
            for i in range(4):
                lanes = slice(((s % 2) * 4 + i) * 128, ((s % 2) * 4 + i) * 128 + 128)
                hi, lo = split_bf16(rows[i])
                lhs_ref[q * 4 + s // 2, :, lanes] = hi
                cb_ref[(q % 2) * 8 + s, q // 2, i, :, 0:128] = hi
                cb_ref[(q % 2) * 8 + s, q // 2, i, :, 128:256] = lo
        return 0

    lax.fori_loop(0, 8, group, 0)
    rows = x_extended(ts_ref, 0, flags_ref[...], xa_ref, xb_ref, 64, even_t)
    for i in range(4):
        lhs_ref[32, :, 128 * i : 128 * i + 128] = rows[i].astype(BF16)
        flag_ref[i] = rows[i]
    lhs_ref[32, :, 512:1024] = jnp.zeros((16, 512), BF16)
    moved = mm(lhs_ref[...].reshape(528, 1024), pack_matrix())
    left, right = moved[:, 0:128], moved[:, 128:256]
    a_ref[0:528] = jnp.where(even_c, right, left).astype(BF16)
    b_ref[0:528] = jnp.where(even_c, left, right).astype(BF16)
    for n in range(9):
        p = 65 + n
        dest = slice(528 + 16 * n, 544 + 16 * n)
        a, b = xa_ref[p].astype(F32), xb_ref[p].astype(F32)
        own_a, own_b = pa_ref[p].astype(F32), pb_ref[p].astype(F32)
        from_left, from_right = jnp.where(even_t, b, a), jnp.where(even_t, a, b)
        own_right, own_left = jnp.where(even_t, own_a, own_b), jnp.where(even_t, own_b, own_a)
        right = jnp.where(comp == N_COMP - 1, from_left, own_right)
        left = jnp.where(comp == 0, from_right, own_left)
        a_ref[dest] = jnp.where(even_c, right, left).astype(BF16)
        b_ref[dest] = jnp.where(even_c, left, right).astype(BF16)


def x_slopes(a):
    sums, diffs = (a[0] + a[3], a[1] + a[2]), (a[0] - a[3], a[1] - a[2])
    across = sums[0] - sums[1]
    out = [None] * 4
    for i in range(2):
        d = DERIV[i]
        odd = float((d[0] - d[3]) / 2) * diffs[0] + float((d[1] - d[2]) / 2) * diffs[1]
        even = float((d[0] + d[3]) / 2) * across
        out[i], out[3 - i] = odd + even, odd - even
    return out


def atm_kernel(
    par_ref,
    scal_ref,
    first_ref,
    flag_ref,
    ya_ref,
    yb_ref,
    vec_ref,
    rhs_ref,
    out_ref,
    table_ref,
    cb_ref,
    abuf_ref,
    dbuf_ref,
    hcb_ref,
    hbuf_ref,
    tm_ref,
    mask_ref,
    r5_ref,
    facc_ref,
    gs_ref,
    first_sem,
):
    first_copy = pltpu.make_async_copy(first_ref, cb_ref, first_sem)
    first_copy.start()
    even_c = par_ref[1] == 0
    comp = par_ref[2]
    lane = iota((16, 128), 1)
    edge = (lane == 0) | (lane == 127)
    quarter = lane >> 5
    halo_edge = ((lane & 31) == 15) | ((lane & 31) == 16)

    def put(ref, index, value):
        hi, lo = split_bf16(value)
        ref[(*index, slice(None), slice(0, 128))] = hi
        ref[(*index, slice(None), slice(128, 256))] = lo

    ya, yb = ya_ref[0:528].astype(F32), yb_ref[0:528].astype(F32)
    from_right, from_left = jnp.where(even_c, ya, yb), jnp.where(even_c, yb, ya)
    arrived = jnp.concatenate([from_right, from_left], axis=1).astype(BF16)
    halo = mm(arrived, unpack_matrix()).astype(BF16)
    for k in range(4):
        for l in range(LEVELS):
            rows = slice((k * 8 + l // 2) * 16, (k * 8 + l // 2) * 16 + 16)
            lanes = slice((l % 2) * 128, (l % 2) * 128 + 128)
            hcb_ref[l, k, :, 0:128] = halo[rows, lanes]
            hcb_ref[l, k, :, 128:256] = jnp.zeros((16, 128), BF16)
    halo_flag = halo[512:528, 0:128].astype(F32)
    halo_r5 = jnp.where(halo_flag == 1.0, 5.0 * DT, 0.0)
    halo_m5 = jnp.where(halo_flag == 2.0, 5.0 * DT, 0.0)
    halo_keep = 1.0 - 2.0 * halo_m5
    halo_keep_t = halo_keep - halo_r5
    for i in range(4):
        flag = flag_ref[i]
        m5 = jnp.where(flag == 2.0, 5.0 * DT, 0.0)
        r5_ref[i] = jnp.where(flag == 1.0, 5.0 * DT, 0.0)
        mask_ref[0, i] = m5
        mask_ref[1, i] = 1.0 - 2.0 * m5
        mask_ref[2, i] = 1.0 - 2.0 * m5 - r5_ref[i]
    facc_ref[...] = jnp.zeros_like(facc_ref)
    dt_y = -DT * vec_ref[0:1, :]
    halo_dt_y = -DT * vec_ref[1:2, :]
    halo_dt_x = -DT * vec_ref[2:3, :]
    ff = vec_ref[pl.ds(4 + comp, 1), :]
    halo_ff = vec_ref[pl.ds(8 + comp, 1), :]
    first_copy.wait()

    def step(si, _):
        which = jnp.minimum(si, 1)
        both = mm(cb_ref[...].reshape(4096, 256), rhs_ref[which, :, 0:256])
        dbuf_ref[...] = both[:, 0:128].reshape(LEVELS, 4, 4, 16, 128)
        abuf_ref[...] = both[:, 128:256].reshape(LEVELS, 4, 4, 16, 128)
        hbuf_ref[...] = mm(hcb_ref[...].reshape(1024, 256), rhs_ref[which, :, 256:640]).reshape(
            LEVELS, 4, 16, 384
        )
        for i in range(4):
            total = abuf_ref[0, 2, i]
            for l in range(1, LEVELS):
                total = total + abuf_ref[l, 2, i]
            mask_ref[3, i] = r5_ref[i] * (total * (1.0 / LEVELS))
        total = hbuf_ref[0, 2, :, 256:384]
        for l in range(1, LEVELS):
            total = total + hbuf_ref[l, 2, :, 256:384]
        tm_ref[...] = halo_r5 * (total * (1.0 / LEVELS))

        def level(l, _):
            above, below = jnp.minimum(l + 1, LEVELS - 1), jnp.maximum(l - 1, 0)
            wind_x, wind_y = scal_ref[l], scal_ref[LEVELS + l]
            cx = -DT * wind_x
            cy = dt_y * wind_y
            a = [[abuf_ref[l, k, i] for i in range(4)] for k in range(4)]

            slopes = [x_slopes(a[k]) for k in range(4)]
            new = [[None] * 4 for _ in range(4)]
            for i in range(4):
                m5, keep, keep_t, relax = [mask_ref[n, i] for n in range(4)]
                d = [slopes[k][i] for k in range(4)]
                dy = [dbuf_ref[l, k, i] for k in range(4)]
                extra = [
                    ff * a[1][i] - DT * d[3],
                    dt_y * dy[3] - ff * a[0][i],
                    relax,
                    dt_y * dy[1] - DT * d[0],
                ]
                for k in range(4):
                    mix = m5 * (abuf_ref[above, k, i] + abuf_ref[below, k, i])
                    own = (keep_t if k == 2 else keep) * a[k][i]
                    new[k][i] = (own + mix) + ((cx * d[k] + cy * dy[k]) + extra[k])

            halo_cx, halo_cy = halo_dt_x * wind_x, halo_dt_y * wind_y
            hx, hy, ha = [
                [hbuf_ref[l, k, :, 128 * n : 128 * n + 128] for k in range(4)] for n in range(3)
            ]
            extra = [
                halo_ff * ha[1] + halo_dt_x * hx[3],
                halo_dt_y * hy[3] - halo_ff * ha[0],
                tm_ref[...],
                halo_dt_y * hy[1] + halo_dt_x * hx[0],
            ]
            for k in range(4):
                first = 0.5 * (new[k][0] + pltpu.roll(new[k][3], 1, 0))
                values = [first, new[k][1], new[k][2], pltpu.roll(first, 15, 0)]
                up, down = hbuf_ref[above, k, :, 256:384], hbuf_ref[below, k, :, 256:384]
                own = (halo_keep_t if k == 2 else halo_keep) * ha[k] + halo_m5 * (up + down)
                own = own + ((halo_cx * hx[k] + halo_cy * hy[k]) + extra[k])
                lower = pltpu.roll(pltpu.roll(own, 32, 1), 1, 0)
                upper = pltpu.roll(pltpu.roll(own, 96, 1), 15, 0)
                partner = jnp.where(quarter == 0, lower, jnp.where(quarter == 3, upper, own))
                own = 0.5 * (own + partner)
                across = None
                for i in range(4):
                    moved = pltpu.roll(values[i], 32 * i + 16, 1)
                    across = moved if i == 0 else jnp.where(quarter == i, moved, across)
                    back = pltpu.roll(own, 112 - 32 * i, 1)
                    put(cb_ref, (l, k, i), jnp.where(edge, 0.5 * (values[i] + back), values[i]))
                put(hcb_ref, (l, k), jnp.where(halo_edge, 0.5 * (own + across), own))
            return 0

        lax.fori_loop(0, LEVELS, level, 0, unroll=2)
        surface = mm(cb_ref[0].reshape(256, 256), rhs_ref[1, :, 128:256]).reshape(4, 4, 16, 128)
        for i in range(4):
            u, v, t, z = [surface[k, i, 0:8] for k in range(4)]
            speed = jnp.sqrt(u * u + v * v + 1.0)
            for c in range(NFLUX):
                m0, m1, m2, m3 = [scal_ref[32 + 4 * c + k] for k in range(4)]
                m = (m0 * u + m1 * v) + (m2 * t + m3 * z)
                facc_ref[c, i] += speed * m * lax.rsqrt(1.0 + 0.5 * (m * m))
        return 0

    lax.fori_loop(0, STEPS, step, 0)
    final = mm(cb_ref[...].reshape(4096, 256), rhs_ref[1, :, 128:256]).reshape(LEVELS, 4, 4, 16, 128)
    for l in range(LEVELS):
        for k in range(4):
            for i in range(4):
                out_ref[k * LEVELS + l, pl.ds(i, 8, stride=4), :] = final[l, k, i, 0:8]
    for i in range(4):
        mean = [(facc_ref[c, i] * (1.0 / STEPS)).astype(BF16).astype(F32) for c in range(NFLUX)]
        for g in range(4):
            total = scal_ref[80 + 12 * g] * mean[0]
            for c in range(1, NFLUX):
                total = total + scal_ref[80 + 12 * g + c] * mean[c]
            gs_ref[g, pl.ds(i, 8, stride=4), :] = 0.25 * total
    table_ref[...] = gs_ref[...].reshape(128, 128).astype(BF16)


def pick_kernel(served_ref, table_ref, rows_ref):
    pick = served_ref[...].astype(F32) == iota((512, 128), 1).astype(F32)
    rows_ref[...] = mm(jnp.where(pick, 1.0, 0.0).astype(BF16), table_ref[...]).astype(BF16)


def ocean_kernel(par_ref, ocean_ref, off_ref, w_ref, ya_ref, yb_ref, n2_ref, wm_ref, sw_ref, o1_ref):
    even_c = par_ref[1] == 0

    def halo_rows(n):
        rows = slice(528 + 16 * n, 544 + 16 * n)
        a, b = ya_ref[rows].astype(F32), yb_ref[rows].astype(F32)
        return jnp.where(even_c, b, a), jnp.where(even_c, a, b)

    pieces = [halo_rows(n) for n in range(9)]
    left = [jnp.concatenate([p[0] for p in pieces[4 * n : 4 * n + 4]], axis=0) for n in range(2)]
    right = [jnp.concatenate([p[1] for p in pieces[4 * n : 4 * n + 4]], axis=0) for n in range(2)]
    values = {-2: left[0], -1: left[1], 8: right[0], 9: right[1]}
    for b in range(8):
        values[b] = ocean_ref[:, 128 * b : 128 * b + 128]
    offw = {-1: pieces[8][0], 8: pieces[8][1]}
    source = iota((384, 128), 0)
    lane = iota((1, 128), 1)
    level = iota((64, 128), 0) & 15

    def matrix(b):
        if b in offw:
            off, w = offw[b][0:6].astype(I32), offw[b][8:14]
        else:
            cells = slice(128 * b, 128 * b + 128)
            off, w = off_ref[:, cells], w_ref[:, cells].astype(BF16).astype(F32)
        total = jnp.zeros((384, 128), F32)
        for j in range(6):
            total = total + jnp.where(source == lane + off[j : j + 1], w[j : j + 1], 0.0)
        return total.astype(BF16), jnp.sum(w, axis=0, keepdims=True)

    def update(own, window, wm, sw):
        hi, lo = split_bf16(window)
        both = mm(jnp.concatenate([hi, lo], axis=0), wm)
        lateral = both[0:64] + both[64:128] - sw * own
        above = jnp.where(level == 15, own, pltpu.roll(own, 63, 0))
        below = jnp.where(level == 0, own, pltpu.roll(own, 1, 0))
        rot = jnp.concatenate([jnp.zeros((32, 128), F32), 0.2 * own[48:64], -0.2 * own[32:48]], axis=0)
        return own + lateral + 0.2 * (above - 2.0 * own + below) + rot

    for b in range(-1, 9):
        wm, sw = matrix(b)
        if 0 <= b < 8:
            wm_ref[b] = wm
            sw_ref[:, 128 * b : 128 * b + 128] = jnp.broadcast_to(sw, (8, 128))
        window = jnp.concatenate([values[b - 1], values[b], values[b + 1]], axis=1)
        o1_ref[b + 1] = update(values[b], window, wm, sw)
    for b in range(8):
        window = jnp.concatenate([o1_ref[b], o1_ref[b + 1], o1_ref[b + 2]], axis=1)
        cells = slice(128 * b, 128 * b + 128)
        n2_ref[:, cells] = update(o1_ref[b + 1], window, wm_ref[b], sw_ref[0:1, cells])


def request_matrix(tcol_ref):
    parts = []
    for chunk in range(4):
        hit = tcol_ref[...] == iota((512, 128), 1) + 128 * chunk
        parts.append(jnp.where(hit, 1.0, 0.0).astype(BF16))
    return jnp.concatenate(parts, axis=1)


def forcing_kernel(par_ref, rows_ref, tcol_ref, weights_ref, f_ref, a_ref, b_ref):
    even_c = par_ref[1] == 0
    gathered = mm(request_matrix(tcol_ref), rows_ref[...])
    for b in range(8):
        lhs = jnp.concatenate(
            [gathered[(b * 8 + k) * 8 : (b * 8 + k) * 8 + 8] for k in range(8)], axis=1
        ).astype(BF16)
        f_ref[:, 128 * b : 128 * b + 128] = mm(lhs, weights_ref[b])
    right, left = f_ref[:, 896:1024], f_ref[:, 0:128]
    a_ref[...] = jnp.where(even_c, right, left)
    b_ref[...] = jnp.where(even_c, left, right)


def return_kernel(
    par_ref,
    n2_ref,
    wm_ref,
    sw_ref,
    f_ref,
    ea_ref,
    eb_ref,
    tcol_ref,
    weights_ref,
    ocean_ref,
    sent_ref,
    parts_ref,
):
    even_c = par_ref[1] == 0
    ea, eb = ea_ref[...], eb_ref[...]
    blocks = [jnp.where(even_c, eb, ea)]
    blocks += [f_ref[:, 128 * b : 128 * b + 128] for b in range(8)]
    blocks += [jnp.where(even_c, ea, eb)]
    ocean_ref[...] = n2_ref[...]
    for b in range(8):
        cells = slice(128 * b, 128 * b + 128)
        window = jnp.concatenate(blocks[b : b + 3], axis=1)
        hi, lo = split_bf16(window)
        own = blocks[b + 1]
        both = mm(jnp.concatenate([hi.astype(F32), lo.astype(F32)], axis=0).astype(BF16), wm_ref[b])
        top = both[0:8] + both[8:16] + (1.8 - sw_ref[:, cells]) * own
        surface = []
        for k in range(4):
            value = n2_ref[16 * k : 16 * k + 1, cells] + top[k : k + 1]
            if k == 2:
                value = value + 0.2 * own[3:4]
            if k == 3:
                value = value - 0.2 * own[2:3]
            ocean_ref[16 * k : 16 * k + 1, cells] = value
            below = n2_ref[16 * k + 1 : 16 * k + 2, cells] + 0.2 * own[k : k + 1]
            ocean_ref[16 * k + 1 : 16 * k + 2, cells] = below
            surface.append(value)
        lhs = jnp.concatenate(surface + [jnp.zeros((4, 128), F32)], axis=0).astype(BF16)
        wide = jnp.concatenate([weights_ref[b, k] for k in range(8)], axis=1)
        parts = mm(lhs, wide)
        for k in range(8):
            rows = slice((b * 8 + k) * 8, (b * 8 + k) * 8 + 8)
            parts_ref[rows, :] = parts[:, 128 * k : 128 * k + 128]
    sent_ref[...] = mm_t(request_matrix(tcol_ref), parts_ref[...].astype(BF16)).astype(BF16)


def collect_kernel(served_ref, incoming_ref, out_ref):
    pick = served_ref[...].astype(F32) == iota((512, 128), 1).astype(F32)
    owner = jnp.where(pick, 1.0, 0.0).astype(BF16)
    out_ref[...] = mm_t(owner, incoming_ref[...]).reshape(4, 32, 128)


def swap_pairs(n):
    near = [(i, i ^ 1) for i in range(n)]
    far = [(i, (i + 1) % n if i % 2 else (i - 1) % n) for i in range(n)]
    return near, far


def exchange(payloads, axis, n):
    near, far = swap_pairs(n)
    return lax.ppermute(payloads[0], axis, near), lax.ppermute(payloads[1], axis, far)


def to_tiles(rows):
    moved = lax.all_to_all(
        rows.reshape(N_TILE, 16, 128), "tile", split_axis=0, concat_axis=0, tiled=True
    )
    return moved.reshape(512, 128)


def call(kernel, out, specs, scratch=(), mib=16, cost=None):
    return pl.pallas_call(
        kernel,
        out_shape=out,
        in_specs=specs,
        out_specs=jax.tree.map(lambda _: VMEM, out),
        scratch_shapes=list(scratch),
        compiler_params=pltpu.CompilerParams(vmem_limit_bytes=mib * 2**20),
        cost_estimate=cost,
    )


ATM_SCRATCH = (
    pltpu.VMEM((LEVELS, 4, 4, 16, 256), BF16),
    pltpu.VMEM((LEVELS, 4, 4, 16, 128), F32),
    pltpu.VMEM((LEVELS, 4, 4, 16, 128), F32),
    pltpu.VMEM((LEVELS, 4, 16, 256), BF16),
    pltpu.VMEM((LEVELS, 4, 16, 384), F32),
    pltpu.VMEM((16, 128), F32),
    pltpu.VMEM((4, 4, 16, 128), F32),
    pltpu.VMEM((4, 16, 128), F32),
    pltpu.VMEM((NFLUX, 4, 8, 128), F32),
    pltpu.VMEM((4, 32, 128), F32),
    pltpu.SemaphoreType.DMA,
)


def per_device(
    atm_state,
    level_winds,
    physics_flags,
    flux_matrix,
    regrid_source,
    regrid_weights,
    return_weights,
    ocean_state,
    ocean_neighbors,
    edge_weights,
    ocean_coupling,
):
    S = jax.ShapeDtypeStruct
    t, c = lax.axis_index("tile"), lax.axis_index("comp")
    par = jnp.stack([t % 2, c % 2, c, t]).astype(I32)
    atm = atm_state.reshape(64, 32, 128)
    ocean = ocean_state.reshape(64, 1024)
    scal = jnp.concatenate(
        [level_winds.reshape(-1), flux_matrix.reshape(-1), ocean_coupling.reshape(-1)]
    )
    rhs = jnp.asarray(lane_matrices())
    vec = jnp.asarray(lane_vectors())

    small = edge_rows(ocean, ocean_neighbors, edge_weights, physics_flags)
    xp_a, xp_b, flags = call(
        x_pack_kernel,
        (S((X_PLANES, 16, 128), BF16),) * 2 + (S((32, 128), F32),),
        [SMEM] + [VMEM] * 2,
    )(par, atm, small)
    xa, xb = exchange((xp_a, xp_b), "tile", N_TILE)
    wanted, tcol, rhs, vec = call(
        slots_kernel,
        (S((512, 128), BF16), S((512, 128), I32), S(rhs.shape, BF16), S(vec.shape, F32)),
        [VMEM] * 3,
    )(regrid_source, rhs, vec)
    wanted, tcol, rhs, vec, xb = lax.optimization_barrier((wanted, tcol, rhs, vec, xb))
    served = to_tiles(wanted)
    *y_payload, first, flag = call(
        y_pack_kernel,
        (S((Y_ROWS, 128), BF16),) * 2
        + (S((LEVELS, 4, 4, 16, 256), BF16), S((4, 16, 128), F32)),
        [SMEM] + [VMEM] * 6,
        [pltpu.VMEM((33, 16, 1024), BF16), pltpu.VMEM((8, 64, 128), F32)],
    )(par, atm, flags, xa, xb, xp_a, xp_b)
    ya, yb = exchange(y_payload, "comp", N_COMP)
    atm_final, table = call(
        atm_kernel,
        (S((64, 32, 128), F32), S((128, 128), BF16)),
        [SMEM] * 2 + [VMEM] * 6,
        ATM_SCRATCH,
        mib=32,
        cost=pl.CostEstimate(flops=2**33, bytes_accessed=2**26, transcendentals=0),
    )(par, scal, first, flag, ya, yb, vec, rhs)
    rows = call(pick_kernel, S((512, 128), BF16), [VMEM] * 2)(served, table)
    mean_rows = to_tiles(rows)
    n2, wm, sw = call(
        ocean_kernel,
        (S((64, 1024), F32), S((8, 384, 128), BF16), S((8, 1024), F32)),
        [SMEM] + [VMEM] * 5,
        [pltpu.VMEM((10, 64, 128), F32)],
        cost=pl.CostEstimate(flops=2**27, bytes_accessed=2**24, transcendentals=0),
    )(par, ocean, ocean_neighbors, edge_weights, ya, yb)
    forcing, *edges = call(
        forcing_kernel,
        (S((8, 1024), F32), S((8, 128), F32), S((8, 128), F32)),
        [SMEM] + [VMEM] * 3,
    )(par, mean_rows, tcol, regrid_weights.reshape(8, 1024, 128))
    ea, eb = exchange(edges, ("tile", "comp"), N_TILE * N_COMP)
    ocean_final, sent = call(
        return_kernel,
        (S((64, 1024), F32), S((512, 128), BF16)),
        [SMEM] + [VMEM] * 8,
        [pltpu.VMEM((512, 128), F32)],
    )(par, n2, wm, sw, forcing, ea, eb, tcol, return_weights)
    incoming = to_tiles(sent)
    ocean_on_atm = call(collect_kernel, S((4, 32, 128), F32), [VMEM] * 2)(served, incoming)
    return (
        atm_final.reshape(atm_state.shape),
        ocean_final.reshape(ocean_state.shape),
        ocean_on_atm,
    )


def solution(mesh):
    return jax.shard_map(
        per_device,
        mesh=mesh,
        in_specs=(
            P(None, None, "tile", "comp"),
            P(),
            P("tile", "comp"),
            P(),
            P(("tile", "comp"), None),
            P(("tile", "comp"), None, None, None),
            P(("tile", "comp"), None, None, None),
            P(None, None, ("tile", "comp")),
            P(None, ("tile", "comp")),
            P(None, ("tile", "comp")),
            P(),
        ),
        out_specs=(
            P(None, None, "tile", "comp"),
            P(None, None, ("tile", "comp")),
            P(None, "tile", "comp"),
        ),
        check_vma=False,
    )
```

```python
import functools

import jax
import jax.numpy as jnp
import ml_dtypes
import numpy as np
from jax import lax
from jax.experimental import pallas as pl
from jax.experimental.pallas import tpu as pltpu
from jax.sharding import PartitionSpec as P

F32 = jnp.float32
BF16 = jnp.bfloat16
I32 = jnp.int32
N_TILE, N_COMP = 32, 4
STEPS = 4
LEVELS = 16
NFLUX = 12
DT = 0.02
VMEM = pl.BlockSpec(memory_space=pltpu.VMEM)
HBM = pl.BlockSpec(memory_space=pltpu.HBM)
SMEM = pl.BlockSpec(memory_space=pltpu.SMEM)
X_PLANES = 74
Y_ROWS = 672


def gll_derivative():
    points = np.array([-1.0, -1.0 / np.sqrt(5.0), 1.0 / np.sqrt(5.0), 1.0])
    products = np.array(
        [np.prod([points[r] - points[s] for s in range(4) if s != r]) for r in range(4)]
    )
    table = np.zeros((4, 4))
    for r in range(4):
        for s in range(4):
            if r != s:
                table[r, s] = products[r] / (products[s] * (points[r] - points[s]))
    table[0, 0], table[3, 3] = -3.0, 3.0
    return 2.0 * table


DERIV = gll_derivative()
ROW_SCALE = np.array([1.375, 1.125, 1.125, 1.375])


SCALED = (DERIV * ROW_SCALE[:, None]).astype(ml_dtypes.bfloat16).astype(np.float64)


def y_nodes():
    lane = np.arange(32)
    return np.where(lane < 16, 143 - lane, 15 - lane)


def lane_operators(nodes):
    count = len(nodes)
    deriv, average = np.zeros((count, count)), np.eye(count)
    where = {int(y): p for p, y in enumerate(nodes)}
    for y, p in where.items():
        for j in range(4):
            deriv[p, where[y - y % 4 + j]] = SCALED[y % 4, j]
        other = y - 1 if y % 4 == 0 else y + 1
        if y % 4 in (0, 3) and other in where:
            average[p, p] = average[p, where[other]] = 0.5
    return deriv, average


def twice(*matrices):
    both = np.concatenate([m.T for m in matrices], axis=1)
    return np.concatenate([both, both], axis=0)


def lane_matrices():
    eye = np.eye(128)
    deriv, average = lane_operators(np.arange(128))
    main = np.stack([twice(deriv, eye), twice(deriv @ average, average)])
    halo_deriv, halo_average = lane_operators(y_nodes())
    dy, av = np.kron(np.eye(4), halo_deriv), np.kron(np.eye(4), halo_average)
    dx = np.kron(SCALED, np.eye(32))
    halo = np.stack([twice(dx, dy, eye), twice(dx @ av, dy @ av, av)])
    return np.concatenate([main, halo], axis=2).astype(ml_dtypes.bfloat16)


def lane_vectors():
    vec = np.zeros((16, 128), np.float32)
    lane = np.arange(128)
    halo = np.tile(y_nodes(), 4)
    vec[0] = 1.0 / ROW_SCALE[lane % 4]
    vec[1] = 1.0 / ROW_SCALE[halo % 4]
    vec[2] = 1.0 / ROW_SCALE[lane // 32]
    for c in range(N_COMP):
        for row, y in ((4 + c, lane), (8 + c, halo)):
            vec[row] = DT * 0.5 * np.sin(2.0 * np.pi * (c * 128 + y + 0.5) / (128 * N_COMP))
    return vec


def split_bf16(x):
    hi = x.astype(BF16)
    return hi, (x - hi.astype(F32)).astype(BF16)


def iota(shape, dim):
    return lax.broadcasted_iota(I32, shape, dim)


def mm(a, b):
    return jnp.dot(a, b, preferred_element_type=F32)


def mm_t(a, b):
    return lax.dot_general(a, b, (((0,), (0,)), ((), ())), preferred_element_type=F32)


def slots_kernel(src_ref, wanted_ref, tcol_ref):
    s = src_ref[...] >> 2
    tile = (s >> 5).astype(F32)
    row = (s & 31).astype(F32)
    r0, a0 = iota((64, 8), 0), iota((64, 8), 1)
    pick_row = ((r0 >> 3) == a0).astype(F32)
    own = (r0 & 7) == a0
    tile_c = jnp.sum(jnp.where(own, mm(pick_row, tile), 0.0), axis=1, keepdims=True)
    b1, r1 = iota((8, 64), 0), iota((8, 64), 1)
    pick_col = (b1 == (r1 & 7)).astype(F32)
    own_t = b1 == (r1 >> 3)
    tile_r = jnp.sum(jnp.where(own_t, mm(tile, pick_col), 0.0), axis=0, keepdims=True)
    row_r = jnp.sum(jnp.where(own_t, mm(row, pick_col), 0.0), axis=0, keepdims=True)
    same = jnp.where(tile_c == tile_r, 1.0, 0.0)
    sub, lane = iota((64, 64), 0), iota((64, 64), 1)
    rank_c = jnp.sum(jnp.where(lane < sub, same, 0.0), axis=1, keepdims=True)
    rank_r = jnp.sum(jnp.where(sub < lane, same, 0.0), axis=0, keepdims=True)
    slot_c = (tile_c * 4.0 + rank_c).astype(I32)
    slot_r = (tile_r * 4.0 + rank_r).astype(I32)
    slot_wide = jnp.broadcast_to(slot_c, (64, 128))
    field = iota((64, 8, 128), 1)
    tcol = jnp.where(field < 4, slot_wide[:, None, :] * 4 + field, -1)
    tcol_ref[...] = tcol.reshape(512, 128)
    q = iota((512, 64), 0)
    val = jnp.sum(jnp.where((q >> 2) == slot_r, row_r + 1.0, 0.0), axis=1, keepdims=True) - 1.0
    f = (iota((512, 1), 0) & 3).astype(F32)
    target = jnp.where(val >= 0.0, f * 32.0 + val, -1.0)
    wanted_ref[...] = jnp.broadcast_to(target, (512, 128)).astype(BF16)


def one_hot(rows, target):
    return jnp.where(iota((rows, 256), 0) == target, 1.0, 0.0).astype(BF16)


def pack_matrix():
    col = iota((1, 256), 1)
    lane = col & 127
    plane = ((lane >> 4) & 1) * 4 + (lane >> 5)
    return one_hot(1024, plane * 128 + (lane & 15) + jnp.where(col < 128, 0, 112))


def unpack_matrix():
    col = iota((1, 256), 1)
    quarter, n = (col & 127) >> 5, col & 31
    base = 32 * quarter + 16 * (col >> 7)
    return one_hot(256, base + jnp.where(n < 16, 15 - n, 159 - n))


def x_pack_kernel(
    par_ref, atm_ref, flags_ref, ocean_ref, off_ref, w_ref, a_ref, b_ref, flags_out_ref
):
    even = par_ref[0] == 0

    def put(index, right, left):
        a_ref[index] = jnp.where(even, right, left).astype(BF16)
        b_ref[index] = jnp.where(even, left, right).astype(BF16)

    put(slice(0, 64), atm_ref[:, 16:32, :], atm_ref[:, 0:16, :])
    flags = flags_ref[...].astype(F32)
    flags_out_ref[...] = flags
    put(64, flags[16:32], flags[0:16])
    for part in range(2):
        right, left = [
            ocean_ref[:, c + 128 * part : c + 128 * part + 128].reshape(4, 16, 128) for c in (768, 0)
        ]
        put(slice(65 + 4 * part, 69 + 4 * part), right, left)
    off = off_ref[...].astype(F32)
    pad = jnp.zeros((2, 128), F32)
    right, left = [
        jnp.concatenate([off[:, c : c + 128], pad, w_ref[:, c : c + 128], pad], axis=0)
        for c in (896, 0)
    ]
    put(73, right, left)


def x_extended(ts_ref, slot, main, xa_ref, xb_ref, p, even):
    a, b = xa_ref[p].astype(F32), xb_ref[p].astype(F32)
    ts_ref[slot, 0:32] = main
    ts_ref[slot, 32:48] = jnp.where(even, a, b)
    ts_ref[slot, 48:64] = jnp.where(even, b, a)
    return [ts_ref[slot, pl.ds(i, 16, stride=4), :] for i in range(4)]


def y_pack_kernel(
    par_ref, atm_ref, flags_ref, xa_ref, xb_ref, pa_ref, pb_ref, a_ref, b_ref, lhs_ref, ts_ref
):
    even_t, even_c = par_ref[0] == 0, par_ref[1] == 0
    comp = par_ref[2]

    def group(q, _):
        for s in range(8):
            p = q * 8 + s
            rows = x_extended(ts_ref, s, atm_ref[p], xa_ref, xb_ref, p, even_t)
            for i in range(4):
                lanes = slice(((s % 2) * 4 + i) * 128, ((s % 2) * 4 + i) * 128 + 128)
                lhs_ref[q * 4 + s // 2, :, lanes] = rows[i].astype(BF16)
        return 0

    lax.fori_loop(0, 8, group, 0)
    rows = x_extended(ts_ref, 0, flags_ref[...], xa_ref, xb_ref, 64, even_t)
    for i in range(4):
        lhs_ref[32, :, 128 * i : 128 * i + 128] = rows[i].astype(BF16)
    lhs_ref[32, :, 512:1024] = jnp.zeros((16, 512), BF16)
    moved = mm(lhs_ref[...].reshape(528, 1024), pack_matrix())
    left, right = moved[:, 0:128], moved[:, 128:256]
    a_ref[0:528] = jnp.where(even_c, right, left).astype(BF16)
    b_ref[0:528] = jnp.where(even_c, left, right).astype(BF16)
    for n in range(9):
        p = 65 + n
        dest = slice(528 + 16 * n, 544 + 16 * n)
        a, b = xa_ref[p].astype(F32), xb_ref[p].astype(F32)
        own_a, own_b = pa_ref[p].astype(F32), pb_ref[p].astype(F32)
        from_left, from_right = jnp.where(even_t, b, a), jnp.where(even_t, a, b)
        own_right, own_left = jnp.where(even_t, own_a, own_b), jnp.where(even_t, own_b, own_a)
        right = jnp.where(comp == N_COMP - 1, from_left, own_right)
        left = jnp.where(comp == 0, from_right, own_left)
        a_ref[dest] = jnp.where(even_c, right, left).astype(BF16)
        b_ref[dest] = jnp.where(even_c, left, right).astype(BF16)


def x_slopes(a):
    sums, diffs = (a[0] + a[3], a[1] + a[2]), (a[0] - a[3], a[1] - a[2])
    across = sums[0] - sums[1]
    out = [None] * 4
    for i in range(2):
        d = DERIV[i]
        odd = float((d[0] - d[3]) / 2) * diffs[0] + float((d[1] - d[2]) / 2) * diffs[1]
        even = float((d[0] + d[3]) / 2) * across
        out[i], out[3 - i] = odd + even, odd - even
    return out


def atm_kernel(
    par_ref,
    scal_ref,
    atm_ref,
    flags_ref,
    xa_ref,
    xb_ref,
    ya_ref,
    yb_ref,
    vec_ref,
    rhs_ref,
    out_ref,
    table_ref,
    cb_ref,
    abuf_ref,
    dbuf_ref,
    hcb_ref,
    hbuf_ref,
    tm_ref,
    mask_ref,
    r5_ref,
    facc_ref,
    gs_ref,
    ts_ref,
    copies,
):
    even_t = par_ref[0] == 0
    even_c = par_ref[1] == 0
    comp = par_ref[2]
    lane = iota((16, 128), 1)
    edge = (lane == 0) | (lane == 127)
    quarter = lane >> 5
    halo_edge = ((lane & 31) == 15) | ((lane & 31) == 16)

    def put(ref, index, value):
        hi, lo = split_bf16(value)
        ref[(*index, slice(None), slice(0, 128))] = hi
        ref[(*index, slice(None), slice(128, 256))] = lo

    ya, yb = ya_ref[0:528].astype(F32), yb_ref[0:528].astype(F32)
    from_right, from_left = jnp.where(even_c, ya, yb), jnp.where(even_c, yb, ya)
    arrived = jnp.concatenate([from_right, from_left], axis=1).astype(BF16)
    halo = mm(arrived, unpack_matrix()).astype(BF16)
    for k in range(4):
        for l in range(LEVELS):
            rows = slice((k * 8 + l // 2) * 16, (k * 8 + l // 2) * 16 + 16)
            lanes = slice((l % 2) * 128, (l % 2) * 128 + 128)
            hcb_ref[l, k, :, 0:128] = halo[rows, lanes]
            hcb_ref[l, k, :, 128:256] = jnp.zeros((16, 128), BF16)
    halo_flag = halo[512:528, 0:128].astype(F32)
    halo_r5 = jnp.where(halo_flag == 1.0, 5.0 * DT, 0.0)
    halo_m5 = jnp.where(halo_flag == 2.0, 5.0 * DT, 0.0)
    halo_keep = 1.0 - 2.0 * halo_m5
    halo_keep_t = halo_keep - halo_r5

    def prepare(q, _):
        for s in range(8):
            p = q * 8 + s
            rows = x_extended(ts_ref, s, atm_ref[p], xa_ref, xb_ref, p, even_t)
            for i in range(4):
                put(cb_ref, ((q % 2) * 8 + s, q // 2, i), rows[i])
        return 0

    lax.fori_loop(0, 8, prepare, 0)
    flag_rows = x_extended(ts_ref, 0, flags_ref[...], xa_ref, xb_ref, 64, even_t)
    for i in range(4):
        flag = flag_rows[i]
        m5 = jnp.where(flag == 2.0, 5.0 * DT, 0.0)
        r5_ref[i] = jnp.where(flag == 1.0, 5.0 * DT, 0.0)
        mask_ref[0, i] = m5
        mask_ref[1, i] = 1.0 - 2.0 * m5
        mask_ref[2, i] = 1.0 - 2.0 * m5 - r5_ref[i]
    facc_ref[...] = jnp.zeros_like(facc_ref)
    dt_y = -DT * vec_ref[0:1, :]
    halo_dt_y = -DT * vec_ref[1:2, :]
    halo_dt_x = -DT * vec_ref[2:3, :]
    ff = vec_ref[pl.ds(4 + comp, 1), :]
    halo_ff = vec_ref[pl.ds(8 + comp, 1), :]
    for copy in copies:
        copy.wait()

    def step(si, _):
        which = jnp.minimum(si, 1)
        both = mm(cb_ref[...].reshape(4096, 256), rhs_ref[which, :, 0:256])
        dbuf_ref[...] = both[:, 0:128].reshape(LEVELS, 4, 4, 16, 128)
        abuf_ref[...] = both[:, 128:256].reshape(LEVELS, 4, 4, 16, 128)
        hbuf_ref[...] = mm(hcb_ref[...].reshape(1024, 256), rhs_ref[which, :, 256:640]).reshape(
            LEVELS, 4, 16, 384
        )
        for i in range(4):
            total = abuf_ref[0, 2, i]
            for l in range(1, LEVELS):
                total = total + abuf_ref[l, 2, i]
            mask_ref[3, i] = r5_ref[i] * (total * (1.0 / LEVELS))
        total = hbuf_ref[0, 2, :, 256:384]
        for l in range(1, LEVELS):
            total = total + hbuf_ref[l, 2, :, 256:384]
        tm_ref[...] = halo_r5 * (total * (1.0 / LEVELS))

        def level(l, _):
            above, below = jnp.minimum(l + 1, LEVELS - 1), jnp.maximum(l - 1, 0)
            wind_x, wind_y = scal_ref[l], scal_ref[LEVELS + l]
            cx = -DT * wind_x
            cy = dt_y * wind_y
            a = [[abuf_ref[l, k, i] for i in range(4)] for k in range(4)]

            slopes = [x_slopes(a[k]) for k in range(4)]
            new = [[None] * 4 for _ in range(4)]
            for i in range(4):
                m5, keep, keep_t, relax = [mask_ref[n, i] for n in range(4)]
                d = [slopes[k][i] for k in range(4)]
                dy = [dbuf_ref[l, k, i] for k in range(4)]
                extra = [
                    ff * a[1][i] - DT * d[3],
                    dt_y * dy[3] - ff * a[0][i],
                    relax,
                    dt_y * dy[1] - DT * d[0],
                ]
                for k in range(4):
                    mix = m5 * (abuf_ref[above, k, i] + abuf_ref[below, k, i])
                    own = (keep_t if k == 2 else keep) * a[k][i]
                    new[k][i] = (own + mix) + ((cx * d[k] + cy * dy[k]) + extra[k])

            halo_cx, halo_cy = halo_dt_x * wind_x, halo_dt_y * wind_y
            hx, hy, ha = [
                [hbuf_ref[l, k, :, 128 * n : 128 * n + 128] for k in range(4)] for n in range(3)
            ]
            extra = [
                halo_ff * ha[1] + halo_dt_x * hx[3],
                halo_dt_y * hy[3] - halo_ff * ha[0],
                tm_ref[...],
                halo_dt_y * hy[1] + halo_dt_x * hx[0],
            ]
            for k in range(4):
                first = 0.5 * (new[k][0] + pltpu.roll(new[k][3], 1, 0))
                values = [first, new[k][1], new[k][2], pltpu.roll(first, 15, 0)]
                up, down = hbuf_ref[above, k, :, 256:384], hbuf_ref[below, k, :, 256:384]
                own = (halo_keep_t if k == 2 else halo_keep) * ha[k] + halo_m5 * (up + down)
                own = own + ((halo_cx * hx[k] + halo_cy * hy[k]) + extra[k])
                lower = pltpu.roll(pltpu.roll(own, 32, 1), 1, 0)
                upper = pltpu.roll(pltpu.roll(own, 96, 1), 15, 0)
                partner = jnp.where(quarter == 0, lower, jnp.where(quarter == 3, upper, own))
                own = 0.5 * (own + partner)
                across = None
                for i in range(4):
                    moved = pltpu.roll(values[i], 32 * i + 16, 1)
                    across = moved if i == 0 else jnp.where(quarter == i, moved, across)
                    back = pltpu.roll(own, 112 - 32 * i, 1)
                    put(cb_ref, (l, k, i), jnp.where(edge, 0.5 * (values[i] + back), values[i]))
                put(hcb_ref, (l, k), jnp.where(halo_edge, 0.5 * (own + across), own))
            return 0

        lax.fori_loop(0, LEVELS, level, 0, unroll=2)
        surface = mm(cb_ref[0].reshape(256, 256), rhs_ref[1, :, 128:256]).reshape(4, 4, 16, 128)
        for i in range(4):
            u, v, t, z = [surface[k, i, 0:8] for k in range(4)]
            speed = jnp.sqrt(u * u + v * v + 1.0)
            for c in range(NFLUX):
                m0, m1, m2, m3 = [scal_ref[32 + 4 * c + k] for k in range(4)]
                m = (m0 * u + m1 * v) + (m2 * t + m3 * z)
                facc_ref[c, i] += speed * m * lax.rsqrt(1.0 + 0.5 * (m * m))
        return 0

    lax.fori_loop(0, STEPS, step, 0)
    final = mm(cb_ref[...].reshape(4096, 256), rhs_ref[1, :, 128:256]).reshape(LEVELS, 4, 4, 16, 128)
    for l in range(LEVELS):
        for k in range(4):
            for i in range(4):
                out_ref[k * LEVELS + l, pl.ds(i, 8, stride=4), :] = final[l, k, i, 0:8]
    for i in range(4):
        mean = [(facc_ref[c, i] * (1.0 / STEPS)).astype(BF16).astype(F32) for c in range(NFLUX)]
        for g in range(4):
            total = scal_ref[80 + 12 * g] * mean[0]
            for c in range(1, NFLUX):
                total = total + scal_ref[80 + 12 * g + c] * mean[c]
            gs_ref[g, pl.ds(i, 8, stride=4), :] = 0.25 * total
    table_ref[...] = gs_ref[...].reshape(128, 128).astype(BF16)


def pick_kernel(served_ref, table_ref, rows_ref):
    pick = served_ref[...].astype(F32) == iota((512, 128), 1).astype(F32)
    rows_ref[...] = mm(jnp.where(pick, 1.0, 0.0).astype(BF16), table_ref[...]).astype(BF16)


def request_matrix(tcol_ref):
    parts = []
    for chunk in range(4):
        hit = tcol_ref[...] == iota((512, 128), 1) + 128 * chunk
        parts.append(jnp.where(hit, 1.0, 0.0).astype(BF16))
    return jnp.concatenate(parts, axis=1)


def force_block(window, wm, sw, n2_ref, ocean_ref, b):
    cells = slice(128 * b, 128 * b + 128)
    hi, lo = split_bf16(window)
    own = window[:, 128:256]
    both = mm(jnp.concatenate([hi.astype(F32), lo.astype(F32)], axis=0).astype(BF16), wm)
    top = both[0:8] + both[8:16] + (1.8 - sw) * own
    surface = []
    for k in range(4):
        value = n2_ref[16 * k : 16 * k + 1, cells] + top[k : k + 1]
        if k == 2:
            value = value + 0.2 * own[3:4]
        if k == 3:
            value = value - 0.2 * own[2:3]
        below = n2_ref[16 * k + 1 : 16 * k + 2, cells] + 0.2 * own[k : k + 1]
        ocean_ref[16 * k : 16 * k + 1, cells] = value
        ocean_ref[16 * k + 1 : 16 * k + 2, cells] = below
        surface.append(value)
    return jnp.concatenate(surface + [jnp.zeros((4, 128), F32)], axis=0).astype(BF16)


def return_parts(surface, weights, parts_ref, b):
    parts = mm(surface, jnp.concatenate([weights[k] for k in range(8)], axis=1))
    for k in range(8):
        rows = slice((b * 8 + k) * 8, (b * 8 + k) * 8 + 8)
        parts_ref[rows, :] = parts[:, 128 * k : 128 * k + 128]


def ocean_kernel(
    par_ref,
    ocean_ref,
    off_ref,
    w_ref,
    ya_ref,
    yb_ref,
    f_ref,
    weights_ref,
    tcol_ref,
    n2_ref,
    ends_ref,
    sw_ref,
    parts_ref,
    table_ref,
    o1_ref,
    wm_ref,
):
    even_c = par_ref[1] == 0

    def halo_rows(n):
        rows = slice(528 + 16 * n, 544 + 16 * n)
        a, b = ya_ref[rows].astype(F32), yb_ref[rows].astype(F32)
        return jnp.where(even_c, b, a), jnp.where(even_c, a, b)

    pieces = [halo_rows(n) for n in range(9)]
    left = [jnp.concatenate([p[0] for p in pieces[4 * n : 4 * n + 4]], axis=0) for n in range(2)]
    right = [jnp.concatenate([p[1] for p in pieces[4 * n : 4 * n + 4]], axis=0) for n in range(2)]
    values = {-2: left[0], -1: left[1], 8: right[0], 9: right[1]}
    for b in range(8):
        values[b] = ocean_ref[:, 128 * b : 128 * b + 128]
    offw = {-1: pieces[8][0], 8: pieces[8][1]}
    source = iota((384, 128), 0)
    lane = iota((1, 128), 1)
    level = iota((64, 128), 0) & 15

    def matrix(b):
        if b in offw:
            off, w = offw[b][0:6].astype(I32), offw[b][8:14]
        else:
            cells = slice(128 * b, 128 * b + 128)
            off, w = off_ref[:, cells], w_ref[:, cells].astype(BF16).astype(F32)
        total = jnp.zeros((384, 128), F32)
        for j in range(6):
            total = total + jnp.where(source == lane + off[j : j + 1], w[j : j + 1], 0.0)
        return total.astype(BF16), jnp.sum(w, axis=0, keepdims=True)

    def update(own, window, wm, sw):
        hi, lo = split_bf16(window)
        both = mm(jnp.concatenate([hi, lo], axis=0), wm)
        lateral = both[0:64] + both[64:128] - sw * own
        above = jnp.where(level == 15, own, pltpu.roll(own, 63, 0))
        below = jnp.where(level == 0, own, pltpu.roll(own, 1, 0))
        rot = jnp.concatenate([jnp.zeros((32, 128), F32), 0.2 * own[48:64], -0.2 * own[32:48]], axis=0)
        return own + lateral + 0.2 * (above - 2.0 * own + below) + rot

    for b in range(-1, 9):
        wm, sw = matrix(b)
        if 0 <= b < 8:
            wm_ref[b] = wm
            sw_ref[:, 128 * b : 128 * b + 128] = jnp.broadcast_to(sw, (8, 128))
        window = jnp.concatenate([values[b - 1], values[b], values[b + 1]], axis=1)
        o1_ref[b + 1] = update(values[b], window, wm, sw)
    for b in range(8):
        window = jnp.concatenate([o1_ref[b], o1_ref[b + 1], o1_ref[b + 2]], axis=1)
        cells = slice(128 * b, 128 * b + 128)
        n2_ref[:, cells] = update(o1_ref[b + 1], window, wm_ref[b], sw_ref[0:1, cells])
    for b in range(1, 7):
        cells = slice(128 * b, 128 * b + 128)
        window = f_ref[:, 128 * b - 128 : 128 * b + 256]
        surface = force_block(window, wm_ref[b], sw_ref[:, cells], n2_ref, n2_ref, b)
        return_parts(surface, weights_ref[b], parts_ref, b)
    ends_ref[0] = wm_ref[0]
    ends_ref[1] = wm_ref[7]
    for b in (0, 7):
        parts_ref[64 * b : 64 * b + 64, :] = jnp.zeros((64, 128), F32)
    table_ref[...] = request_matrix(tcol_ref)


def forcing_kernel(par_ref, rows_ref, tcol_ref, weights_ref, f_ref, a_ref, b_ref):
    even_c = par_ref[1] == 0
    gathered = mm(request_matrix(tcol_ref), rows_ref[...])
    for b in range(8):
        lhs = jnp.concatenate(
            [gathered[(b * 8 + k) * 8 : (b * 8 + k) * 8 + 8] for k in range(8)], axis=1
        ).astype(BF16)
        f_ref[:, 128 * b : 128 * b + 128] = mm(lhs, weights_ref[b])
    right, left = f_ref[:, 896:1024], f_ref[:, 0:128]
    a_ref[...] = jnp.where(even_c, right, left)
    b_ref[...] = jnp.where(even_c, left, right)


def return_kernel(
    par_ref,
    n2_ref,
    ends_ref,
    sw_ref,
    f_ref,
    ea_ref,
    eb_ref,
    inner_ref,
    table_ref,
    first_ref,
    last_ref,
    ocean_ref,
    sent_ref,
    parts_ref,
):
    even_c = par_ref[1] == 0
    ea, eb = ea_ref[...], eb_ref[...]
    ocean_ref[...] = n2_ref[...]
    parts_ref[...] = inner_ref[...]
    window = jnp.concatenate([jnp.where(even_c, eb, ea), f_ref[:, 0:256]], axis=1)
    surface = force_block(window, ends_ref[0], sw_ref[:, 0:128], n2_ref, ocean_ref, 0)
    return_parts(surface, first_ref, parts_ref, 0)
    window = jnp.concatenate([f_ref[:, 768:1024], jnp.where(even_c, ea, eb)], axis=1)
    surface = force_block(window, ends_ref[1], sw_ref[:, 896:1024], n2_ref, ocean_ref, 7)
    return_parts(surface, last_ref, parts_ref, 7)
    sent_ref[...] = mm_t(table_ref[...], parts_ref[...].astype(BF16)).astype(BF16)


def collect_kernel(served_ref, incoming_ref, out_ref):
    pick = served_ref[...].astype(F32) == iota((512, 128), 1).astype(F32)
    owner = jnp.where(pick, 1.0, 0.0).astype(BF16)
    out_ref[...] = mm_t(owner, incoming_ref[...]).reshape(4, 32, 128)


def swap_pairs(n):
    near = [(i, i ^ 1) for i in range(n)]
    far = [(i, (i + 1) % n if i % 2 else (i - 1) % n) for i in range(n)]
    return near, far


def exchange(payloads, axis, n):
    near, far = swap_pairs(n)
    return lax.ppermute(payloads[0], axis, near), lax.ppermute(payloads[1], axis, far)


def to_tiles(rows):
    moved = lax.all_to_all(
        rows.reshape(N_TILE, 16, 128), "tile", split_axis=0, concat_axis=0, tiled=True
    )
    return moved.reshape(512, 128)


def call(kernel, out, specs, scratch=(), mib=16, cost=None):
    return pl.pallas_call(
        kernel,
        out_shape=out,
        in_specs=specs,
        out_specs=jax.tree.map(lambda _: VMEM, out),
        scratch_shapes=list(scratch),
        compiler_params=pltpu.CompilerParams(vmem_limit_bytes=mib * 2**20),
        cost_estimate=cost,
    )


def staged(kernel, out, scalars, resident, arrays, scratch=(), late=0, mib=16, cost=None):
    n_lead, n = len(scalars) + len(resident), len(arrays)
    n_out = len(jax.tree.leaves(out))

    def body(*refs):
        lead_refs, hbm_refs = refs[:n_lead], refs[n_lead : n_lead + n]
        out_refs = refs[n_lead + n : n_lead + n + n_out]
        held, (sems, *rest) = refs[-n - 1 - len(scratch) :][:n], refs[-1 - len(scratch) :]
        copies = [pltpu.make_async_copy(hbm_refs[i], held[i], sems.at[i]) for i in range(n)]
        for copy in copies:
            copy.start()
        for copy in copies[: n - late]:
            copy.wait()
        extra = (copies[n - late :],) if late else ()
        kernel(*lead_refs, *held, *out_refs, *rest, *extra)

    buffers = [pltpu.VMEM(a.shape, a.dtype) for a in arrays]
    scratch_shapes = buffers + [pltpu.SemaphoreType.DMA((n,))] + list(scratch)
    specs = [SMEM] * len(scalars) + [VMEM] * len(resident) + [HBM] * n
    return call(body, out, specs, scratch_shapes, mib, cost)(*scalars, *resident, *arrays)


ATM_SCRATCH = (
    pltpu.VMEM((LEVELS, 4, 4, 16, 256), BF16),
    pltpu.VMEM((LEVELS, 4, 4, 16, 128), F32),
    pltpu.VMEM((LEVELS, 4, 4, 16, 128), F32),
    pltpu.VMEM((LEVELS, 4, 16, 256), BF16),
    pltpu.VMEM((LEVELS, 4, 16, 384), F32),
    pltpu.VMEM((16, 128), F32),
    pltpu.VMEM((4, 4, 16, 128), F32),
    pltpu.VMEM((4, 16, 128), F32),
    pltpu.VMEM((NFLUX, 4, 8, 128), F32),
    pltpu.VMEM((4, 32, 128), F32),
    pltpu.VMEM((8, 64, 128), F32),
)


def per_device(
    atm_state,
    level_winds,
    physics_flags,
    flux_matrix,
    regrid_source,
    regrid_weights,
    return_weights,
    ocean_state,
    ocean_neighbors,
    edge_weights,
    ocean_coupling,
):
    S = jax.ShapeDtypeStruct
    t, c = lax.axis_index("tile"), lax.axis_index("comp")
    par = jnp.stack([t % 2, c % 2, c, t]).astype(I32)
    atm = atm_state.reshape(64, 32, 128)
    ocean = ocean_state.reshape(64, 1024)
    scal = jnp.concatenate(
        [level_winds.reshape(-1), flux_matrix.reshape(-1), ocean_coupling.reshape(-1)]
    )
    rhs = jnp.asarray(lane_matrices())
    vec = jnp.asarray(lane_vectors())

    xp_a, xp_b, flags = staged(
        x_pack_kernel,
        (S((X_PLANES, 16, 128), BF16),) * 2 + (S((32, 128), F32),),
        (par,),
        (),
        (atm, physics_flags, ocean, ocean_neighbors, edge_weights),
        mib=12,
    )
    xa, xb = exchange((xp_a, xp_b), "tile", N_TILE)
    wanted, tcol = call(slots_kernel, (S((512, 128), BF16), S((512, 128), I32)), [VMEM])(
        regrid_source
    )
    wanted, tcol, xb = lax.optimization_barrier((wanted, tcol, xb))
    served = to_tiles(wanted)
    y_payload = call(
        y_pack_kernel,
        (S((Y_ROWS, 128), BF16),) * 2,
        [SMEM] + [VMEM] * 6,
        [pltpu.VMEM((33, 16, 1024), BF16), pltpu.VMEM((8, 64, 128), F32)],
    )(par, atm, flags, xa, xb, xp_a, xp_b)
    ya, yb = exchange(y_payload, "comp", N_COMP)
    atm_final, table = staged(
        atm_kernel,
        (S((64, 32, 128), F32), S((128, 128), BF16)),
        (par, scal),
        (atm, flags, xa, xb, ya, yb),
        (vec, rhs),
        ATM_SCRATCH,
        late=1,
        mib=32,
        cost=pl.CostEstimate(flops=2**33, bytes_accessed=2**26, transcendentals=0),
    )
    rows = call(pick_kernel, S((512, 128), BF16), [VMEM] * 2)(served, table)
    mean_rows = to_tiles(rows)
    forcing, *edges = call(
        forcing_kernel,
        (S((8, 1024), F32), S((8, 128), F32), S((8, 128), F32)),
        [SMEM] + [VMEM] * 3,
    )(par, mean_rows, tcol, regrid_weights.reshape(8, 1024, 128))
    ea, eb = exchange(edges, ("tile", "comp"), N_TILE * N_COMP)
    n2, ends, sw, parts, table = call(
        ocean_kernel,
        (
            S((64, 1024), F32),
            S((2, 384, 128), BF16),
            S((8, 1024), F32),
            S((512, 128), F32),
            S((512, 512), BF16),
        ),
        [SMEM] + [VMEM] * 8,
        [pltpu.VMEM((10, 64, 128), F32), pltpu.VMEM((8, 384, 128), BF16)],
        cost=pl.CostEstimate(flops=2**27, bytes_accessed=2**24, transcendentals=0),
    )(par, ocean, ocean_neighbors, edge_weights, ya, yb, forcing, return_weights, tcol)
    ocean_final, sent = call(
        return_kernel,
        (S((64, 1024), F32), S((512, 128), BF16)),
        [SMEM] + [VMEM] * 10,
        [pltpu.VMEM((512, 128), F32)],
    )(par, n2, ends, sw, forcing, ea, eb, parts, table, return_weights[0], return_weights[7])
    incoming = to_tiles(sent)
    ocean_on_atm = call(collect_kernel, S((4, 32, 128), F32), [VMEM] * 2)(served, incoming)
    return (
        atm_final.reshape(atm_state.shape),
        ocean_final.reshape(ocean_state.shape),
        ocean_on_atm,
    )


def solution(mesh):
    return jax.shard_map(
        per_device,
        mesh=mesh,
        in_specs=(
            P(None, None, "tile", "comp"),
            P(),
            P("tile", "comp"),
            P(),
            P(("tile", "comp"), None),
            P(("tile", "comp"), None, None, None),
            P(("tile", "comp"), None, None, None),
            P(None, None, ("tile", "comp")),
            P(None, ("tile", "comp")),
            P(None, ("tile", "comp")),
            P(),
        ),
        out_specs=(
            P(None, None, "tile", "comp"),
            P(None, None, ("tile", "comp")),
            P(None, "tile", "comp"),
        ),
        check_vma=False,
    )
```

```python
import functools

import jax
import jax.numpy as jnp
import ml_dtypes
import numpy as np
from jax import lax
from jax.experimental import pallas as pl
from jax.experimental.pallas import tpu as pltpu
from jax.sharding import PartitionSpec as P

F32 = jnp.float32
BF16 = jnp.bfloat16
I32 = jnp.int32
N_TILE, N_COMP = 32, 4
STEPS = 4
LEVELS = 16
NFLUX = 12
DT = 0.02
VMEM = pl.BlockSpec(memory_space=pltpu.VMEM)
HBM = pl.BlockSpec(memory_space=pltpu.HBM)
SMEM = pl.BlockSpec(memory_space=pltpu.SMEM)
X_PLANES = 74
Y_ROWS = 672


def gll_derivative():
    points = np.array([-1.0, -1.0 / np.sqrt(5.0), 1.0 / np.sqrt(5.0), 1.0])
    products = np.array(
        [np.prod([points[r] - points[s] for s in range(4) if s != r]) for r in range(4)]
    )
    table = np.zeros((4, 4))
    for r in range(4):
        for s in range(4):
            if r != s:
                table[r, s] = products[r] / (products[s] * (points[r] - points[s]))
    table[0, 0], table[3, 3] = -3.0, 3.0
    return 2.0 * table


DERIV = gll_derivative()
ROW_SCALE = np.array([1.375, 1.125, 1.125, 1.375])


SCALED = (DERIV * ROW_SCALE[:, None]).astype(ml_dtypes.bfloat16).astype(np.float64)


def y_nodes():
    lane = np.arange(32)
    return np.where(lane < 16, 143 - lane, 15 - lane)


def lane_operators(nodes):
    count = len(nodes)
    deriv, average = np.zeros((count, count)), np.eye(count)
    where = {int(y): p for p, y in enumerate(nodes)}
    for y, p in where.items():
        for j in range(4):
            deriv[p, where[y - y % 4 + j]] = SCALED[y % 4, j]
        other = y - 1 if y % 4 == 0 else y + 1
        if y % 4 in (0, 3) and other in where:
            average[p, p] = average[p, where[other]] = 0.5
    return deriv, average


def twice(*matrices):
    both = np.concatenate([m.T for m in matrices], axis=1)
    return np.concatenate([both, both], axis=0)


def lane_matrices():
    eye = np.eye(128)
    deriv, average = lane_operators(np.arange(128))
    main = np.stack([twice(deriv, eye), twice(deriv @ average, average)])
    halo_deriv, halo_average = lane_operators(y_nodes())
    dy, av = np.kron(np.eye(4), halo_deriv), np.kron(np.eye(4), halo_average)
    dx = np.kron(SCALED, np.eye(32))
    halo = np.stack([twice(dx, dy, eye), twice(dx @ av, dy @ av, av)])
    return np.concatenate([main, halo], axis=2).astype(ml_dtypes.bfloat16)


def lane_vectors():
    vec = np.zeros((16, 128), np.float32)
    lane = np.arange(128)
    halo = np.tile(y_nodes(), 4)
    vec[0] = 1.0 / ROW_SCALE[lane % 4]
    vec[1] = 1.0 / ROW_SCALE[halo % 4]
    vec[2] = 1.0 / ROW_SCALE[lane // 32]
    for c in range(N_COMP):
        for row, y in ((4 + c, lane), (8 + c, halo)):
            vec[row] = DT * 0.5 * np.sin(2.0 * np.pi * (c * 128 + y + 0.5) / (128 * N_COMP))
    return vec


def split_bf16(x):
    hi = x.astype(BF16)
    return hi, (x - hi.astype(F32)).astype(BF16)


def iota(shape, dim):
    return lax.broadcasted_iota(I32, shape, dim)


def mm(a, b):
    return jnp.dot(a, b, preferred_element_type=F32)


def mm_t(a, b):
    return lax.dot_general(a, b, (((0,), (0,)), ((), ())), preferred_element_type=F32)


def slots_kernel(src_ref, wanted_ref, tcol_ref):
    s = src_ref[...] >> 2
    tile = (s >> 5).astype(F32)
    row = (s & 31).astype(F32)
    r0, a0 = iota((64, 8), 0), iota((64, 8), 1)
    pick_row = ((r0 >> 3) == a0).astype(F32)
    own = (r0 & 7) == a0
    tile_c = jnp.sum(jnp.where(own, mm(pick_row, tile), 0.0), axis=1, keepdims=True)
    b1, r1 = iota((8, 64), 0), iota((8, 64), 1)
    pick_col = (b1 == (r1 & 7)).astype(F32)
    own_t = b1 == (r1 >> 3)
    tile_r = jnp.sum(jnp.where(own_t, mm(tile, pick_col), 0.0), axis=0, keepdims=True)
    row_r = jnp.sum(jnp.where(own_t, mm(row, pick_col), 0.0), axis=0, keepdims=True)
    same = jnp.where(tile_c == tile_r, 1.0, 0.0)
    sub, lane = iota((64, 64), 0), iota((64, 64), 1)
    rank_c = jnp.sum(jnp.where(lane < sub, same, 0.0), axis=1, keepdims=True)
    rank_r = jnp.sum(jnp.where(sub < lane, same, 0.0), axis=0, keepdims=True)
    slot_c = (tile_c * 4.0 + rank_c).astype(I32)
    slot_r = (tile_r * 4.0 + rank_r).astype(I32)
    slot_wide = jnp.broadcast_to(slot_c, (64, 128))
    field = iota((64, 8, 128), 1)
    tcol = jnp.where(field < 4, slot_wide[:, None, :] * 4 + field, -1)
    tcol_ref[...] = tcol.reshape(512, 128)
    q = iota((512, 64), 0)
    val = jnp.sum(jnp.where((q >> 2) == slot_r, row_r + 1.0, 0.0), axis=1, keepdims=True) - 1.0
    f = (iota((512, 1), 0) & 3).astype(F32)
    target = jnp.where(val >= 0.0, f * 32.0 + val, -1.0)
    wanted_ref[...] = jnp.broadcast_to(target, (512, 128)).astype(BF16)


def one_hot(rows, target):
    return jnp.where(iota((rows, 256), 0) == target, 1.0, 0.0).astype(BF16)


def pack_matrix():
    col = iota((1, 256), 1)
    lane = col & 127
    plane = ((lane >> 4) & 1) * 4 + (lane >> 5)
    return one_hot(1024, plane * 128 + (lane & 15) + jnp.where(col < 128, 0, 112))


def unpack_matrix():
    col = iota((1, 256), 1)
    quarter, n = (col & 127) >> 5, col & 31
    base = 32 * quarter + 16 * (col >> 7)
    return one_hot(256, base + jnp.where(n < 16, 15 - n, 159 - n))


def x_pack_kernel(
    par_ref, atm_ref, flags_ref, ocean_ref, off_ref, w_ref, a_ref, b_ref, flags_out_ref
):
    even = par_ref[0] == 0

    def put(index, right, left):
        a_ref[index] = jnp.where(even, right, left).astype(BF16)
        b_ref[index] = jnp.where(even, left, right).astype(BF16)

    put(slice(0, 64), atm_ref[:, 16:32, :], atm_ref[:, 0:16, :])
    flags = flags_ref[...].astype(F32)
    flags_out_ref[...] = flags
    put(64, flags[16:32], flags[0:16])
    for part in range(2):
        right, left = [
            ocean_ref[:, c + 128 * part : c + 128 * part + 128].reshape(4, 16, 128) for c in (768, 0)
        ]
        put(slice(65 + 4 * part, 69 + 4 * part), right, left)
    off = off_ref[...].astype(F32)
    pad = jnp.zeros((2, 128), F32)
    right, left = [
        jnp.concatenate([off[:, c : c + 128], pad, w_ref[:, c : c + 128], pad], axis=0)
        for c in (896, 0)
    ]
    put(73, right, left)


def x_extended(ts_ref, slot, main, xa_ref, xb_ref, p, even):
    a, b = xa_ref[p].astype(F32), xb_ref[p].astype(F32)
    ts_ref[slot, 0:32] = main
    ts_ref[slot, 32:48] = jnp.where(even, a, b)
    ts_ref[slot, 48:64] = jnp.where(even, b, a)
    return [ts_ref[slot, pl.ds(i, 16, stride=4), :] for i in range(4)]


def y_pack_kernel(
    par_ref, atm_ref, flags_ref, xa_ref, xb_ref, pa_ref, pb_ref, a_ref, b_ref, lhs_ref, ts_ref
):
    even_t, even_c = par_ref[0] == 0, par_ref[1] == 0
    comp = par_ref[2]

    def group(q, _):
        for s in range(8):
            p = q * 8 + s
            rows = x_extended(ts_ref, s, atm_ref[p], xa_ref, xb_ref, p, even_t)
            for i in range(4):
                lanes = slice(((s % 2) * 4 + i) * 128, ((s % 2) * 4 + i) * 128 + 128)
                lhs_ref[q * 4 + s // 2, :, lanes] = rows[i].astype(BF16)
        return 0

    lax.fori_loop(0, 8, group, 0)
    rows = x_extended(ts_ref, 0, flags_ref[...], xa_ref, xb_ref, 64, even_t)
    for i in range(4):
        lhs_ref[32, :, 128 * i : 128 * i + 128] = rows[i].astype(BF16)
    lhs_ref[32, :, 512:1024] = jnp.zeros((16, 512), BF16)
    moved = mm(lhs_ref[...].reshape(528, 1024), pack_matrix())
    left, right = moved[:, 0:128], moved[:, 128:256]
    a_ref[0:528] = jnp.where(even_c, right, left).astype(BF16)
    b_ref[0:528] = jnp.where(even_c, left, right).astype(BF16)
    for n in range(9):
        p = 65 + n
        dest = slice(528 + 16 * n, 544 + 16 * n)
        a, b = xa_ref[p].astype(F32), xb_ref[p].astype(F32)
        own_a, own_b = pa_ref[p].astype(F32), pb_ref[p].astype(F32)
        from_left, from_right = jnp.where(even_t, b, a), jnp.where(even_t, a, b)
        own_right, own_left = jnp.where(even_t, own_a, own_b), jnp.where(even_t, own_b, own_a)
        right = jnp.where(comp == N_COMP - 1, from_left, own_right)
        left = jnp.where(comp == 0, from_right, own_left)
        a_ref[dest] = jnp.where(even_c, right, left).astype(BF16)
        b_ref[dest] = jnp.where(even_c, left, right).astype(BF16)


def prepare_kernel(par_ref, atm_ref, flags_ref, xa_ref, xb_ref, cb_ref, flag_ref, ts_ref):
    even_t = par_ref[0] == 0

    def group(q, _):
        for s in range(8):
            p = q * 8 + s
            rows = x_extended(ts_ref, s, atm_ref[p], xa_ref, xb_ref, p, even_t)
            for i in range(4):
                hi, lo = split_bf16(rows[i])
                cb_ref[(q % 2) * 8 + s, q // 2, i, :, 0:128] = hi
                cb_ref[(q % 2) * 8 + s, q // 2, i, :, 128:256] = lo
        return 0

    lax.fori_loop(0, 8, group, 0)
    rows = x_extended(ts_ref, 0, flags_ref[...], xa_ref, xb_ref, 64, even_t)
    for i in range(4):
        flag_ref[i] = rows[i]


def x_slopes(a):
    sums, diffs = (a[0] + a[3], a[1] + a[2]), (a[0] - a[3], a[1] - a[2])
    across = sums[0] - sums[1]
    out = [None] * 4
    for i in range(2):
        d = DERIV[i]
        odd = float((d[0] - d[3]) / 2) * diffs[0] + float((d[1] - d[2]) / 2) * diffs[1]
        even = float((d[0] + d[3]) / 2) * across
        out[i], out[3 - i] = odd + even, odd - even
    return out


def atm_kernel(
    par_ref,
    scal_ref,
    first_ref,
    flag_ref,
    ya_ref,
    yb_ref,
    vec_ref,
    rhs_ref,
    out_ref,
    table_ref,
    cb_ref,
    abuf_ref,
    dbuf_ref,
    hcb_ref,
    hbuf_ref,
    tm_ref,
    mask_ref,
    r5_ref,
    facc_ref,
    gs_ref,
    first_sem,
    copies,
):
    first_copy = pltpu.make_async_copy(first_ref, cb_ref, first_sem)
    first_copy.start()
    even_c = par_ref[1] == 0
    comp = par_ref[2]
    lane = iota((16, 128), 1)
    edge = (lane == 0) | (lane == 127)
    quarter = lane >> 5
    halo_edge = ((lane & 31) == 15) | ((lane & 31) == 16)

    def put(ref, index, value):
        hi, lo = split_bf16(value)
        ref[(*index, slice(None), slice(0, 128))] = hi
        ref[(*index, slice(None), slice(128, 256))] = lo

    ya, yb = ya_ref[0:528].astype(F32), yb_ref[0:528].astype(F32)
    from_right, from_left = jnp.where(even_c, ya, yb), jnp.where(even_c, yb, ya)
    arrived = jnp.concatenate([from_right, from_left], axis=1).astype(BF16)
    halo = mm(arrived, unpack_matrix()).astype(BF16)
    for k in range(4):
        for l in range(LEVELS):
            rows = slice((k * 8 + l // 2) * 16, (k * 8 + l // 2) * 16 + 16)
            lanes = slice((l % 2) * 128, (l % 2) * 128 + 128)
            hcb_ref[l, k, :, 0:128] = halo[rows, lanes]
            hcb_ref[l, k, :, 128:256] = jnp.zeros((16, 128), BF16)
    halo_flag = halo[512:528, 0:128].astype(F32)
    halo_r5 = jnp.where(halo_flag == 1.0, 5.0 * DT, 0.0)
    halo_m5 = jnp.where(halo_flag == 2.0, 5.0 * DT, 0.0)
    halo_keep = 1.0 - 2.0 * halo_m5
    halo_keep_t = halo_keep - halo_r5
    for i in range(4):
        flag = flag_ref[i]
        m5 = jnp.where(flag == 2.0, 5.0 * DT, 0.0)
        r5_ref[i] = jnp.where(flag == 1.0, 5.0 * DT, 0.0)
        mask_ref[0, i] = m5
        mask_ref[1, i] = 1.0 - 2.0 * m5
        mask_ref[2, i] = 1.0 - 2.0 * m5 - r5_ref[i]
    facc_ref[...] = jnp.zeros_like(facc_ref)
    dt_y = -DT * vec_ref[0:1, :]
    halo_dt_y = -DT * vec_ref[1:2, :]
    halo_dt_x = -DT * vec_ref[2:3, :]
    ff = vec_ref[pl.ds(4 + comp, 1), :]
    halo_ff = vec_ref[pl.ds(8 + comp, 1), :]
    for copy in (first_copy, *copies):
        copy.wait()

    def step(si, _):
        which = jnp.minimum(si, 1)
        both = mm(cb_ref[...].reshape(4096, 256), rhs_ref[which, :, 0:256])
        dbuf_ref[...] = both[:, 0:128].reshape(LEVELS, 4, 4, 16, 128)
        abuf_ref[...] = both[:, 128:256].reshape(LEVELS, 4, 4, 16, 128)
        hbuf_ref[...] = mm(hcb_ref[...].reshape(1024, 256), rhs_ref[which, :, 256:640]).reshape(
            LEVELS, 4, 16, 384
        )
        for i in range(4):
            total = abuf_ref[0, 2, i]
            for l in range(1, LEVELS):
                total = total + abuf_ref[l, 2, i]
            mask_ref[3, i] = r5_ref[i] * (total * (1.0 / LEVELS))
        total = hbuf_ref[0, 2, :, 256:384]
        for l in range(1, LEVELS):
            total = total + hbuf_ref[l, 2, :, 256:384]
        tm_ref[...] = halo_r5 * (total * (1.0 / LEVELS))

        def level(l, _):
            above, below = jnp.minimum(l + 1, LEVELS - 1), jnp.maximum(l - 1, 0)
            wind_x, wind_y = scal_ref[l], scal_ref[LEVELS + l]
            cx = -DT * wind_x
            cy = dt_y * wind_y
            a = [[abuf_ref[l, k, i] for i in range(4)] for k in range(4)]

            slopes = [x_slopes(a[k]) for k in range(4)]
            new = [[None] * 4 for _ in range(4)]
            for i in range(4):
                m5, keep, keep_t, relax = [mask_ref[n, i] for n in range(4)]
                d = [slopes[k][i] for k in range(4)]
                dy = [dbuf_ref[l, k, i] for k in range(4)]
                extra = [
                    ff * a[1][i] - DT * d[3],
                    dt_y * dy[3] - ff * a[0][i],
                    relax,
                    dt_y * dy[1] - DT * d[0],
                ]
                for k in range(4):
                    mix = m5 * (abuf_ref[above, k, i] + abuf_ref[below, k, i])
                    own = (keep_t if k == 2 else keep) * a[k][i]
                    new[k][i] = (own + mix) + ((cx * d[k] + cy * dy[k]) + extra[k])

            halo_cx, halo_cy = halo_dt_x * wind_x, halo_dt_y * wind_y
            hx, hy, ha = [
                [hbuf_ref[l, k, :, 128 * n : 128 * n + 128] for k in range(4)] for n in range(3)
            ]
            extra = [
                halo_ff * ha[1] + halo_dt_x * hx[3],
                halo_dt_y * hy[3] - halo_ff * ha[0],
                tm_ref[...],
                halo_dt_y * hy[1] + halo_dt_x * hx[0],
            ]
            for k in range(4):
                first = 0.5 * (new[k][0] + pltpu.roll(new[k][3], 1, 0))
                values = [first, new[k][1], new[k][2], pltpu.roll(first, 15, 0)]
                up, down = hbuf_ref[above, k, :, 256:384], hbuf_ref[below, k, :, 256:384]
                own = (halo_keep_t if k == 2 else halo_keep) * ha[k] + halo_m5 * (up + down)
                own = own + ((halo_cx * hx[k] + halo_cy * hy[k]) + extra[k])
                lower = pltpu.roll(pltpu.roll(own, 32, 1), 1, 0)
                upper = pltpu.roll(pltpu.roll(own, 96, 1), 15, 0)
                partner = jnp.where(quarter == 0, lower, jnp.where(quarter == 3, upper, own))
                own = 0.5 * (own + partner)
                across = None
                for i in range(4):
                    moved = pltpu.roll(values[i], 32 * i + 16, 1)
                    across = moved if i == 0 else jnp.where(quarter == i, moved, across)
                    back = pltpu.roll(own, 112 - 32 * i, 1)
                    put(cb_ref, (l, k, i), jnp.where(edge, 0.5 * (values[i] + back), values[i]))
                put(hcb_ref, (l, k), jnp.where(halo_edge, 0.5 * (own + across), own))
            return 0

        lax.fori_loop(0, LEVELS, level, 0, unroll=2)
        surface = mm(cb_ref[0].reshape(256, 256), rhs_ref[1, :, 128:256]).reshape(4, 4, 16, 128)
        for i in range(4):
            u, v, t, z = [surface[k, i, 0:8] for k in range(4)]
            speed = jnp.sqrt(u * u + v * v + 1.0)
            for c in range(NFLUX):
                m0, m1, m2, m3 = [scal_ref[32 + 4 * c + k] for k in range(4)]
                m = (m0 * u + m1 * v) + (m2 * t + m3 * z)
                facc_ref[c, i] += speed * m * lax.rsqrt(1.0 + 0.5 * (m * m))
        return 0

    lax.fori_loop(0, STEPS, step, 0)
    final = mm(cb_ref[...].reshape(4096, 256), rhs_ref[1, :, 128:256]).reshape(LEVELS, 4, 4, 16, 128)
    for l in range(LEVELS):
        for k in range(4):
            for i in range(4):
                out_ref[k * LEVELS + l, pl.ds(i, 8, stride=4), :] = final[l, k, i, 0:8]
    for i in range(4):
        mean = [(facc_ref[c, i] * (1.0 / STEPS)).astype(BF16).astype(F32) for c in range(NFLUX)]
        for g in range(4):
            total = scal_ref[80 + 12 * g] * mean[0]
            for c in range(1, NFLUX):
                total = total + scal_ref[80 + 12 * g + c] * mean[c]
            gs_ref[g, pl.ds(i, 8, stride=4), :] = 0.25 * total
    table_ref[...] = gs_ref[...].reshape(128, 128).astype(BF16)


def pick_kernel(served_ref, table_ref, rows_ref):
    pick = served_ref[...].astype(F32) == iota((512, 128), 1).astype(F32)
    rows_ref[...] = mm(jnp.where(pick, 1.0, 0.0).astype(BF16), table_ref[...]).astype(BF16)


def request_matrix(tcol_ref):
    parts = []
    for chunk in range(4):
        hit = tcol_ref[...] == iota((512, 128), 1) + 128 * chunk
        parts.append(jnp.where(hit, 1.0, 0.0).astype(BF16))
    return jnp.concatenate(parts, axis=1)


def force_block(window, wm, sw, n2_ref, ocean_ref, b):
    cells = slice(128 * b, 128 * b + 128)
    hi, lo = split_bf16(window)
    own = window[:, 128:256]
    both = mm(jnp.concatenate([hi.astype(F32), lo.astype(F32)], axis=0).astype(BF16), wm)
    top = both[0:8] + both[8:16] + (1.8 - sw) * own
    surface = []
    for k in range(4):
        value = n2_ref[16 * k : 16 * k + 1, cells] + top[k : k + 1]
        if k == 2:
            value = value + 0.2 * own[3:4]
        if k == 3:
            value = value - 0.2 * own[2:3]
        below = n2_ref[16 * k + 1 : 16 * k + 2, cells] + 0.2 * own[k : k + 1]
        ocean_ref[16 * k : 16 * k + 1, cells] = value
        ocean_ref[16 * k + 1 : 16 * k + 2, cells] = below
        surface.append(value)
    return jnp.concatenate(surface + [jnp.zeros((4, 128), F32)], axis=0).astype(BF16)


def return_parts(surface, weights, parts_ref, b):
    parts = mm(surface, jnp.concatenate([weights[k] for k in range(8)], axis=1))
    for k in range(8):
        rows = slice((b * 8 + k) * 8, (b * 8 + k) * 8 + 8)
        parts_ref[rows, :] = parts[:, 128 * k : 128 * k + 128]


def ocean_kernel(
    par_ref,
    ocean_ref,
    off_ref,
    w_ref,
    ya_ref,
    yb_ref,
    f_ref,
    weights_ref,
    tcol_ref,
    n2_ref,
    ends_ref,
    sw_ref,
    parts_ref,
    table_ref,
    o1_ref,
    wm_ref,
):
    even_c = par_ref[1] == 0

    def halo_rows(n):
        rows = slice(528 + 16 * n, 544 + 16 * n)
        a, b = ya_ref[rows].astype(F32), yb_ref[rows].astype(F32)
        return jnp.where(even_c, b, a), jnp.where(even_c, a, b)

    pieces = [halo_rows(n) for n in range(9)]
    left = [jnp.concatenate([p[0] for p in pieces[4 * n : 4 * n + 4]], axis=0) for n in range(2)]
    right = [jnp.concatenate([p[1] for p in pieces[4 * n : 4 * n + 4]], axis=0) for n in range(2)]
    values = {-2: left[0], -1: left[1], 8: right[0], 9: right[1]}
    for b in range(8):
        values[b] = ocean_ref[:, 128 * b : 128 * b + 128]
    offw = {-1: pieces[8][0], 8: pieces[8][1]}
    source = iota((384, 128), 0)
    lane = iota((1, 128), 1)
    level = iota((64, 128), 0) & 15

    def matrix(b):
        if b in offw:
            off, w = offw[b][0:6].astype(I32), offw[b][8:14]
        else:
            cells = slice(128 * b, 128 * b + 128)
            off, w = off_ref[:, cells], w_ref[:, cells].astype(BF16).astype(F32)
        total = jnp.zeros((384, 128), F32)
        for j in range(6):
            total = total + jnp.where(source == lane + off[j : j + 1], w[j : j + 1], 0.0)
        return total.astype(BF16), jnp.sum(w, axis=0, keepdims=True)

    def update(own, window, wm, sw):
        hi, lo = split_bf16(window)
        both = mm(jnp.concatenate([hi, lo], axis=0), wm)
        lateral = both[0:64] + both[64:128] - sw * own
        above = jnp.where(level == 15, own, pltpu.roll(own, 63, 0))
        below = jnp.where(level == 0, own, pltpu.roll(own, 1, 0))
        rot = jnp.concatenate([jnp.zeros((32, 128), F32), 0.2 * own[48:64], -0.2 * own[32:48]], axis=0)
        return own + lateral + 0.2 * (above - 2.0 * own + below) + rot

    for b in range(-1, 9):
        wm, sw = matrix(b)
        if 0 <= b < 8:
            wm_ref[b] = wm
            sw_ref[:, 128 * b : 128 * b + 128] = jnp.broadcast_to(sw, (8, 128))
        window = jnp.concatenate([values[b - 1], values[b], values[b + 1]], axis=1)
        o1_ref[b + 1] = update(values[b], window, wm, sw)
    for b in range(8):
        window = jnp.concatenate([o1_ref[b], o1_ref[b + 1], o1_ref[b + 2]], axis=1)
        cells = slice(128 * b, 128 * b + 128)
        n2_ref[:, cells] = update(o1_ref[b + 1], window, wm_ref[b], sw_ref[0:1, cells])
    for b in range(1, 7):
        cells = slice(128 * b, 128 * b + 128)
        window = f_ref[:, 128 * b - 128 : 128 * b + 256]
        surface = force_block(window, wm_ref[b], sw_ref[:, cells], n2_ref, n2_ref, b)
        return_parts(surface, weights_ref[b], parts_ref, b)
    ends_ref[0] = wm_ref[0]
    ends_ref[1] = wm_ref[7]
    for b in (0, 7):
        parts_ref[64 * b : 64 * b + 64, :] = jnp.zeros((64, 128), F32)
    table_ref[...] = request_matrix(tcol_ref)


def forcing_kernel(par_ref, rows_ref, tcol_ref, weights_ref, f_ref, a_ref, b_ref):
    even_c = par_ref[1] == 0
    gathered = mm(request_matrix(tcol_ref), rows_ref[...])
    for b in range(8):
        lhs = jnp.concatenate(
            [gathered[(b * 8 + k) * 8 : (b * 8 + k) * 8 + 8] for k in range(8)], axis=1
        ).astype(BF16)
        f_ref[:, 128 * b : 128 * b + 128] = mm(lhs, weights_ref[b])
    right, left = f_ref[:, 896:1024], f_ref[:, 0:128]
    a_ref[...] = jnp.where(even_c, right, left)
    b_ref[...] = jnp.where(even_c, left, right)


def return_kernel(
    par_ref,
    n2_ref,
    ends_ref,
    sw_ref,
    f_ref,
    ea_ref,
    eb_ref,
    inner_ref,
    table_ref,
    first_ref,
    last_ref,
    ocean_ref,
    sent_ref,
    parts_ref,
):
    even_c = par_ref[1] == 0
    ea, eb = ea_ref[...], eb_ref[...]
    ocean_ref[...] = n2_ref[...]
    parts_ref[...] = inner_ref[...]
    window = jnp.concatenate([jnp.where(even_c, eb, ea), f_ref[:, 0:256]], axis=1)
    surface = force_block(window, ends_ref[0], sw_ref[:, 0:128], n2_ref, ocean_ref, 0)
    return_parts(surface, first_ref, parts_ref, 0)
    window = jnp.concatenate([f_ref[:, 768:1024], jnp.where(even_c, ea, eb)], axis=1)
    surface = force_block(window, ends_ref[1], sw_ref[:, 896:1024], n2_ref, ocean_ref, 7)
    return_parts(surface, last_ref, parts_ref, 7)
    sent_ref[...] = mm_t(table_ref[...], parts_ref[...].astype(BF16)).astype(BF16)


def collect_kernel(served_ref, incoming_ref, out_ref):
    pick = served_ref[...].astype(F32) == iota((512, 128), 1).astype(F32)
    owner = jnp.where(pick, 1.0, 0.0).astype(BF16)
    out_ref[...] = mm_t(owner, incoming_ref[...]).reshape(4, 32, 128)


def swap_pairs(n):
    near = [(i, i ^ 1) for i in range(n)]
    far = [(i, (i + 1) % n if i % 2 else (i - 1) % n) for i in range(n)]
    return near, far


def exchange(payloads, axis, n):
    near, far = swap_pairs(n)
    return lax.ppermute(payloads[0], axis, near), lax.ppermute(payloads[1], axis, far)


def to_tiles(rows):
    moved = lax.all_to_all(
        rows.reshape(N_TILE, 16, 128), "tile", split_axis=0, concat_axis=0, tiled=True
    )
    return moved.reshape(512, 128)


def call(kernel, out, specs, scratch=(), mib=16, cost=None):
    return pl.pallas_call(
        kernel,
        out_shape=out,
        in_specs=specs,
        out_specs=jax.tree.map(lambda _: VMEM, out),
        scratch_shapes=list(scratch),
        compiler_params=pltpu.CompilerParams(vmem_limit_bytes=mib * 2**20),
        cost_estimate=cost,
    )


def staged(kernel, out, scalars, resident, arrays, scratch=(), late=0, mib=16, cost=None):
    n_lead, n = len(scalars) + len(resident), len(arrays)
    n_out = len(jax.tree.leaves(out))

    def body(*refs):
        lead_refs, hbm_refs = refs[:n_lead], refs[n_lead : n_lead + n]
        out_refs = refs[n_lead + n : n_lead + n + n_out]
        held, (sems, *rest) = refs[-n - 1 - len(scratch) :][:n], refs[-1 - len(scratch) :]
        copies = [pltpu.make_async_copy(hbm_refs[i], held[i], sems.at[i]) for i in range(n)]
        for copy in copies:
            copy.start()
        for copy in copies[: n - late]:
            copy.wait()
        extra = (copies[n - late :],) if late else ()
        kernel(*lead_refs, *held, *out_refs, *rest, *extra)

    buffers = [pltpu.VMEM(a.shape, a.dtype) for a in arrays]
    scratch_shapes = buffers + [pltpu.SemaphoreType.DMA((n,))] + list(scratch)
    specs = [SMEM] * len(scalars) + [VMEM] * len(resident) + [HBM] * n
    return call(body, out, specs, scratch_shapes, mib, cost)(*scalars, *resident, *arrays)


ATM_SCRATCH = (
    pltpu.VMEM((LEVELS, 4, 4, 16, 256), BF16),
    pltpu.VMEM((LEVELS, 4, 4, 16, 128), F32),
    pltpu.VMEM((LEVELS, 4, 4, 16, 128), F32),
    pltpu.VMEM((LEVELS, 4, 16, 256), BF16),
    pltpu.VMEM((LEVELS, 4, 16, 384), F32),
    pltpu.VMEM((16, 128), F32),
    pltpu.VMEM((4, 4, 16, 128), F32),
    pltpu.VMEM((4, 16, 128), F32),
    pltpu.VMEM((NFLUX, 4, 8, 128), F32),
    pltpu.VMEM((4, 32, 128), F32),
    pltpu.SemaphoreType.DMA,
)


def per_device(
    atm_state,
    level_winds,
    physics_flags,
    flux_matrix,
    regrid_source,
    regrid_weights,
    return_weights,
    ocean_state,
    ocean_neighbors,
    edge_weights,
    ocean_coupling,
):
    S = jax.ShapeDtypeStruct
    t, c = lax.axis_index("tile"), lax.axis_index("comp")
    par = jnp.stack([t % 2, c % 2, c, t]).astype(I32)
    atm = atm_state.reshape(64, 32, 128)
    ocean = ocean_state.reshape(64, 1024)
    scal = jnp.concatenate(
        [level_winds.reshape(-1), flux_matrix.reshape(-1), ocean_coupling.reshape(-1)]
    )
    rhs = jnp.asarray(lane_matrices())
    vec = jnp.asarray(lane_vectors())

    xp_a, xp_b, flags = staged(
        x_pack_kernel,
        (S((X_PLANES, 16, 128), BF16),) * 2 + (S((32, 128), F32),),
        (par,),
        (),
        (atm, physics_flags, ocean, ocean_neighbors, edge_weights),
        mib=12,
    )
    xa, xb = exchange((xp_a, xp_b), "tile", N_TILE)
    wanted, tcol = call(slots_kernel, (S((512, 128), BF16), S((512, 128), I32)), [VMEM])(
        regrid_source
    )
    wanted, tcol, xb = lax.optimization_barrier((wanted, tcol, xb))
    served = to_tiles(wanted)
    y_payload = call(
        y_pack_kernel,
        (S((Y_ROWS, 128), BF16),) * 2,
        [SMEM] + [VMEM] * 6,
        [pltpu.VMEM((33, 16, 1024), BF16), pltpu.VMEM((8, 64, 128), F32)],
    )(par, atm, flags, xa, xb, xp_a, xp_b)
    ya, yb = exchange(y_payload, "comp", N_COMP)
    first, flag = call(
        prepare_kernel,
        (S((LEVELS, 4, 4, 16, 256), BF16), S((4, 16, 128), F32)),
        [SMEM] + [VMEM] * 4,
        [pltpu.VMEM((8, 64, 128), F32)],
        cost=pl.CostEstimate(flops=2**23, bytes_accessed=2**23, transcendentals=0),
    )(par, atm, flags, xa, xb)
    atm_final, table = staged(
        atm_kernel,
        (S((64, 32, 128), F32), S((128, 128), BF16)),
        (par, scal),
        (first, flag, ya, yb),
        (vec, rhs),
        ATM_SCRATCH,
        late=1,
        mib=32,
        cost=pl.CostEstimate(flops=2**33, bytes_accessed=2**26, transcendentals=0),
    )
    rows = call(pick_kernel, S((512, 128), BF16), [VMEM] * 2)(served, table)
    mean_rows = to_tiles(rows)
    forcing, *edges = call(
        forcing_kernel,
        (S((8, 1024), F32), S((8, 128), F32), S((8, 128), F32)),
        [SMEM] + [VMEM] * 3,
    )(par, mean_rows, tcol, regrid_weights.reshape(8, 1024, 128))
    ea, eb = exchange(edges, ("tile", "comp"), N_TILE * N_COMP)
    n2, ends, sw, parts, table = call(
        ocean_kernel,
        (
            S((64, 1024), F32),
            S((2, 384, 128), BF16),
            S((8, 1024), F32),
            S((512, 128), F32),
            S((512, 512), BF16),
        ),
        [SMEM] + [VMEM] * 8,
        [pltpu.VMEM((10, 64, 128), F32), pltpu.VMEM((8, 384, 128), BF16)],
        cost=pl.CostEstimate(flops=2**27, bytes_accessed=2**24, transcendentals=0),
    )(par, ocean, ocean_neighbors, edge_weights, ya, yb, forcing, return_weights, tcol)
    ocean_final, sent = call(
        return_kernel,
        (S((64, 1024), F32), S((512, 128), BF16)),
        [SMEM] + [VMEM] * 10,
        [pltpu.VMEM((512, 128), F32)],
    )(par, n2, ends, sw, forcing, ea, eb, parts, table, return_weights[0], return_weights[7])
    incoming = to_tiles(sent)
    ocean_on_atm = call(collect_kernel, S((4, 32, 128), F32), [VMEM] * 2)(served, incoming)
    return (
        atm_final.reshape(atm_state.shape),
        ocean_final.reshape(ocean_state.shape),
        ocean_on_atm,
    )


def solution(mesh):
    return jax.shard_map(
        per_device,
        mesh=mesh,
        in_specs=(
            P(None, None, "tile", "comp"),
            P(),
            P("tile", "comp"),
            P(),
            P(("tile", "comp"), None),
            P(("tile", "comp"), None, None, None),
            P(("tile", "comp"), None, None, None),
            P(None, None, ("tile", "comp")),
            P(None, ("tile", "comp")),
            P(None, ("tile", "comp")),
            P(),
        ),
        out_specs=(
            P(None, None, "tile", "comp"),
            P(None, None, ("tile", "comp")),
            P(None, "tile", "comp"),
        ),
        check_vma=False,
    )
```

```python
import functools

import jax
import jax.numpy as jnp
import ml_dtypes
import numpy as np
from jax import lax
from jax.experimental import pallas as pl
from jax.experimental.pallas import tpu as pltpu
from jax.sharding import PartitionSpec as P

F32 = jnp.float32
BF16 = jnp.bfloat16
I32 = jnp.int32
N_TILE, N_COMP = 32, 4
STEPS = 4
LEVELS = 16
NFLUX = 12
DT = 0.02
VMEM = pl.BlockSpec(memory_space=pltpu.VMEM)
HBM = pl.BlockSpec(memory_space=pltpu.HBM)
SMEM = pl.BlockSpec(memory_space=pltpu.SMEM)
X_PLANES = 74
Y_ROWS = 672


def gll_derivative():
    points = np.array([-1.0, -1.0 / np.sqrt(5.0), 1.0 / np.sqrt(5.0), 1.0])
    products = np.array(
        [np.prod([points[r] - points[s] for s in range(4) if s != r]) for r in range(4)]
    )
    table = np.zeros((4, 4))
    for r in range(4):
        for s in range(4):
            if r != s:
                table[r, s] = products[r] / (products[s] * (points[r] - points[s]))
    table[0, 0], table[3, 3] = -3.0, 3.0
    return 2.0 * table


DERIV = gll_derivative()
ROW_SCALE = np.array([1.375, 1.125, 1.125, 1.375])


SCALED = (DERIV * ROW_SCALE[:, None]).astype(ml_dtypes.bfloat16).astype(np.float64)


def y_nodes():
    lane = np.arange(32)
    return np.where(lane < 16, 143 - lane, 15 - lane)


def lane_operators(nodes):
    count = len(nodes)
    deriv, average = np.zeros((count, count)), np.eye(count)
    where = {int(y): p for p, y in enumerate(nodes)}
    for y, p in where.items():
        for j in range(4):
            deriv[p, where[y - y % 4 + j]] = SCALED[y % 4, j]
        other = y - 1 if y % 4 == 0 else y + 1
        if y % 4 in (0, 3) and other in where:
            average[p, p] = average[p, where[other]] = 0.5
    return deriv, average


def twice(*matrices):
    both = np.concatenate([m.T for m in matrices], axis=1)
    return np.concatenate([both, both], axis=0)


def lane_matrices():
    eye = np.eye(128)
    deriv, average = lane_operators(np.arange(128))
    main = np.stack([twice(deriv, eye), twice(deriv @ average, average)])
    halo_deriv, halo_average = lane_operators(y_nodes())
    dy, av = np.kron(np.eye(4), halo_deriv), np.kron(np.eye(4), halo_average)
    dx = np.kron(SCALED, np.eye(32))
    halo = np.stack([twice(dx, dy, eye), twice(dx @ av, dy @ av, av)])
    return np.concatenate([main, halo], axis=2).astype(ml_dtypes.bfloat16)


def lane_vectors():
    vec = np.zeros((16, 128), np.float32)
    lane = np.arange(128)
    halo = np.tile(y_nodes(), 4)
    vec[0] = 1.0 / ROW_SCALE[lane % 4]
    vec[1] = 1.0 / ROW_SCALE[halo % 4]
    vec[2] = 1.0 / ROW_SCALE[lane // 32]
    for c in range(N_COMP):
        for row, y in ((4 + c, lane), (8 + c, halo)):
            vec[row] = DT * 0.5 * np.sin(2.0 * np.pi * (c * 128 + y + 0.5) / (128 * N_COMP))
    return vec


def split_bf16(x):
    hi = x.astype(BF16)
    return hi, (x - hi.astype(F32)).astype(BF16)


def iota(shape, dim):
    return lax.broadcasted_iota(I32, shape, dim)


def mm(a, b):
    return jnp.dot(a, b, preferred_element_type=F32)


def mm_t(a, b):
    return lax.dot_general(a, b, (((0,), (0,)), ((), ())), preferred_element_type=F32)


def slots_kernel(src_ref, wanted_ref, tcol_ref):
    s = src_ref[...] >> 2
    tile = (s >> 5).astype(F32)
    row = (s & 31).astype(F32)
    r0, a0 = iota((64, 8), 0), iota((64, 8), 1)
    pick_row = ((r0 >> 3) == a0).astype(F32)
    own = (r0 & 7) == a0
    tile_c = jnp.sum(jnp.where(own, mm(pick_row, tile), 0.0), axis=1, keepdims=True)
    b1, r1 = iota((8, 64), 0), iota((8, 64), 1)
    pick_col = (b1 == (r1 & 7)).astype(F32)
    own_t = b1 == (r1 >> 3)
    tile_r = jnp.sum(jnp.where(own_t, mm(tile, pick_col), 0.0), axis=0, keepdims=True)
    row_r = jnp.sum(jnp.where(own_t, mm(row, pick_col), 0.0), axis=0, keepdims=True)
    same = jnp.where(tile_c == tile_r, 1.0, 0.0)
    sub, lane = iota((64, 64), 0), iota((64, 64), 1)
    rank_c = jnp.sum(jnp.where(lane < sub, same, 0.0), axis=1, keepdims=True)
    rank_r = jnp.sum(jnp.where(sub < lane, same, 0.0), axis=0, keepdims=True)
    slot_c = (tile_c * 4.0 + rank_c).astype(I32)
    slot_r = (tile_r * 4.0 + rank_r).astype(I32)
    slot_wide = jnp.broadcast_to(slot_c, (64, 128))
    field = iota((64, 8, 128), 1)
    tcol = jnp.where(field < 4, slot_wide[:, None, :] * 4 + field, -1)
    tcol_ref[...] = tcol.reshape(512, 128)
    q = iota((512, 64), 0)
    val = jnp.sum(jnp.where((q >> 2) == slot_r, row_r + 1.0, 0.0), axis=1, keepdims=True) - 1.0
    f = (iota((512, 1), 0) & 3).astype(F32)
    target = jnp.where(val >= 0.0, f * 32.0 + val, -1.0)
    wanted_ref[...] = jnp.broadcast_to(target, (512, 128)).astype(BF16)


def one_hot(rows, target):
    return jnp.where(iota((rows, 256), 0) == target, 1.0, 0.0).astype(BF16)


def pack_matrix():
    col = iota((1, 256), 1)
    lane = col & 127
    plane = ((lane >> 4) & 1) * 4 + (lane >> 5)
    return one_hot(1024, plane * 128 + (lane & 15) + jnp.where(col < 128, 0, 112))


def unpack_matrix():
    col = iota((1, 256), 1)
    quarter, n = (col & 127) >> 5, col & 31
    base = 32 * quarter + 16 * (col >> 7)
    return one_hot(256, base + jnp.where(n < 16, 15 - n, 159 - n))


def x_pack_kernel(
    par_ref, atm_ref, flags_ref, ocean_ref, off_ref, w_ref, a_ref, b_ref, flags_out_ref
):
    even = par_ref[0] == 0

    def put(index, right, left):
        a_ref[index] = jnp.where(even, right, left).astype(BF16)
        b_ref[index] = jnp.where(even, left, right).astype(BF16)

    put(slice(0, 64), atm_ref[:, 16:32, :], atm_ref[:, 0:16, :])
    flags = flags_ref[...].astype(F32)
    flags_out_ref[...] = flags
    put(64, flags[16:32], flags[0:16])
    for part in range(2):
        right, left = [
            ocean_ref[:, c + 128 * part : c + 128 * part + 128].reshape(4, 16, 128) for c in (768, 0)
        ]
        put(slice(65 + 4 * part, 69 + 4 * part), right, left)
    off = off_ref[...].astype(F32)
    pad = jnp.zeros((2, 128), F32)
    right, left = [
        jnp.concatenate([off[:, c : c + 128], pad, w_ref[:, c : c + 128], pad], axis=0)
        for c in (896, 0)
    ]
    put(73, right, left)


def x_extended(ts_ref, slot, main, xa_ref, xb_ref, p, even):
    a, b = xa_ref[p].astype(F32), xb_ref[p].astype(F32)
    ts_ref[slot, 0:32] = main
    ts_ref[slot, 32:48] = jnp.where(even, a, b)
    ts_ref[slot, 48:64] = jnp.where(even, b, a)
    return [ts_ref[slot, pl.ds(i, 16, stride=4), :] for i in range(4)]


def y_pack_kernel(
    par_ref, atm_ref, flags_ref, xa_ref, xb_ref, pa_ref, pb_ref, a_ref, b_ref, lhs_ref, ts_ref
):
    even_t, even_c = par_ref[0] == 0, par_ref[1] == 0
    comp = par_ref[2]

    def group(q, _):
        for s in range(8):
            p = q * 8 + s
            rows = x_extended(ts_ref, s, atm_ref[p], xa_ref, xb_ref, p, even_t)
            for i in range(4):
                lanes = slice(((s % 2) * 4 + i) * 128, ((s % 2) * 4 + i) * 128 + 128)
                lhs_ref[q * 4 + s // 2, :, lanes] = rows[i].astype(BF16)
        return 0

    lax.fori_loop(0, 8, group, 0)
    rows = x_extended(ts_ref, 0, flags_ref[...], xa_ref, xb_ref, 64, even_t)
    for i in range(4):
        lhs_ref[32, :, 128 * i : 128 * i + 128] = rows[i].astype(BF16)
    lhs_ref[32, :, 512:1024] = jnp.zeros((16, 512), BF16)
    moved = mm(lhs_ref[...].reshape(528, 1024), pack_matrix())
    left, right = moved[:, 0:128], moved[:, 128:256]
    a_ref[0:528] = jnp.where(even_c, right, left).astype(BF16)
    b_ref[0:528] = jnp.where(even_c, left, right).astype(BF16)
    for n in range(9):
        p = 65 + n
        dest = slice(528 + 16 * n, 544 + 16 * n)
        a, b = xa_ref[p].astype(F32), xb_ref[p].astype(F32)
        own_a, own_b = pa_ref[p].astype(F32), pb_ref[p].astype(F32)
        from_left, from_right = jnp.where(even_t, b, a), jnp.where(even_t, a, b)
        own_right, own_left = jnp.where(even_t, own_a, own_b), jnp.where(even_t, own_b, own_a)
        right = jnp.where(comp == N_COMP - 1, from_left, own_right)
        left = jnp.where(comp == 0, from_right, own_left)
        a_ref[dest] = jnp.where(even_c, right, left).astype(BF16)
        b_ref[dest] = jnp.where(even_c, left, right).astype(BF16)


def prepare_kernel(par_ref, atm_ref, flags_ref, xa_ref, xb_ref, cb_ref, flag_ref, ts_ref):
    even_t = par_ref[0] == 0

    def group(q, _):
        for s in range(8):
            p = q * 8 + s
            rows = x_extended(ts_ref, s, atm_ref[p], xa_ref, xb_ref, p, even_t)
            for i in range(4):
                hi, lo = split_bf16(rows[i])
                cb_ref[(q % 2) * 8 + s, q // 2, i, :, 0:128] = hi
                cb_ref[(q % 2) * 8 + s, q // 2, i, :, 128:256] = lo
        return 0

    lax.fori_loop(0, 8, group, 0)
    rows = x_extended(ts_ref, 0, flags_ref[...], xa_ref, xb_ref, 64, even_t)
    for i in range(4):
        flag_ref[i] = rows[i]


def x_slopes(a):
    sums, diffs = (a[0] + a[3], a[1] + a[2]), (a[0] - a[3], a[1] - a[2])
    across = sums[0] - sums[1]
    out = [None] * 4
    for i in range(2):
        d = DERIV[i]
        odd = float((d[0] - d[3]) / 2) * diffs[0] + float((d[1] - d[2]) / 2) * diffs[1]
        even = float((d[0] + d[3]) / 2) * across
        out[i], out[3 - i] = odd + even, odd - even
    return out


def atm_kernel(
    par_ref,
    scal_ref,
    first_ref,
    flag_ref,
    ya_ref,
    yb_ref,
    vec_ref,
    rhs_ref,
    out_ref,
    table_ref,
    cb_ref,
    abuf_ref,
    dbuf_ref,
    hcb_ref,
    hbuf_ref,
    tm_ref,
    mask_ref,
    r5_ref,
    facc_ref,
    gs_ref,
    first_sem,
    copies,
):
    first_copy = pltpu.make_async_copy(first_ref, cb_ref, first_sem)
    first_copy.start()
    even_c = par_ref[1] == 0
    comp = par_ref[2]
    lane = iota((16, 128), 1)
    edge = (lane == 0) | (lane == 127)
    quarter = lane >> 5
    halo_edge = ((lane & 31) == 15) | ((lane & 31) == 16)

    def put(ref, index, value):
        hi, lo = split_bf16(value)
        ref[(*index, slice(None), slice(0, 128))] = hi
        ref[(*index, slice(None), slice(128, 256))] = lo

    ya, yb = ya_ref[0:528].astype(F32), yb_ref[0:528].astype(F32)
    from_right, from_left = jnp.where(even_c, ya, yb), jnp.where(even_c, yb, ya)
    arrived = jnp.concatenate([from_right, from_left], axis=1).astype(BF16)
    halo = mm(arrived, unpack_matrix()).astype(BF16)
    for k in range(4):
        for l in range(LEVELS):
            rows = slice((k * 8 + l // 2) * 16, (k * 8 + l // 2) * 16 + 16)
            lanes = slice((l % 2) * 128, (l % 2) * 128 + 128)
            hcb_ref[l, k, :, 0:128] = halo[rows, lanes]
            hcb_ref[l, k, :, 128:256] = jnp.zeros((16, 128), BF16)
    halo_flag = halo[512:528, 0:128].astype(F32)
    halo_r5 = jnp.where(halo_flag == 1.0, 5.0 * DT, 0.0)
    halo_m5 = jnp.where(halo_flag == 2.0, 5.0 * DT, 0.0)
    halo_keep = 1.0 - 2.0 * halo_m5
    halo_keep_t = halo_keep - halo_r5
    for i in range(4):
        flag = flag_ref[i]
        m5 = jnp.where(flag == 2.0, 5.0 * DT, 0.0)
        r5_ref[i] = jnp.where(flag == 1.0, 5.0 * DT, 0.0)
        mask_ref[0, i] = m5
        mask_ref[1, i] = 1.0 - 2.0 * m5
        mask_ref[2, i] = 1.0 - 2.0 * m5 - r5_ref[i]
    facc_ref[...] = jnp.zeros_like(facc_ref)
    dt_y = -DT * vec_ref[0:1, :]
    halo_dt_y = -DT * vec_ref[1:2, :]
    halo_dt_x = -DT * vec_ref[2:3, :]
    ff = vec_ref[pl.ds(4 + comp, 1), :]
    halo_ff = vec_ref[pl.ds(8 + comp, 1), :]
    for copy in (first_copy, *copies):
        copy.wait()

    def step(si, _):
        which = jnp.minimum(si, 1)
        both = mm(cb_ref[...].reshape(4096, 256), rhs_ref[which, :, 0:256])
        dbuf_ref[...] = both[:, 0:128].reshape(LEVELS, 4, 4, 16, 128)
        abuf_ref[...] = both[:, 128:256].reshape(LEVELS, 4, 4, 16, 128)
        hbuf_ref[...] = mm(hcb_ref[...].reshape(1024, 256), rhs_ref[which, :, 256:640]).reshape(
            LEVELS, 4, 16, 384
        )
        for i in range(4):
            total = abuf_ref[0, 2, i]
            for l in range(1, LEVELS):
                total = total + abuf_ref[l, 2, i]
            mask_ref[3, i] = r5_ref[i] * (total * (1.0 / LEVELS))
        total = hbuf_ref[0, 2, :, 256:384]
        for l in range(1, LEVELS):
            total = total + hbuf_ref[l, 2, :, 256:384]
        tm_ref[...] = halo_r5 * (total * (1.0 / LEVELS))

        def level(l, _):
            above, below = jnp.minimum(l + 1, LEVELS - 1), jnp.maximum(l - 1, 0)
            wind_x, wind_y = scal_ref[l], scal_ref[LEVELS + l]
            cx = -DT * wind_x
            cy = dt_y * wind_y
            a = [[abuf_ref[l, k, i] for i in range(4)] for k in range(4)]

            slopes = [x_slopes(a[k]) for k in range(4)]
            new = [[None] * 4 for _ in range(4)]
            for i in range(4):
                m5, keep, keep_t, relax = [mask_ref[n, i] for n in range(4)]
                d = [slopes[k][i] for k in range(4)]
                dy = [dbuf_ref[l, k, i] for k in range(4)]
                extra = [
                    ff * a[1][i] - DT * d[3],
                    dt_y * dy[3] - ff * a[0][i],
                    relax,
                    dt_y * dy[1] - DT * d[0],
                ]
                for k in range(4):
                    mix = m5 * (abuf_ref[above, k, i] + abuf_ref[below, k, i])
                    own = (keep_t if k == 2 else keep) * a[k][i]
                    new[k][i] = (own + mix) + ((cx * d[k] + cy * dy[k]) + extra[k])

            halo_cx, halo_cy = halo_dt_x * wind_x, halo_dt_y * wind_y
            hx, hy, ha = [
                [hbuf_ref[l, k, :, 128 * n : 128 * n + 128] for k in range(4)] for n in range(3)
            ]
            extra = [
                halo_ff * ha[1] + halo_dt_x * hx[3],
                halo_dt_y * hy[3] - halo_ff * ha[0],
                tm_ref[...],
                halo_dt_y * hy[1] + halo_dt_x * hx[0],
            ]
            for k in range(4):
                first = 0.5 * (new[k][0] + pltpu.roll(new[k][3], 1, 0))
                values = [first, new[k][1], new[k][2], pltpu.roll(first, 15, 0)]
                up, down = hbuf_ref[above, k, :, 256:384], hbuf_ref[below, k, :, 256:384]
                own = (halo_keep_t if k == 2 else halo_keep) * ha[k] + halo_m5 * (up + down)
                own = own + ((halo_cx * hx[k] + halo_cy * hy[k]) + extra[k])
                lower = pltpu.roll(pltpu.roll(own, 32, 1), 1, 0)
                upper = pltpu.roll(pltpu.roll(own, 96, 1), 15, 0)
                partner = jnp.where(quarter == 0, lower, jnp.where(quarter == 3, upper, own))
                own = 0.5 * (own + partner)
                across = None
                for i in range(4):
                    moved = pltpu.roll(values[i], 32 * i + 16, 1)
                    across = moved if i == 0 else jnp.where(quarter == i, moved, across)
                    back = pltpu.roll(own, 112 - 32 * i, 1)
                    put(cb_ref, (l, k, i), jnp.where(edge, 0.5 * (values[i] + back), values[i]))
                put(hcb_ref, (l, k), jnp.where(halo_edge, 0.5 * (own + across), own))
            return 0

        lax.fori_loop(0, LEVELS, level, 0, unroll=2)
        surface = mm(cb_ref[0].reshape(256, 256), rhs_ref[1, :, 128:256]).reshape(4, 4, 16, 128)
        for i in range(4):
            u, v, t, z = [surface[k, i, 0:8] for k in range(4)]
            speed = jnp.sqrt(u * u + v * v + 1.0)
            for c in range(NFLUX):
                m0, m1, m2, m3 = [scal_ref[32 + 4 * c + k] for k in range(4)]
                m = (m0 * u + m1 * v) + (m2 * t + m3 * z)
                facc_ref[c, i] += speed * m * lax.rsqrt(1.0 + 0.5 * (m * m))
        return 0

    lax.fori_loop(0, STEPS, step, 0)
    final = mm(cb_ref[...].reshape(4096, 256), rhs_ref[1, :, 128:256]).reshape(LEVELS, 4, 4, 16, 128)
    for l in range(LEVELS):
        for k in range(4):
            for i in range(4):
                out_ref[k * LEVELS + l, pl.ds(i, 8, stride=4), :] = final[l, k, i, 0:8]
    for i in range(4):
        mean = [(facc_ref[c, i] * (1.0 / STEPS)).astype(BF16).astype(F32) for c in range(NFLUX)]
        for g in range(4):
            total = scal_ref[80 + 12 * g] * mean[0]
            for c in range(1, NFLUX):
                total = total + scal_ref[80 + 12 * g + c] * mean[c]
            gs_ref[g, pl.ds(i, 8, stride=4), :] = 0.25 * total
    table_ref[...] = gs_ref[...].reshape(128, 128).astype(BF16)


def pick_kernel(served_ref, table_ref, rows_ref):
    pick = served_ref[...].astype(F32) == iota((512, 128), 1).astype(F32)
    rows_ref[...] = mm(jnp.where(pick, 1.0, 0.0).astype(BF16), table_ref[...]).astype(BF16)


def request_matrix(tcol_ref):
    parts = []
    for chunk in range(4):
        hit = tcol_ref[...] == iota((512, 128), 1) + 128 * chunk
        parts.append(jnp.where(hit, 1.0, 0.0).astype(BF16))
    return jnp.concatenate(parts, axis=1)


def force_block(window, wm, sw, n2_ref, ocean_ref, b):
    cells = slice(128 * b, 128 * b + 128)
    hi, lo = split_bf16(window)
    own = window[:, 128:256]
    both = mm(jnp.concatenate([hi.astype(F32), lo.astype(F32)], axis=0).astype(BF16), wm)
    top = both[0:8] + both[8:16] + (1.8 - sw) * own
    surface = []
    for k in range(4):
        value = n2_ref[16 * k : 16 * k + 1, cells] + top[k : k + 1]
        if k == 2:
            value = value + 0.2 * own[3:4]
        if k == 3:
            value = value - 0.2 * own[2:3]
        below = n2_ref[16 * k + 1 : 16 * k + 2, cells] + 0.2 * own[k : k + 1]
        ocean_ref[16 * k : 16 * k + 1, cells] = value
        ocean_ref[16 * k + 1 : 16 * k + 2, cells] = below
        surface.append(value)
    return jnp.concatenate(surface + [jnp.zeros((4, 128), F32)], axis=0).astype(BF16)


def return_parts(surface, weights, parts_ref, b):
    parts = mm(surface, jnp.concatenate([weights[k] for k in range(8)], axis=1))
    for k in range(8):
        rows = slice((b * 8 + k) * 8, (b * 8 + k) * 8 + 8)
        parts_ref[rows, :] = parts[:, 128 * k : 128 * k + 128]


def ocean_kernel(
    par_ref,
    ocean_ref,
    off_ref,
    w_ref,
    ya_ref,
    yb_ref,
    f_ref,
    weights_ref,
    tcol_ref,
    n2_ref,
    ends_ref,
    sw_ref,
    parts_ref,
    table_ref,
    o1_ref,
    wm_ref,
):
    even_c = par_ref[1] == 0

    def halo_rows(n):
        rows = slice(528 + 16 * n, 544 + 16 * n)
        a, b = ya_ref[rows].astype(F32), yb_ref[rows].astype(F32)
        return jnp.where(even_c, b, a), jnp.where(even_c, a, b)

    pieces = [halo_rows(n) for n in range(9)]
    left = [jnp.concatenate([p[0] for p in pieces[4 * n : 4 * n + 4]], axis=0) for n in range(2)]
    right = [jnp.concatenate([p[1] for p in pieces[4 * n : 4 * n + 4]], axis=0) for n in range(2)]
    values = {-2: left[0], -1: left[1], 8: right[0], 9: right[1]}
    for b in range(8):
        values[b] = ocean_ref[:, 128 * b : 128 * b + 128]
    offw = {-1: pieces[8][0], 8: pieces[8][1]}
    source = iota((384, 128), 0)
    lane = iota((1, 128), 1)
    level = iota((64, 128), 0) & 15

    def matrix(b):
        if b in offw:
            off, w = offw[b][0:6].astype(I32), offw[b][8:14]
        else:
            cells = slice(128 * b, 128 * b + 128)
            off, w = off_ref[:, cells], w_ref[:, cells].astype(BF16).astype(F32)
        total = jnp.zeros((384, 128), F32)
        for j in range(6):
            total = total + jnp.where(source == lane + off[j : j + 1], w[j : j + 1], 0.0)
        return total.astype(BF16), jnp.sum(w, axis=0, keepdims=True)

    def update(own, window, wm, sw):
        hi, lo = split_bf16(window)
        both = mm(jnp.concatenate([hi, lo], axis=0), wm)
        lateral = both[0:64] + both[64:128] - sw * own
        above = jnp.where(level == 15, own, pltpu.roll(own, 63, 0))
        below = jnp.where(level == 0, own, pltpu.roll(own, 1, 0))
        rot = jnp.concatenate([jnp.zeros((32, 128), F32), 0.2 * own[48:64], -0.2 * own[32:48]], axis=0)
        return own + lateral + 0.2 * (above - 2.0 * own + below) + rot

    for b in range(-1, 9):
        wm, sw = matrix(b)
        if 0 <= b < 8:
            wm_ref[b] = wm
            sw_ref[:, 128 * b : 128 * b + 128] = jnp.broadcast_to(sw, (8, 128))
        window = jnp.concatenate([values[b - 1], values[b], values[b + 1]], axis=1)
        o1_ref[b + 1] = update(values[b], window, wm, sw)
    for b in range(8):
        window = jnp.concatenate([o1_ref[b], o1_ref[b + 1], o1_ref[b + 2]], axis=1)
        cells = slice(128 * b, 128 * b + 128)
        n2_ref[:, cells] = update(o1_ref[b + 1], window, wm_ref[b], sw_ref[0:1, cells])
    for b in range(1, 7):
        cells = slice(128 * b, 128 * b + 128)
        window = f_ref[:, 128 * b - 128 : 128 * b + 256]
        surface = force_block(window, wm_ref[b], sw_ref[:, cells], n2_ref, n2_ref, b)
        return_parts(surface, weights_ref[b], parts_ref, b)
    ends_ref[0] = wm_ref[0]
    ends_ref[1] = wm_ref[7]
    for b in (0, 7):
        parts_ref[64 * b : 64 * b + 64, :] = jnp.zeros((64, 128), F32)
    table_ref[...] = request_matrix(tcol_ref)


def forcing_kernel(par_ref, rows_ref, tcol_ref, weights_ref, f_ref, a_ref, b_ref):
    even_c = par_ref[1] == 0
    gathered = mm(request_matrix(tcol_ref), rows_ref[...])
    for b in range(8):
        lhs = jnp.concatenate(
            [gathered[(b * 8 + k) * 8 : (b * 8 + k) * 8 + 8] for k in range(8)], axis=1
        ).astype(BF16)
        f_ref[:, 128 * b : 128 * b + 128] = mm(lhs, weights_ref[b])
    right, left = f_ref[:, 896:1024], f_ref[:, 0:128]
    a_ref[...] = jnp.where(even_c, right, left)
    b_ref[...] = jnp.where(even_c, left, right)


def return_kernel(
    par_ref,
    n2_ref,
    ends_ref,
    sw_ref,
    f_ref,
    ea_ref,
    eb_ref,
    inner_ref,
    table_ref,
    first_ref,
    last_ref,
    ocean_ref,
    sent_ref,
    parts_ref,
):
    even_c = par_ref[1] == 0
    ea, eb = ea_ref[...], eb_ref[...]
    ocean_ref[...] = n2_ref[...]
    parts_ref[...] = inner_ref[...]
    window = jnp.concatenate([jnp.where(even_c, eb, ea), f_ref[:, 0:256]], axis=1)
    surface = force_block(window, ends_ref[0], sw_ref[:, 0:128], n2_ref, ocean_ref, 0)
    return_parts(surface, first_ref, parts_ref, 0)
    window = jnp.concatenate([f_ref[:, 768:1024], jnp.where(even_c, ea, eb)], axis=1)
    surface = force_block(window, ends_ref[1], sw_ref[:, 896:1024], n2_ref, ocean_ref, 7)
    return_parts(surface, last_ref, parts_ref, 7)
    sent_ref[...] = mm_t(table_ref[...], parts_ref[...].astype(BF16)).astype(BF16)


def collect_kernel(served_ref, incoming_ref, out_ref):
    pick = served_ref[...].astype(F32) == iota((512, 128), 1).astype(F32)
    owner = jnp.where(pick, 1.0, 0.0).astype(BF16)
    out_ref[...] = mm_t(owner, incoming_ref[...]).reshape(4, 32, 128)


def swap_pairs(n):
    near = [(i, i ^ 1) for i in range(n)]
    far = [(i, (i + 1) % n if i % 2 else (i - 1) % n) for i in range(n)]
    return near, far


def exchange(payloads, axis, n):
    near, far = swap_pairs(n)
    return lax.ppermute(payloads[0], axis, near), lax.ppermute(payloads[1], axis, far)


def to_tiles(rows):
    moved = lax.all_to_all(
        rows.reshape(N_TILE, 16, 128), "tile", split_axis=0, concat_axis=0, tiled=True
    )
    return moved.reshape(512, 128)


def call(kernel, out, specs, scratch=(), mib=16, cost=None):
    return pl.pallas_call(
        kernel,
        out_shape=out,
        in_specs=specs,
        out_specs=jax.tree.map(lambda _: VMEM, out),
        scratch_shapes=list(scratch),
        compiler_params=pltpu.CompilerParams(vmem_limit_bytes=mib * 2**20),
        cost_estimate=cost,
    )


def staged(kernel, out, scalars, resident, arrays, scratch=(), late=0, mib=16, cost=None):
    n_lead, n = len(scalars) + len(resident), len(arrays)
    n_out = len(jax.tree.leaves(out))

    def body(*refs):
        lead_refs, hbm_refs = refs[:n_lead], refs[n_lead : n_lead + n]
        out_refs = refs[n_lead + n : n_lead + n + n_out]
        held, (sems, *rest) = refs[-n - 1 - len(scratch) :][:n], refs[-1 - len(scratch) :]
        copies = [pltpu.make_async_copy(hbm_refs[i], held[i], sems.at[i]) for i in range(n)]
        for copy in copies:
            copy.start()
        for copy in copies[: n - late]:
            copy.wait()
        extra = (copies[n - late :],) if late else ()
        kernel(*lead_refs, *held, *out_refs, *rest, *extra)

    buffers = [pltpu.VMEM(a.shape, a.dtype) for a in arrays]
    scratch_shapes = buffers + [pltpu.SemaphoreType.DMA((n,))] + list(scratch)
    specs = [SMEM] * len(scalars) + [VMEM] * len(resident) + [HBM] * n
    return call(body, out, specs, scratch_shapes, mib, cost)(*scalars, *resident, *arrays)


ATM_SCRATCH = (
    pltpu.VMEM((LEVELS, 4, 4, 16, 256), BF16),
    pltpu.VMEM((LEVELS, 4, 4, 16, 128), F32),
    pltpu.VMEM((LEVELS, 4, 4, 16, 128), F32),
    pltpu.VMEM((LEVELS, 4, 16, 256), BF16),
    pltpu.VMEM((LEVELS, 4, 16, 384), F32),
    pltpu.VMEM((16, 128), F32),
    pltpu.VMEM((4, 4, 16, 128), F32),
    pltpu.VMEM((4, 16, 128), F32),
    pltpu.VMEM((NFLUX, 4, 8, 128), F32),
    pltpu.VMEM((4, 32, 128), F32),
    pltpu.SemaphoreType.DMA,
)


def per_device(
    atm_state,
    level_winds,
    physics_flags,
    flux_matrix,
    regrid_source,
    regrid_weights,
    return_weights,
    ocean_state,
    ocean_neighbors,
    edge_weights,
    ocean_coupling,
):
    S = jax.ShapeDtypeStruct
    t, c = lax.axis_index("tile"), lax.axis_index("comp")
    par = jnp.stack([t % 2, c % 2, c, t]).astype(I32)
    atm = atm_state.reshape(64, 32, 128)
    ocean = ocean_state.reshape(64, 1024)
    scal = jnp.concatenate(
        [level_winds.reshape(-1), flux_matrix.reshape(-1), ocean_coupling.reshape(-1)]
    )
    rhs = jnp.asarray(lane_matrices())
    vec = jnp.asarray(lane_vectors())

    xp_a, xp_b, flags = staged(
        x_pack_kernel,
        (S((X_PLANES, 16, 128), BF16),) * 2 + (S((32, 128), F32),),
        (par,),
        (),
        (atm, physics_flags, ocean, ocean_neighbors, edge_weights),
        mib=12,
    )
    xa, xb = exchange((xp_a, xp_b), "tile", N_TILE)
    wanted, tcol = call(slots_kernel, (S((512, 128), BF16), S((512, 128), I32)), [VMEM])(
        regrid_source
    )
    wanted, tcol, xb = lax.optimization_barrier((wanted, tcol, xb))
    served = to_tiles(wanted)
    y_payload = call(
        y_pack_kernel,
        (S((Y_ROWS, 128), BF16),) * 2,
        [SMEM] + [VMEM] * 6,
        [pltpu.VMEM((33, 16, 1024), BF16), pltpu.VMEM((8, 64, 128), F32)],
    )(par, atm, flags, xa, xb, xp_a, xp_b)
    ya, yb = exchange(y_payload, "comp", N_COMP)
    first, flag = call(
        prepare_kernel,
        (S((LEVELS, 4, 4, 16, 256), BF16), S((4, 16, 128), F32)),
        [SMEM] + [VMEM] * 4,
        [pltpu.VMEM((8, 64, 128), F32)],
        cost=pl.CostEstimate(flops=2**23, bytes_accessed=2**23, transcendentals=0),
    )(par, atm, flags, xa, xb)
    atm_final, table = staged(
        atm_kernel,
        (S((64, 32, 128), F32), S((128, 128), BF16)),
        (par, scal),
        (first, flag, ya, yb),
        (vec, rhs),
        ATM_SCRATCH,
        late=1,
        mib=32,
        cost=pl.CostEstimate(flops=2**33, bytes_accessed=2**26, transcendentals=0),
    )
    rows = call(pick_kernel, S((512, 128), BF16), [VMEM] * 2)(served, table)
    mean_rows = to_tiles(rows)
    mean_rows, return_weights = lax.optimization_barrier((mean_rows, return_weights))
    forcing, *edges = call(
        forcing_kernel,
        (S((8, 1024), F32), S((8, 128), F32), S((8, 128), F32)),
        [SMEM] + [VMEM] * 3,
    )(par, mean_rows, tcol, regrid_weights.reshape(8, 1024, 128))
    ea, eb = exchange(edges, ("tile", "comp"), N_TILE * N_COMP)
    n2, ends, sw, parts, table = call(
        ocean_kernel,
        (
            S((64, 1024), F32),
            S((2, 384, 128), BF16),
            S((8, 1024), F32),
            S((512, 128), F32),
            S((512, 512), BF16),
        ),
        [SMEM] + [VMEM] * 8,
        [pltpu.VMEM((10, 64, 128), F32), pltpu.VMEM((8, 384, 128), BF16)],
        cost=pl.CostEstimate(flops=2**27, bytes_accessed=2**24, transcendentals=0),
    )(par, ocean, ocean_neighbors, edge_weights, ya, yb, forcing, return_weights, tcol)
    ocean_final, sent = call(
        return_kernel,
        (S((64, 1024), F32), S((512, 128), BF16)),
        [SMEM] + [VMEM] * 10,
        [pltpu.VMEM((512, 128), F32)],
    )(par, n2, ends, sw, forcing, ea, eb, parts, table, return_weights[0], return_weights[7])
    incoming = to_tiles(sent)
    ocean_on_atm = call(collect_kernel, S((4, 32, 128), F32), [VMEM] * 2)(served, incoming)
    return (
        atm_final.reshape(atm_state.shape),
        ocean_final.reshape(ocean_state.shape),
        ocean_on_atm,
    )


def solution(mesh):
    return jax.shard_map(
        per_device,
        mesh=mesh,
        in_specs=(
            P(None, None, "tile", "comp"),
            P(),
            P("tile", "comp"),
            P(),
            P(("tile", "comp"), None),
            P(("tile", "comp"), None, None, None),
            P(("tile", "comp"), None, None, None),
            P(None, None, ("tile", "comp")),
            P(None, ("tile", "comp")),
            P(None, ("tile", "comp")),
            P(),
        ),
        out_specs=(
            P(None, None, "tile", "comp"),
            P(None, None, ("tile", "comp")),
            P(None, "tile", "comp"),
        ),
        check_vma=False,
    )
```

```python
import functools

import jax
import jax.numpy as jnp
import ml_dtypes
import numpy as np
from jax import lax
from jax.experimental import pallas as pl
from jax.experimental.pallas import tpu as pltpu
from jax.sharding import PartitionSpec as P

F32 = jnp.float32
BF16 = jnp.bfloat16
I32 = jnp.int32
N_TILE, N_COMP = 32, 4
STEPS = 4
LEVELS = 16
NFLUX = 12
DT = 0.02
VMEM = pl.BlockSpec(memory_space=pltpu.VMEM)
HBM = pl.BlockSpec(memory_space=pltpu.HBM)
SMEM = pl.BlockSpec(memory_space=pltpu.SMEM)
X_PLANES = 74
Y_ROWS = 672


def gll_derivative():
    points = np.array([-1.0, -1.0 / np.sqrt(5.0), 1.0 / np.sqrt(5.0), 1.0])
    products = np.array(
        [np.prod([points[r] - points[s] for s in range(4) if s != r]) for r in range(4)]
    )
    table = np.zeros((4, 4))
    for r in range(4):
        for s in range(4):
            if r != s:
                table[r, s] = products[r] / (products[s] * (points[r] - points[s]))
    table[0, 0], table[3, 3] = -3.0, 3.0
    return 2.0 * table


DERIV = gll_derivative()
ROW_SCALE = np.array([1.375, 1.125, 1.125, 1.375])


SCALED = (DERIV * ROW_SCALE[:, None]).astype(ml_dtypes.bfloat16).astype(np.float64)


def y_nodes():
    lane = np.arange(32)
    return np.where(lane < 16, 143 - lane, 15 - lane)


def lane_operators(nodes):
    count = len(nodes)
    deriv, average = np.zeros((count, count)), np.eye(count)
    where = {int(y): p for p, y in enumerate(nodes)}
    for y, p in where.items():
        for j in range(4):
            deriv[p, where[y - y % 4 + j]] = SCALED[y % 4, j]
        other = y - 1 if y % 4 == 0 else y + 1
        if y % 4 in (0, 3) and other in where:
            average[p, p] = average[p, where[other]] = 0.5
    return deriv, average


def twice(*matrices):
    both = np.concatenate([m.T for m in matrices], axis=1)
    return np.concatenate([both, both], axis=0)


def lane_matrices():
    eye = np.eye(128)
    deriv, average = lane_operators(np.arange(128))
    main = np.stack([twice(deriv, eye), twice(deriv @ average, average)])
    halo_deriv, halo_average = lane_operators(y_nodes())
    dy, av = np.kron(np.eye(4), halo_deriv), np.kron(np.eye(4), halo_average)
    dx = np.kron(SCALED, np.eye(32))
    halo = np.stack([twice(dx, dy, eye), twice(dx @ av, dy @ av, av)])
    return np.concatenate([main, halo], axis=2).astype(ml_dtypes.bfloat16)


def lane_vectors():
    vec = np.zeros((16, 128), np.float32)
    lane = np.arange(128)
    halo = np.tile(y_nodes(), 4)
    vec[0] = 1.0 / ROW_SCALE[lane % 4]
    vec[1] = 1.0 / ROW_SCALE[halo % 4]
    vec[2] = 1.0 / ROW_SCALE[lane // 32]
    for c in range(N_COMP):
        for row, y in ((4 + c, lane), (8 + c, halo)):
            vec[row] = DT * 0.5 * np.sin(2.0 * np.pi * (c * 128 + y + 0.5) / (128 * N_COMP))
    return vec


def split_bf16(x):
    hi = x.astype(BF16)
    return hi, (x - hi.astype(F32)).astype(BF16)


def iota(shape, dim):
    return lax.broadcasted_iota(I32, shape, dim)


def mm(a, b):
    return jnp.dot(a, b, preferred_element_type=F32)


def mm_t(a, b):
    return lax.dot_general(a, b, (((0,), (0,)), ((), ())), preferred_element_type=F32)


def slots_kernel(src_ref, wanted_ref, tcol_ref):
    s = src_ref[...] >> 2
    tile = (s >> 5).astype(F32)
    row = (s & 31).astype(F32)
    r0, a0 = iota((64, 8), 0), iota((64, 8), 1)
    pick_row = ((r0 >> 3) == a0).astype(F32)
    own = (r0 & 7) == a0
    tile_c = jnp.sum(jnp.where(own, mm(pick_row, tile), 0.0), axis=1, keepdims=True)
    b1, r1 = iota((8, 64), 0), iota((8, 64), 1)
    pick_col = (b1 == (r1 & 7)).astype(F32)
    own_t = b1 == (r1 >> 3)
    tile_r = jnp.sum(jnp.where(own_t, mm(tile, pick_col), 0.0), axis=0, keepdims=True)
    row_r = jnp.sum(jnp.where(own_t, mm(row, pick_col), 0.0), axis=0, keepdims=True)
    same = jnp.where(tile_c == tile_r, 1.0, 0.0)
    sub, lane = iota((64, 64), 0), iota((64, 64), 1)
    rank_c = jnp.sum(jnp.where(lane < sub, same, 0.0), axis=1, keepdims=True)
    rank_r = jnp.sum(jnp.where(sub < lane, same, 0.0), axis=0, keepdims=True)
    slot_c = (tile_c * 4.0 + rank_c).astype(I32)
    slot_r = (tile_r * 4.0 + rank_r).astype(I32)
    slot_wide = jnp.broadcast_to(slot_c, (64, 128))
    field = iota((64, 8, 128), 1)
    tcol = jnp.where(field < 4, slot_wide[:, None, :] * 4 + field, -1)
    tcol_ref[...] = tcol.reshape(512, 128)
    q = iota((512, 64), 0)
    val = jnp.sum(jnp.where((q >> 2) == slot_r, row_r + 1.0, 0.0), axis=1, keepdims=True) - 1.0
    f = (iota((512, 1), 0) & 3).astype(F32)
    target = jnp.where(val >= 0.0, f * 32.0 + val, -1.0)
    wanted_ref[...] = jnp.broadcast_to(target, (512, 128)).astype(BF16)


def one_hot(rows, target):
    return jnp.where(iota((rows, 256), 0) == target, 1.0, 0.0).astype(BF16)


def pack_matrix():
    col = iota((1, 256), 1)
    lane = col & 127
    plane = ((lane >> 4) & 1) * 4 + (lane >> 5)
    return one_hot(1024, plane * 128 + (lane & 15) + jnp.where(col < 128, 0, 112))


def unpack_matrix():
    col = iota((1, 256), 1)
    quarter, n = (col & 127) >> 5, col & 31
    base = 32 * quarter + 16 * (col >> 7)
    return one_hot(256, base + jnp.where(n < 16, 15 - n, 159 - n))


def x_pack_kernel(
    par_ref, atm_ref, flags_ref, ocean_ref, off_ref, w_ref, a_ref, b_ref, flags_out_ref
):
    even = par_ref[0] == 0

    def put(index, right, left):
        a_ref[index] = jnp.where(even, right, left).astype(BF16)
        b_ref[index] = jnp.where(even, left, right).astype(BF16)

    put(slice(0, 64), atm_ref[:, 16:32, :], atm_ref[:, 0:16, :])
    flags = flags_ref[...].astype(F32)
    flags_out_ref[...] = flags
    put(64, flags[16:32], flags[0:16])
    for part in range(2):
        right, left = [
            ocean_ref[:, c + 128 * part : c + 128 * part + 128].reshape(4, 16, 128) for c in (768, 0)
        ]
        put(slice(65 + 4 * part, 69 + 4 * part), right, left)
    off = off_ref[...].astype(F32)
    pad = jnp.zeros((2, 128), F32)
    right, left = [
        jnp.concatenate([off[:, c : c + 128], pad, w_ref[:, c : c + 128], pad], axis=0)
        for c in (896, 0)
    ]
    put(73, right, left)


def x_extended(ts_ref, slot, main, xa_ref, xb_ref, p, even):
    a, b = xa_ref[p].astype(F32), xb_ref[p].astype(F32)
    ts_ref[slot, 0:32] = main
    ts_ref[slot, 32:48] = jnp.where(even, a, b)
    ts_ref[slot, 48:64] = jnp.where(even, b, a)
    return [ts_ref[slot, pl.ds(i, 16, stride=4), :] for i in range(4)]


def y_pack_kernel(
    par_ref, atm_ref, flags_ref, xa_ref, xb_ref, pa_ref, pb_ref, a_ref, b_ref, lhs_ref, ts_ref
):
    even_t, even_c = par_ref[0] == 0, par_ref[1] == 0
    comp = par_ref[2]

    def group(q, _):
        for s in range(8):
            p = q * 8 + s
            rows = x_extended(ts_ref, s, atm_ref[p], xa_ref, xb_ref, p, even_t)
            for i in range(4):
                lanes = slice(((s % 2) * 4 + i) * 128, ((s % 2) * 4 + i) * 128 + 128)
                lhs_ref[q * 4 + s // 2, :, lanes] = rows[i].astype(BF16)
        return 0

    lax.fori_loop(0, 8, group, 0)
    rows = x_extended(ts_ref, 0, flags_ref[...], xa_ref, xb_ref, 64, even_t)
    for i in range(4):
        lhs_ref[32, :, 128 * i : 128 * i + 128] = rows[i].astype(BF16)
    lhs_ref[32, :, 512:1024] = jnp.zeros((16, 512), BF16)
    moved = mm(lhs_ref[...].reshape(528, 1024), pack_matrix())
    left, right = moved[:, 0:128], moved[:, 128:256]
    a_ref[0:528] = jnp.where(even_c, right, left).astype(BF16)
    b_ref[0:528] = jnp.where(even_c, left, right).astype(BF16)
    for n in range(9):
        p = 65 + n
        dest = slice(528 + 16 * n, 544 + 16 * n)
        a, b = xa_ref[p].astype(F32), xb_ref[p].astype(F32)
        own_a, own_b = pa_ref[p].astype(F32), pb_ref[p].astype(F32)
        from_left, from_right = jnp.where(even_t, b, a), jnp.where(even_t, a, b)
        own_right, own_left = jnp.where(even_t, own_a, own_b), jnp.where(even_t, own_b, own_a)
        right = jnp.where(comp == N_COMP - 1, from_left, own_right)
        left = jnp.where(comp == 0, from_right, own_left)
        a_ref[dest] = jnp.where(even_c, right, left).astype(BF16)
        b_ref[dest] = jnp.where(even_c, left, right).astype(BF16)


def prepare_kernel(par_ref, atm_ref, flags_ref, xa_ref, xb_ref, cb_ref, flag_ref, ts_ref):
    even_t = par_ref[0] == 0

    def group(q, _):
        for s in range(8):
            p = q * 8 + s
            rows = x_extended(ts_ref, s, atm_ref[p], xa_ref, xb_ref, p, even_t)
            for i in range(4):
                hi, lo = split_bf16(rows[i])
                cb_ref[(q % 2) * 8 + s, q // 2, i, :, 0:128] = hi
                cb_ref[(q % 2) * 8 + s, q // 2, i, :, 128:256] = lo
        return 0

    lax.fori_loop(0, 8, group, 0)
    rows = x_extended(ts_ref, 0, flags_ref[...], xa_ref, xb_ref, 64, even_t)
    for i in range(4):
        flag_ref[i] = rows[i]


def x_slopes(a):
    sums, diffs = (a[0] + a[3], a[1] + a[2]), (a[0] - a[3], a[1] - a[2])
    across = sums[0] - sums[1]
    out = [None] * 4
    for i in range(2):
        d = DERIV[i]
        odd = float((d[0] - d[3]) / 2) * diffs[0] + float((d[1] - d[2]) / 2) * diffs[1]
        even = float((d[0] + d[3]) / 2) * across
        out[i], out[3 - i] = odd + even, odd - even
    return out


def atm_kernel(
    par_ref,
    scal_ref,
    first_ref,
    flag_ref,
    ya_ref,
    yb_ref,
    vec_ref,
    rhs_ref,
    out_ref,
    table_ref,
    cb_ref,
    abuf_ref,
    dbuf_ref,
    hcb_ref,
    hbuf_ref,
    tm_ref,
    mask_ref,
    r5_ref,
    facc_ref,
    gs_ref,
    first_sem,
    copies,
):
    first_copy = pltpu.make_async_copy(first_ref, cb_ref, first_sem)
    first_copy.start()
    even_c = par_ref[1] == 0
    comp = par_ref[2]
    lane = iota((16, 128), 1)
    edge = (lane == 0) | (lane == 127)
    quarter = lane >> 5
    halo_edge = ((lane & 31) == 15) | ((lane & 31) == 16)

    def put(ref, index, value):
        hi, lo = split_bf16(value)
        ref[(*index, slice(None), slice(0, 128))] = hi
        ref[(*index, slice(None), slice(128, 256))] = lo

    ya, yb = ya_ref[0:528].astype(F32), yb_ref[0:528].astype(F32)
    from_right, from_left = jnp.where(even_c, ya, yb), jnp.where(even_c, yb, ya)
    arrived = jnp.concatenate([from_right, from_left], axis=1).astype(BF16)
    halo = mm(arrived, unpack_matrix()).astype(BF16)
    for k in range(4):
        for l in range(LEVELS):
            rows = slice((k * 8 + l // 2) * 16, (k * 8 + l // 2) * 16 + 16)
            lanes = slice((l % 2) * 128, (l % 2) * 128 + 128)
            hcb_ref[l, k, :, 0:128] = halo[rows, lanes]
            hcb_ref[l, k, :, 128:256] = jnp.zeros((16, 128), BF16)
    halo_flag = halo[512:528, 0:128].astype(F32)
    halo_r5 = jnp.where(halo_flag == 1.0, 5.0 * DT, 0.0)
    halo_m5 = jnp.where(halo_flag == 2.0, 5.0 * DT, 0.0)
    halo_keep = 1.0 - 2.0 * halo_m5
    halo_keep_t = halo_keep - halo_r5
    for i in range(4):
        flag = flag_ref[i]
        m5 = jnp.where(flag == 2.0, 5.0 * DT, 0.0)
        r5_ref[i] = jnp.where(flag == 1.0, 5.0 * DT, 0.0)
        mask_ref[0, i] = m5
        mask_ref[1, i] = 1.0 - 2.0 * m5
        mask_ref[2, i] = 1.0 - 2.0 * m5 - r5_ref[i]
    facc_ref[...] = jnp.zeros_like(facc_ref)
    dt_y = -DT * vec_ref[0:1, :]
    halo_dt_y = -DT * vec_ref[1:2, :]
    halo_dt_x = -DT * vec_ref[2:3, :]
    ff = vec_ref[pl.ds(4 + comp, 1), :]
    halo_ff = vec_ref[pl.ds(8 + comp, 1), :]
    for copy in (first_copy, *copies):
        copy.wait()

    def step(si, _):
        which = jnp.minimum(si, 1)
        both = mm(cb_ref[...].reshape(4096, 256), rhs_ref[which, :, 0:256])
        dbuf_ref[...] = both[:, 0:128].reshape(LEVELS, 4, 4, 16, 128)
        abuf_ref[...] = both[:, 128:256].reshape(LEVELS, 4, 4, 16, 128)
        hbuf_ref[...] = mm(hcb_ref[...].reshape(1024, 256), rhs_ref[which, :, 256:640]).reshape(
            LEVELS, 4, 16, 384
        )
        for i in range(4):
            total = abuf_ref[0, 2, i]
            for l in range(1, LEVELS):
                total = total + abuf_ref[l, 2, i]
            mask_ref[3, i] = r5_ref[i] * (total * (1.0 / LEVELS))
        total = hbuf_ref[0, 2, :, 256:384]
        for l in range(1, LEVELS):
            total = total + hbuf_ref[l, 2, :, 256:384]
        tm_ref[...] = halo_r5 * (total * (1.0 / LEVELS))

        def level(l, _):
            above, below = jnp.minimum(l + 1, LEVELS - 1), jnp.maximum(l - 1, 0)
            wind_x, wind_y = scal_ref[l], scal_ref[LEVELS + l]
            cx = -DT * wind_x
            cy = dt_y * wind_y
            a = [[abuf_ref[l, k, i] for i in range(4)] for k in range(4)]

            slopes = [x_slopes(a[k]) for k in range(4)]
            new = [[None] * 4 for _ in range(4)]
            for i in range(4):
                m5, keep, keep_t, relax = [mask_ref[n, i] for n in range(4)]
                d = [slopes[k][i] for k in range(4)]
                dy = [dbuf_ref[l, k, i] for k in range(4)]
                extra = [
                    ff * a[1][i] - DT * d[3],
                    dt_y * dy[3] - ff * a[0][i],
                    relax,
                    dt_y * dy[1] - DT * d[0],
                ]
                for k in range(4):
                    mix = m5 * (abuf_ref[above, k, i] + abuf_ref[below, k, i])
                    own = (keep_t if k == 2 else keep) * a[k][i]
                    new[k][i] = (own + mix) + ((cx * d[k] + cy * dy[k]) + extra[k])

            halo_cx, halo_cy = halo_dt_x * wind_x, halo_dt_y * wind_y
            hx, hy, ha = [
                [hbuf_ref[l, k, :, 128 * n : 128 * n + 128] for k in range(4)] for n in range(3)
            ]
            extra = [
                halo_ff * ha[1] + halo_dt_x * hx[3],
                halo_dt_y * hy[3] - halo_ff * ha[0],
                tm_ref[...],
                halo_dt_y * hy[1] + halo_dt_x * hx[0],
            ]
            for k in range(4):
                first = 0.5 * (new[k][0] + pltpu.roll(new[k][3], 1, 0))
                values = [first, new[k][1], new[k][2], pltpu.roll(first, 15, 0)]
                up, down = hbuf_ref[above, k, :, 256:384], hbuf_ref[below, k, :, 256:384]
                own = (halo_keep_t if k == 2 else halo_keep) * ha[k] + halo_m5 * (up + down)
                own = own + ((halo_cx * hx[k] + halo_cy * hy[k]) + extra[k])
                lower = pltpu.roll(pltpu.roll(own, 32, 1), 1, 0)
                upper = pltpu.roll(pltpu.roll(own, 96, 1), 15, 0)
                partner = jnp.where(quarter == 0, lower, jnp.where(quarter == 3, upper, own))
                own = 0.5 * (own + partner)
                across = None
                for i in range(4):
                    moved = pltpu.roll(values[i], 32 * i + 16, 1)
                    across = moved if i == 0 else jnp.where(quarter == i, moved, across)
                    back = pltpu.roll(own, 112 - 32 * i, 1)
                    put(cb_ref, (l, k, i), jnp.where(edge, 0.5 * (values[i] + back), values[i]))
                put(hcb_ref, (l, k), jnp.where(halo_edge, 0.5 * (own + across), own))
            return 0

        lax.fori_loop(0, LEVELS, level, 0, unroll=2)
        surface = mm(cb_ref[0].reshape(256, 256), rhs_ref[1, :, 128:256]).reshape(4, 4, 16, 128)
        for i in range(4):
            u, v, t, z = [surface[k, i, 0:8] for k in range(4)]
            speed = jnp.sqrt(u * u + v * v + 1.0)
            for c in range(NFLUX):
                m0, m1, m2, m3 = [scal_ref[32 + 4 * c + k] for k in range(4)]
                m = (m0 * u + m1 * v) + (m2 * t + m3 * z)
                facc_ref[c, i] += speed * m * lax.rsqrt(1.0 + 0.5 * (m * m))
        return 0

    lax.fori_loop(0, STEPS, step, 0)
    final = mm(cb_ref[...].reshape(4096, 256), rhs_ref[1, :, 128:256]).reshape(LEVELS, 4, 4, 16, 128)
    for l in range(LEVELS):
        for k in range(4):
            for i in range(4):
                out_ref[k * LEVELS + l, pl.ds(i, 8, stride=4), :] = final[l, k, i, 0:8]
    for i in range(4):
        mean = [(facc_ref[c, i] * (1.0 / STEPS)).astype(BF16).astype(F32) for c in range(NFLUX)]
        for g in range(4):
            total = scal_ref[80 + 12 * g] * mean[0]
            for c in range(1, NFLUX):
                total = total + scal_ref[80 + 12 * g + c] * mean[c]
            gs_ref[g, pl.ds(i, 8, stride=4), :] = 0.25 * total
    table_ref[...] = gs_ref[...].reshape(128, 128).astype(BF16)


def pick_kernel(served_ref, table_ref, weights_ref, rows_ref):
    pick = served_ref[...].astype(F32) == iota((512, 128), 1).astype(F32)
    rows_ref[...] = mm(jnp.where(pick, 1.0, 0.0).astype(BF16), table_ref[...]).astype(BF16)


def request_matrix(tcol_ref):
    parts = []
    for chunk in range(4):
        hit = tcol_ref[...] == iota((512, 128), 1) + 128 * chunk
        parts.append(jnp.where(hit, 1.0, 0.0).astype(BF16))
    return jnp.concatenate(parts, axis=1)


def force_block(window, wm, sw, n2_ref, ocean_ref, b):
    cells = slice(128 * b, 128 * b + 128)
    hi, lo = split_bf16(window)
    own = window[:, 128:256]
    both = mm(jnp.concatenate([hi.astype(F32), lo.astype(F32)], axis=0).astype(BF16), wm)
    top = both[0:8] + both[8:16] + (1.8 - sw) * own
    surface = []
    for k in range(4):
        value = n2_ref[16 * k : 16 * k + 1, cells] + top[k : k + 1]
        if k == 2:
            value = value + 0.2 * own[3:4]
        if k == 3:
            value = value - 0.2 * own[2:3]
        below = n2_ref[16 * k + 1 : 16 * k + 2, cells] + 0.2 * own[k : k + 1]
        ocean_ref[16 * k : 16 * k + 1, cells] = value
        ocean_ref[16 * k + 1 : 16 * k + 2, cells] = below
        surface.append(value)
    return jnp.concatenate(surface + [jnp.zeros((4, 128), F32)], axis=0).astype(BF16)


def return_parts(surface, weights, parts_ref, b):
    parts = mm(surface, jnp.concatenate([weights[k] for k in range(8)], axis=1))
    for k in range(8):
        rows = slice((b * 8 + k) * 8, (b * 8 + k) * 8 + 8)
        parts_ref[rows, :] = parts[:, 128 * k : 128 * k + 128]


def ocean_kernel(
    par_ref,
    ocean_ref,
    off_ref,
    w_ref,
    ya_ref,
    yb_ref,
    f_ref,
    weights_ref,
    tcol_ref,
    n2_ref,
    ends_ref,
    sw_ref,
    parts_ref,
    table_ref,
    o1_ref,
    wm_ref,
):
    even_c = par_ref[1] == 0

    def halo_rows(n):
        rows = slice(528 + 16 * n, 544 + 16 * n)
        a, b = ya_ref[rows].astype(F32), yb_ref[rows].astype(F32)
        return jnp.where(even_c, b, a), jnp.where(even_c, a, b)

    pieces = [halo_rows(n) for n in range(9)]
    left = [jnp.concatenate([p[0] for p in pieces[4 * n : 4 * n + 4]], axis=0) for n in range(2)]
    right = [jnp.concatenate([p[1] for p in pieces[4 * n : 4 * n + 4]], axis=0) for n in range(2)]
    values = {-2: left[0], -1: left[1], 8: right[0], 9: right[1]}
    for b in range(8):
        values[b] = ocean_ref[:, 128 * b : 128 * b + 128]
    offw = {-1: pieces[8][0], 8: pieces[8][1]}
    source = iota((384, 128), 0)
    lane = iota((1, 128), 1)
    level = iota((64, 128), 0) & 15

    def matrix(b):
        if b in offw:
            off, w = offw[b][0:6].astype(I32), offw[b][8:14]
        else:
            cells = slice(128 * b, 128 * b + 128)
            off, w = off_ref[:, cells], w_ref[:, cells].astype(BF16).astype(F32)
        total = jnp.zeros((384, 128), F32)
        for j in range(6):
            total = total + jnp.where(source == lane + off[j : j + 1], w[j : j + 1], 0.0)
        return total.astype(BF16), jnp.sum(w, axis=0, keepdims=True)

    def update(own, window, wm, sw):
        hi, lo = split_bf16(window)
        both = mm(jnp.concatenate([hi, lo], axis=0), wm)
        lateral = both[0:64] + both[64:128] - sw * own
        above = jnp.where(level == 15, own, pltpu.roll(own, 63, 0))
        below = jnp.where(level == 0, own, pltpu.roll(own, 1, 0))
        rot = jnp.concatenate([jnp.zeros((32, 128), F32), 0.2 * own[48:64], -0.2 * own[32:48]], axis=0)
        return own + lateral + 0.2 * (above - 2.0 * own + below) + rot

    for b in range(-1, 9):
        wm, sw = matrix(b)
        if 0 <= b < 8:
            wm_ref[b] = wm
            sw_ref[:, 128 * b : 128 * b + 128] = jnp.broadcast_to(sw, (8, 128))
        window = jnp.concatenate([values[b - 1], values[b], values[b + 1]], axis=1)
        o1_ref[b + 1] = update(values[b], window, wm, sw)
    for b in range(8):
        window = jnp.concatenate([o1_ref[b], o1_ref[b + 1], o1_ref[b + 2]], axis=1)
        cells = slice(128 * b, 128 * b + 128)
        n2_ref[:, cells] = update(o1_ref[b + 1], window, wm_ref[b], sw_ref[0:1, cells])
    for b in range(1, 7):
        cells = slice(128 * b, 128 * b + 128)
        window = f_ref[:, 128 * b - 128 : 128 * b + 256]
        surface = force_block(window, wm_ref[b], sw_ref[:, cells], n2_ref, n2_ref, b)
        return_parts(surface, weights_ref[b], parts_ref, b)
    ends_ref[0] = wm_ref[0]
    ends_ref[1] = wm_ref[7]
    for b in (0, 7):
        parts_ref[64 * b : 64 * b + 64, :] = jnp.zeros((64, 128), F32)
    table_ref[...] = request_matrix(tcol_ref)


def forcing_kernel(par_ref, rows_ref, tcol_ref, weights_ref, f_ref, a_ref, b_ref):
    even_c = par_ref[1] == 0
    gathered = mm(request_matrix(tcol_ref), rows_ref[...])
    for b in range(8):
        lhs = jnp.concatenate(
            [gathered[(b * 8 + k) * 8 : (b * 8 + k) * 8 + 8] for k in range(8)], axis=1
        ).astype(BF16)
        f_ref[:, 128 * b : 128 * b + 128] = mm(lhs, weights_ref[b])
    right, left = f_ref[:, 896:1024], f_ref[:, 0:128]
    a_ref[...] = jnp.where(even_c, right, left)
    b_ref[...] = jnp.where(even_c, left, right)


def return_kernel(
    par_ref,
    n2_ref,
    ends_ref,
    sw_ref,
    f_ref,
    ea_ref,
    eb_ref,
    inner_ref,
    table_ref,
    first_ref,
    last_ref,
    ocean_ref,
    sent_ref,
    parts_ref,
):
    even_c = par_ref[1] == 0
    ea, eb = ea_ref[...], eb_ref[...]
    ocean_ref[...] = n2_ref[...]
    parts_ref[...] = inner_ref[...]
    window = jnp.concatenate([jnp.where(even_c, eb, ea), f_ref[:, 0:256]], axis=1)
    surface = force_block(window, ends_ref[0], sw_ref[:, 0:128], n2_ref, ocean_ref, 0)
    return_parts(surface, first_ref, parts_ref, 0)
    window = jnp.concatenate([f_ref[:, 768:1024], jnp.where(even_c, ea, eb)], axis=1)
    surface = force_block(window, ends_ref[1], sw_ref[:, 896:1024], n2_ref, ocean_ref, 7)
    return_parts(surface, last_ref, parts_ref, 7)
    sent_ref[...] = mm_t(table_ref[...], parts_ref[...].astype(BF16)).astype(BF16)


def collect_kernel(served_ref, incoming_ref, out_ref):
    pick = served_ref[...].astype(F32) == iota((512, 128), 1).astype(F32)
    owner = jnp.where(pick, 1.0, 0.0).astype(BF16)
    out_ref[...] = mm_t(owner, incoming_ref[...]).reshape(4, 32, 128)


def swap_pairs(n):
    near = [(i, i ^ 1) for i in range(n)]
    far = [(i, (i + 1) % n if i % 2 else (i - 1) % n) for i in range(n)]
    return near, far


def exchange(payloads, axis, n):
    near, far = swap_pairs(n)
    return lax.ppermute(payloads[0], axis, near), lax.ppermute(payloads[1], axis, far)


def to_tiles(rows):
    moved = lax.all_to_all(
        rows.reshape(N_TILE, 16, 128), "tile", split_axis=0, concat_axis=0, tiled=True
    )
    return moved.reshape(512, 128)


def call(kernel, out, specs, scratch=(), mib=16, cost=None):
    return pl.pallas_call(
        kernel,
        out_shape=out,
        in_specs=specs,
        out_specs=jax.tree.map(lambda _: VMEM, out),
        scratch_shapes=list(scratch),
        compiler_params=pltpu.CompilerParams(vmem_limit_bytes=mib * 2**20),
        cost_estimate=cost,
    )


def staged(kernel, out, scalars, resident, arrays, scratch=(), late=0, mib=16, cost=None):
    n_lead, n = len(scalars) + len(resident), len(arrays)
    n_out = len(jax.tree.leaves(out))

    def body(*refs):
        lead_refs, hbm_refs = refs[:n_lead], refs[n_lead : n_lead + n]
        out_refs = refs[n_lead + n : n_lead + n + n_out]
        held, (sems, *rest) = refs[-n - 1 - len(scratch) :][:n], refs[-1 - len(scratch) :]
        copies = [pltpu.make_async_copy(hbm_refs[i], held[i], sems.at[i]) for i in range(n)]
        for copy in copies:
            copy.start()
        for copy in copies[: n - late]:
            copy.wait()
        extra = (copies[n - late :],) if late else ()
        kernel(*lead_refs, *held, *out_refs, *rest, *extra)

    buffers = [pltpu.VMEM(a.shape, a.dtype) for a in arrays]
    scratch_shapes = buffers + [pltpu.SemaphoreType.DMA((n,))] + list(scratch)
    specs = [SMEM] * len(scalars) + [VMEM] * len(resident) + [HBM] * n
    return call(body, out, specs, scratch_shapes, mib, cost)(*scalars, *resident, *arrays)


ATM_SCRATCH = (
    pltpu.VMEM((LEVELS, 4, 4, 16, 256), BF16),
    pltpu.VMEM((LEVELS, 4, 4, 16, 128), F32),
    pltpu.VMEM((LEVELS, 4, 4, 16, 128), F32),
    pltpu.VMEM((LEVELS, 4, 16, 256), BF16),
    pltpu.VMEM((LEVELS, 4, 16, 384), F32),
    pltpu.VMEM((16, 128), F32),
    pltpu.VMEM((4, 4, 16, 128), F32),
    pltpu.VMEM((4, 16, 128), F32),
    pltpu.VMEM((NFLUX, 4, 8, 128), F32),
    pltpu.VMEM((4, 32, 128), F32),
    pltpu.SemaphoreType.DMA,
)


def per_device(
    atm_state,
    level_winds,
    physics_flags,
    flux_matrix,
    regrid_source,
    regrid_weights,
    return_weights,
    ocean_state,
    ocean_neighbors,
    edge_weights,
    ocean_coupling,
):
    S = jax.ShapeDtypeStruct
    t, c = lax.axis_index("tile"), lax.axis_index("comp")
    par = jnp.stack([t % 2, c % 2, c, t]).astype(I32)
    atm = atm_state.reshape(64, 32, 128)
    ocean = ocean_state.reshape(64, 1024)
    scal = jnp.concatenate(
        [level_winds.reshape(-1), flux_matrix.reshape(-1), ocean_coupling.reshape(-1)]
    )
    rhs = jnp.asarray(lane_matrices())
    vec = jnp.asarray(lane_vectors())

    xp_a, xp_b, flags = staged(
        x_pack_kernel,
        (S((X_PLANES, 16, 128), BF16),) * 2 + (S((32, 128), F32),),
        (par,),
        (),
        (atm, physics_flags, ocean, ocean_neighbors, edge_weights),
        mib=12,
    )
    xa, xb = exchange((xp_a, xp_b), "tile", N_TILE)
    wanted, tcol = call(slots_kernel, (S((512, 128), BF16), S((512, 128), I32)), [VMEM])(
        regrid_source
    )
    wanted, tcol, xb = lax.optimization_barrier((wanted, tcol, xb))
    served = to_tiles(wanted)
    y_payload = call(
        y_pack_kernel,
        (S((Y_ROWS, 128), BF16),) * 2,
        [SMEM] + [VMEM] * 6,
        [pltpu.VMEM((33, 16, 1024), BF16), pltpu.VMEM((8, 64, 128), F32)],
    )(par, atm, flags, xa, xb, xp_a, xp_b)
    ya, yb = exchange(y_payload, "comp", N_COMP)
    first, flag = call(
        prepare_kernel,
        (S((LEVELS, 4, 4, 16, 256), BF16), S((4, 16, 128), F32)),
        [SMEM] + [VMEM] * 4,
        [pltpu.VMEM((8, 64, 128), F32)],
        cost=pl.CostEstimate(flops=2**23, bytes_accessed=2**23, transcendentals=0),
    )(par, atm, flags, xa, xb)
    atm_final, table = staged(
        atm_kernel,
        (S((64, 32, 128), F32), S((128, 128), BF16)),
        (par, scal),
        (first, flag, ya, yb),
        (vec, rhs),
        ATM_SCRATCH,
        late=1,
        mib=32,
        cost=pl.CostEstimate(flops=2**33, bytes_accessed=2**26, transcendentals=0),
    )
    rows = call(pick_kernel, S((512, 128), BF16), [VMEM] * 3)(
        served, table, regrid_weights.reshape(8, 1024, 128)
    )
    mean_rows = to_tiles(rows)
    mean_rows, return_weights = lax.optimization_barrier((mean_rows, return_weights))
    forcing, *edges = call(
        forcing_kernel,
        (S((8, 1024), F32), S((8, 128), F32), S((8, 128), F32)),
        [SMEM] + [VMEM] * 3,
    )(par, mean_rows, tcol, regrid_weights.reshape(8, 1024, 128))
    ea, eb = exchange(edges, ("tile", "comp"), N_TILE * N_COMP)
    n2, ends, sw, parts, table = call(
        ocean_kernel,
        (
            S((64, 1024), F32),
            S((2, 384, 128), BF16),
            S((8, 1024), F32),
            S((512, 128), F32),
            S((512, 512), BF16),
        ),
        [SMEM] + [VMEM] * 8,
        [pltpu.VMEM((10, 64, 128), F32), pltpu.VMEM((8, 384, 128), BF16)],
        cost=pl.CostEstimate(flops=2**27, bytes_accessed=2**24, transcendentals=0),
    )(par, ocean, ocean_neighbors, edge_weights, ya, yb, forcing, return_weights, tcol)
    ocean_final, sent = call(
        return_kernel,
        (S((64, 1024), F32), S((512, 128), BF16)),
        [SMEM] + [VMEM] * 10,
        [pltpu.VMEM((512, 128), F32)],
    )(par, n2, ends, sw, forcing, ea, eb, parts, table, return_weights[0], return_weights[7])
    incoming = to_tiles(sent)
    ocean_on_atm = call(collect_kernel, S((4, 32, 128), F32), [VMEM] * 2)(served, incoming)
    return (
        atm_final.reshape(atm_state.shape),
        ocean_final.reshape(ocean_state.shape),
        ocean_on_atm,
    )


def solution(mesh):
    return jax.shard_map(
        per_device,
        mesh=mesh,
        in_specs=(
            P(None, None, "tile", "comp"),
            P(),
            P("tile", "comp"),
            P(),
            P(("tile", "comp"), None),
            P(("tile", "comp"), None, None, None),
            P(("tile", "comp"), None, None, None),
            P(None, None, ("tile", "comp")),
            P(None, ("tile", "comp")),
            P(None, ("tile", "comp")),
            P(),
        ),
        out_specs=(
            P(None, None, "tile", "comp"),
            P(None, None, ("tile", "comp")),
            P(None, "tile", "comp"),
        ),
        check_vma=False,
    )
```
